256 devices in a mesh: branch: 16 (over z, core), grid: 16 (over y, x).
Axes of the slice: x: 4, y: 4, z: 8, core: 2. Of those that a mesh axis runs over, the one named last changes fastest.
Arguments:
- sigma_top: float32 [8192, 8192], P('grid', 'branch'), as said below
- mid_struct: int32 [16, 12], P('branch'), may hold values from 0 to 31, as said below
- leaf_struct: int32 [16, 6], P('branch'), may hold values from 0 to 11, as said below
- mid_inv: float32 [16, 256, 256], P('branch'), as said below
- mid_off: float32 [16, 12, 256, 256], P('branch'), may hold values from -0.375 to 0.375
- leaf_inv: float32 [16, 256, 256], P('branch'), as said below
- leaf_off: float32 [16, 7, 256, 256], P('branch'), may hold values from -0.375 to 0.375
Outputs:
- sigma_mid_off: float32 [16, 12, 256, 256], P('branch', None, 'grid')
- sigma_mid_diag: float32 [16, 256, 256], P('branch')
- sigma_leaf_off: float32 [16, 12, 256, 256], P('branch', None, 'grid')
- sigma_leaf_parent: float32 [16, 256, 256], P('branch')
- sigma_leaf_diag: float32 [16, 256, 256], P('branch')
The draws below stay inside these ranges and needn't reach their ends.
Inputs may be any that keep to these rules, and one draw needn't show every extreme that they name: sigma_top is exactly symmetric. `mid_struct`: each row holds 12 different top row blocks in increasing order; the last is always 32 - 1. `leaf_struct`: each row holds 6 different positions in increasing order; the last is always 12 - 1. `mid_inv`: lower triangular with a positive diagonal. `leaf_inv`: lower triangular with a positive diagonal.
All inputs are finite; a program needn't handle non-finite values.
Results may differ from the reference program's by a relative error of at most 0.0003.
Values sent between devices are 32-bit elements; how exact they have to be, the bound alone decides.
A program may use at most 128 MiB of HBM per device.

```python
import math
import jax
import jax.numpy as jnp
from jax import lax

BS = 256
NA = 32
NS1 = 12
NS2 = 6
BRANCHES = 16


def lower_factor(rough, key):
    diag = jax.random.uniform(key, rough.shape[:-1], jnp.float32, 0.5, 1.5)
    strict = jnp.tril(rough * (0.5 / math.sqrt(BS)), -1)
    ident = jnp.eye(BS, dtype=jnp.float32)
    return strict + diag[..., None] * ident


def draw_sigma_top(key, part):
    key = jax.random.fold_in(key, 11)
    first_key, second_key = jax.random.split(key)
    count = NA * BS
    rough = jax.random.normal(first_key, (count, count), jnp.float32)
    rough = rough * (0.5 / math.sqrt(count))
    sym = (rough + rough.T) * 0.5
    diag = jax.random.uniform(second_key, (count,), jnp.float32, 1.0, 2.0)
    index = jnp.arange(count)
    return sym.at[index, index].set(diag)


def draw_mid_inv(key, part):
    key = jax.random.fold_in(key, 12)
    first_key, second_key = jax.random.split(key)
    rough = jax.random.normal(first_key, (BRANCHES, BS, BS), jnp.float32)
    return lower_factor(rough, second_key)


def draw_leaf_inv(key, part):
    key = jax.random.fold_in(key, 14)
    first_key, second_key = jax.random.split(key)
    rough = jax.random.normal(first_key, (BRANCHES, BS, BS), jnp.float32)
    return lower_factor(rough, second_key)


def draw_mid_struct(key, part):
    key = jax.random.fold_in(key, 13)
    keys = jax.random.split(key, BRANCHES)

    def one_row(row_key):
        chosen = jax.random.permutation(row_key, NA - 1)[:NS1 - 1]
        return jnp.concatenate([jnp.sort(chosen), jnp.array([NA - 1])]).astype(jnp.int32)
    return jax.vmap(one_row)(keys)


def draw_leaf_struct(key, part):
    key = jax.random.fold_in(key, 15)
    keys = jax.random.split(key, BRANCHES)

    def one_row(row_key):
        chosen = jax.random.permutation(row_key, NS1 - 1)[:NS2 - 1]
        return jnp.concatenate([jnp.sort(chosen), jnp.array([NS1 - 1])]).astype(jnp.int32)
    return jax.vmap(one_row)(keys)


def levels(key, shape, cuts, smallest, largest):
    level, own = 1.0, jax.random.fold_in(key, 6)
    for axis_at, blocks in cuts:
        draws = jnp.exp(jax.random.uniform(jax.random.fold_in(own, axis_at), (blocks,), jnp.float32, smallest / len(cuts), largest / len(cuts)))
        level = level * jnp.repeat(draws, shape[axis_at] // blocks).reshape([-1 if axis == axis_at else 1 for axis in range(len(shape))])
    return level


def normal_values(own_key, extent, scale, bound, cuts=(), held_as=jnp.bfloat16):
    loudness = levels(own_key, extent, cuts, -0.22, 0.18) if cuts else 1.0
    values = jax.random.normal(own_key, extent, jnp.float32) * scale * loudness
    return jnp.minimum(jnp.maximum(values, -bound), bound).astype(held_as)


def setup_inputs(seed: int = 0) -> dict:
    arg_keys = jax.random.split(jax.random.key(seed), 8)
    return {
        "sigma_top": draw_sigma_top(jax.random.fold_in(arg_keys[7], 71), 0),
        "mid_struct": draw_mid_struct(jax.random.fold_in(arg_keys[7], 71), 0),
        "leaf_struct": draw_leaf_struct(jax.random.fold_in(arg_keys[7], 71), 0),
        "mid_inv": draw_mid_inv(jax.random.fold_in(arg_keys[7], 71), 0),
        "mid_off": normal_values(arg_keys[4], (BRANCHES, NS1, BS, BS), BS ** -0.5, 0.375, ((0, 16),), jnp.float32),
        "leaf_inv": draw_leaf_inv(jax.random.fold_in(arg_keys[7], 71), 0),
        "leaf_off": normal_values(arg_keys[6], (BRANCHES, NS2 + 1, BS, BS), BS ** -0.5, 0.375, ((0, 16),), jnp.float32),
    }


def reference(sigma_top, mid_struct, leaf_struct, mid_inv, mid_off, leaf_inv, leaf_off):
    highest = lax.Precision.HIGHEST
    blocks = sigma_top.reshape(NA, BS, NA, BS)

    def branch_work(inputs):
        struct, leaf_pos, minv, moff, linv, loff = inputs
        rows_sel = jnp.take(blocks, struct, axis=0)
        square = jnp.take(rows_sel, struct, axis=2).reshape(NS1 * BS, NS1 * BS)
        upper = jnp.einsum('kab,bc->kac', moff, minv, precision=highest).reshape(NS1 * BS, BS)
        mid_col = -jnp.dot(square, upper, precision=highest)
        mid_diag = jnp.dot(minv.T, minv, precision=highest) - jnp.dot(upper.T, mid_col, precision=highest)
        leaf_v = jnp.einsum('kab,bc->kac', loff, linv, precision=highest)
        first = leaf_v[0]
        place = (leaf_pos[:, None] == jnp.arange(NS1, dtype=jnp.int32)[None, :]).astype(jnp.float32)
        spread = jnp.einsum('ti,tab->iab', place, leaf_v[1:], precision=highest).reshape(NS1 * BS, BS)
        zpar = jnp.dot(mid_diag, first, precision=highest) + jnp.dot(mid_col.T, spread, precision=highest)
        zstr = jnp.dot(mid_col, first, precision=highest) + jnp.dot(square, spread, precision=highest)
        leaf_diag = (jnp.dot(linv.T, linv, precision=highest) + jnp.dot(first.T, zpar, precision=highest)
                     + jnp.dot(spread.T, zstr, precision=highest))
        marks = jnp.sum(place, axis=0)
        leaf_col = -zstr.reshape(NS1, BS, BS) * marks[:, None, None]
        return mid_col.reshape(NS1, BS, BS), mid_diag, leaf_col, -zpar, leaf_diag

    outs = lax.map(branch_work, (mid_struct, leaf_struct, mid_inv, mid_off, leaf_inv, leaf_off))
    return outs[0], outs[1], outs[2], outs[3], outs[4]
```

```python
import functools

import jax
import jax.numpy as jnp
from jax import lax
from jax.experimental import pallas as pl
from jax.experimental.pallas import tpu as pltpu
from jax.sharding import PartitionSpec as P

MESH = pl.DeviceIdType.MESH
F32 = jnp.float32
BF16 = jnp.bfloat16
BS = 256
NS1 = 12
NS2 = 6
SIDE = 4
RING = 8
SUB = BS // SIDE
SLICE = 16
SLOTS = 17
PIECES = ((0, 4), (4, 4), (8, 4), (12, 5))
ROWS = NS1 * SUB
OUTS = NS1 + NS2


def split(value):
    high = value.astype(BF16)
    return high, (value - high.astype(F32)).astype(BF16)


def product(left, right, dims=(((1,), (0,)), ((), ()))):
    def one(a, b):
        return lax.dot_general(a, b, dims, preferred_element_type=F32)
    return one(left[0], right[0]) + (one(left[0], right[1]) + one(left[1], right[0]))


def product_t(left, right):
    return product(left, right, (((0,), (0,)), ((), ())))


def kernel(
    struct, leaf, sigma, minv_hbm, moff_hbm, linv_hbm, loff_hbm,
    mid_out, diag_out, leaf_out, parent_out, leaf_diag_out,
    packed, extra, gathered, moff, loff, first_raw, minv, linv, vblocks, v0_hi, v0_lo, base,
    w_hi, w_lo, wt_hi, wt_lo, a_hi, a_lo, ysum, ysend, yrecv, ycomb, gsend, grecv, gcomb, gred, gexch, gall,
    load_sem, pack_send, pack_recv, extra_send, extra_recv, z_send, right_recv, left_recv,
    pair_send, pair_recv, y_send_sem, y_recv_sem, g_send_sem, g_recv_sem,
):
    branch = lax.axis_index("branch")
    grid = lax.axis_index("grid")
    z, core = branch // 2, branch % 2
    y, x = grid // SIDE, grid % SIDE

    def slots(which_core, source, slot, size=None):
        start = (which_core * RING + source) * SLOTS + slot
        return gathered.at[start] if size is None else gathered.at[pl.ds(start, size)]

    def at_grid(index):
        return {"branch": branch, "grid": index}

    def at_branch(index):
        return {"branch": index, "grid": grid}

    up = at_branch(lax.rem(z + 1, RING) * 2 + core)
    down = at_branch(lax.rem(z + RING - 1, RING) * 2 + core)
    pair = at_branch(z * 2 + (1 - core))
    around = (
        (at_grid(y * SIDE + lax.rem(x + 1, SIDE)), at_grid(y * SIDE + lax.rem(x + SIDE - 1, SIDE))),
        (at_grid(lax.rem(y + 1, SIDE) * SIDE + x), at_grid(lax.rem(y + SIDE - 1, SIDE) * SIDE + x)),
    )
    place = (x, y)

    row_c = pl.multiple_of(y * SUB, SUB)
    loads = [
        pltpu.make_async_copy(minv_hbm.at[0], minv, load_sem.at[0]),
        pltpu.make_async_copy(linv_hbm.at[0], linv, load_sem.at[1]),
        pltpu.make_async_copy(loff_hbm.at[0, 0], first_raw, load_sem.at[2]),
        pltpu.make_async_copy(moff_hbm.at[0, :, pl.ds(row_c, SUB), :], moff.at[0], load_sem.at[3]),
        pltpu.make_async_copy(loff_hbm.at[0, pl.ds(1, NS2), pl.ds(row_c, SUB), :], loff.at[0], load_sem.at[4]),
    ]
    for m in range(SIDE):
        row_r = pl.multiple_of(m * SUB + x * SLICE, SLICE)
        into = pl.ds(m * SLICE, SLICE)
        loads.append(pltpu.make_async_copy(
            moff_hbm.at[0, :, pl.ds(row_r, SLICE), :], moff.at[1, :, into, :], load_sem.at[5 + m]))
        loads.append(pltpu.make_async_copy(
            loff_hbm.at[0, pl.ds(1, NS2), pl.ds(row_r, SLICE), :], loff.at[1, :, into, :], load_sem.at[9 + m]))
    for load in loads:
        load.start()

    barrier = pltpu.get_barrier_semaphore()

    def greet(step, carry):
        pl.semaphore_signal(
            barrier, inc=1, device_id=at_grid(lax.rem(grid + step, SIDE * SIDE)), device_id_type=MESH)
        return carry

    lax.fori_loop(1, SIDE * SIDE, greet, 0)
    for other in (up, down, pair):
        pl.semaphore_signal(barrier, inc=1, device_id=other, device_id_type=MESH)

    flip = (grid > branch).astype(jnp.int32)
    lane = lax.broadcasted_iota(jnp.int32, (BS, 128), 1)
    for half in range(2):
        one = sigma[0:BS, pl.ds(pl.multiple_of(flip * BS + half * 128, 128), 128)]
        two = sigma[BS:2 * BS, pl.ds(pl.multiple_of((1 - flip) * BS + half * 128, 128), 128)]
        even = jnp.where(lane < SUB, one, pltpu.roll(two, SUB, 1))
        odd = jnp.where(lane < SUB, pltpu.roll(one, SUB, 1), two)
        for side, value in ((2 * half, even), (2 * half + 1, odd)):
            for m in range(SIDE):
                for xx in range(SIDE):
                    start = m * SUB + xx * SLICE
                    packed[side * SIDE + xx, m * SLICE:(m + 1) * SLICE, :] = value[start:start + SLICE, :]

    @pl.when(grid == branch)
    def _():
        for half in range(2):
            value = sigma[0:BS, BS + half * 128:BS + (half + 1) * 128]
            for side, turned in ((2 * half, value), (2 * half + 1, pltpu.roll(value, SUB, 1))):
                for m in range(SIDE):
                    for xx in range(SIDE):
                        start = m * SUB + xx * SLICE
                        extra[side * SIDE + xx, m * SLICE:(m + 1) * SLICE, :] = turned[start:start + SLICE, :]

    pl.semaphore_wait(barrier, SIDE * SIDE + 2)

    pltpu.make_async_copy(packed.at[grid], slots(core, z, grid), pack_recv.at[grid // SIDE]).start()

    def hand_out(step, carry):
        to = lax.rem(grid + step, SIDE * SIDE)
        pltpu.make_async_remote_copy(
            src_ref=packed.at[to], dst_ref=slots(core, z, grid), send_sem=pack_send,
            recv_sem=pack_recv.at[grid // SIDE], device_id=at_grid(to), device_id_type=MESH).start()
        return carry

    lax.fori_loop(1, SIDE * SIDE, hand_out, 0)

    @pl.when(grid == branch)
    def _():
        pltpu.make_async_copy(extra.at[grid], slots(core, z, SLOTS - 1), extra_recv).start()

        def hand_extra(step, carry):
            to = lax.rem(grid + step, SIDE * SIDE)
            pltpu.make_async_remote_copy(
                src_ref=extra.at[to], dst_ref=slots(core, z, SLOTS - 1), send_sem=extra_send,
                recv_sem=extra_recv, device_id=at_grid(to), device_id_type=MESH).start()
            return carry

        lax.fori_loop(1, SIDE * SIDE, hand_extra, 0)

    def piece_of(source, piece):
        start, size = PIECES[piece]
        return slots(core, source, start, size)

    def pass_on(source, piece, to, recv_sem):
        ref = piece_of(source, piece)
        pltpu.make_async_remote_copy(
            src_ref=ref, dst_ref=ref, send_sem=z_send, recv_sem=recv_sem, device_id=to, device_id_type=MESH).start()

    def to_pair(source, piece):
        ref = piece_of(source, piece)
        pltpu.make_async_remote_copy(
            src_ref=ref, dst_ref=ref, send_sem=pair_send, recv_sem=pair_recv, device_id=pair,
            device_id_type=MESH).start()

    def await_bytes(ref, sem):
        pltpu.make_async_copy(ref, ref, sem).wait()

    for piece in range(4):
        await_bytes(slots(core, z, 4 * piece, 4), pack_recv.at[piece])
        if piece == 3:
            await_bytes(slots(core, z, SLOTS - 1), extra_recv)
        pass_on(z, piece, up, right_recv.at[1, piece])
        pass_on(z, piece, down, left_recv.at[1, piece])
        to_pair(z, piece)

    def leaf_of(k):
        found, index = 0, 0
        for t in range(NS2):
            same = (leaf[0, t] == k).astype(jnp.int32)
            found = found + same
            index = index + same * t
        return jnp.minimum(index, NS2 - 1), found.astype(F32)

    def factors():
        for load in loads:
            load.wait()
        minv_s = split(minv[...])
        linv_s = split(linv[...])
        v0_s = split(product(split(first_raw[...]), linv_s))
        v0_hi[...], v0_lo[...] = v0_s
        for part in range(2):
            vblocks[part] = product(split(loff[part].reshape(NS2 * SUB, BS)), linv_s).reshape(NS2, SUB, BS)
        square = product_t(minv_s, minv_s)
        base[0] = square
        turned = product(split(square), v0_s)
        base[1] = -turned
        base[2] = product_t(linv_s, linv_s) + product_t(v0_s, split(turned))
        for part in range(2):
            def rows(q, carry):
                raw = moff[part, pl.ds(q * 4, 4)].reshape(BS, BS)
                u = product(split(raw), (split(minv[...])))
                u_s = split(u)
                uv = product(u_s, (v0_hi[...], v0_lo[...]))
                spread = []
                for j in range(4):
                    index, mark = leaf_of(q * 4 + j)
                    spread.append(vblocks[part, index] * mark)
                t = jnp.concatenate(spread, axis=0) - uv
                t_s = split(t)
                at = pl.ds(pl.multiple_of(q * BS, BS), BS)
                for kind, pieces in ((0, u_s), (1, t_s)):
                    w_hi[part, at, kind * BS:(kind + 1) * BS] = pieces[0]
                    w_lo[part, at, kind * BS:(kind + 1) * BS] = pieces[1]
                if part == 1:
                    for kind, value in ((0, u), (1, t)):
                        high, low = split(value.T)
                        wt_hi[kind * BS:(kind + 1) * BS, at] = high
                        wt_lo[kind * BS:(kind + 1) * BS, at] = low
                return carry
            lax.fori_loop(0, 3, rows, 0)

    factors()

    for step in range(1, 5):
        below = lax.rem(z + RING - step, RING)
        above = lax.rem(z + step, RING)
        for piece in range(4):
            if step < 4 or piece < 2:
                await_bytes(piece_of(below, piece), right_recv.at[step, piece])
                if step < 3 or (step == 3 and piece < 2):
                    pass_on(below, piece, up, right_recv.at[step + 1, piece])
                to_pair(below, piece)
            if step < 4 or piece >= 2:
                await_bytes(piece_of(above, piece), left_recv.at[step, piece])
                if step < 3 or (step == 3 and piece >= 2):
                    pass_on(above, piece, down, left_recv.at[step + 1, piece])
                to_pair(above, piece)
    await_bytes(slots(1 - core, 0, 0, RING * SLOTS), pair_recv)

    narrow = lax.broadcasted_iota(jnp.int32, (SUB, 128), 1) < SUB

    def select(k, carry):
        si = struct[0, k]
        gi, ai = si >> 1, si & 1
        row = pl.ds(pl.multiple_of(k * SUB, SUB), SUB)
        for p in range(NS1 // 2):
            sides = []
            for h in range(2):
                sj = struct[0, 2 * p + h]
                bj, cj = sj >> 1, sj & 1
                beyond = (gi > bj).astype(jnp.int32)
                plain = (cj == (ai ^ beyond)).astype(jnp.int32)
                own = ((gi == bj).astype(jnp.int32)) * (1 - ai) * cj
                slot = own * (SLOTS - 1) + (1 - own) * gi
                there = (1 - own) * ai
                weight = (plain + own).astype(F32) * (1.0 - 0.5 * (si == sj).astype(F32))
                stay = (there == h).astype(F32)
                share = gathered[((bj & 1) * RING + (bj >> 1)) * SLOTS + slot]
                sides.append(share * (weight * stay) + pltpu.roll(share, SUB, 1) * (weight * (1.0 - stay)))
            high, low = split(jnp.where(narrow, sides[0], sides[1]))
            a_hi[row, p * 128:(p + 1) * 128] = high
            a_lo[row, p * 128:(p + 1) * 128] = low
        return carry

    lax.fori_loop(0, NS1, select, 0)

    def send(src, dst, send_sem, recv_sem, to):
        copy = pltpu.make_async_remote_copy(
            src_ref=src, dst_ref=dst, send_sem=send_sem, recv_sem=recv_sem, device_id=to, device_id_type=MESH)
        copy.start()
        return copy

    started = []

    def first_hop(axis, chunk, half, recv, sends, recvs):
        me = place[axis]
        plus, minus = around[axis]
        far, nxt, prv = lax.rem(me + 2, SIDE), lax.rem(me + 1, SIDE), lax.rem(me + 3, SIDE)
        started.append(send(chunk(far, 0), recv.at[0], sends.at[0], recvs.at[0], plus))
        started.append(send(chunk(far, 1), recv.at[2], sends.at[2], recvs.at[2], minus))
        started.append(send(chunk(nxt, 1), recv.at[1], sends.at[1], recvs.at[1], plus))
        started.append(send(chunk(prv, 0), recv.at[3], sends.at[3], recvs.at[3], minus))

    def second_hop(axis, chunk, half, recv, comb, sends, recvs):
        me = place[axis]
        plus, minus = around[axis]
        nxt, prv = lax.rem(me + 1, SIDE), lax.rem(me + 3, SIDE)
        await_bytes(recv.at[0], recvs.at[0])
        comb[0] = recv[0] + chunk(nxt, 0)[...]
        started.append(send(comb.at[0], recv.at[4], sends.at[4], recvs.at[4], plus))
        await_bytes(recv.at[2], recvs.at[2])
        comb[1] = recv[2] + chunk(prv, 1)[...]
        started.append(send(comb.at[1], recv.at[5], sends.at[5], recvs.at[5], minus))

    def arrive(recv, recvs):
        for slot in (1, 3, 4, 5):
            await_bytes(recv.at[slot], recvs.at[slot])

    def left_rows(r, carry):
        at = pl.ds(pl.multiple_of(r * BS, BS), BS)
        ysum[0, pl.ds(r * 4, 4)] = product((a_hi[at, :], a_lo[at, :]), (w_hi[0], w_lo[0])).reshape(4, SUB, 2 * BS)
        return carry

    lax.fori_loop(0, 3, left_rows, 0)

    def gram(left, right):
        at = slice(left * BS, (left + 1) * BS)
        return product((wt_hi[at, :], wt_lo[at, :]), split(ysum[0, :, :, right * BS:(right + 1) * BS].reshape(ROWS, BS)))

    def put_gram(index, value):
        for part in range(16):
            if part * 48 // BS > index or (part * 48 + 47) // BS < index:
                continue
            low, high = max(part * 48, index * BS), min(part * 48 + 48, index * BS + BS)
            gsend[part // 8, part % 8 // 2, part % 2, low - part * 48:high - part * 48, :] = (
                value[low - index * BS:high - index * BS, :])

    h00 = gram(0, 0)
    put_gram(0, h00 + h00.T)
    put_gram(1, gram(0, 1) + gram(1, 0).T)
    h11 = gram(1, 1)
    put_gram(2, h11 + h11.T)

    def g_chunk(axis):
        return lambda t, h: gsend.at[axis, t, h]

    def y_chunk(axis):
        return lambda t, h: ysend.at[axis, t, h]

    for axis in (0, 1):
        first_hop(axis, g_chunk(axis), 48, grecv.at[axis], g_send_sem.at[axis], g_recv_sem.at[axis])

    def pack_rows(source, axis):
        for n in range(OUTS):
            if n < NS1:
                value = ysum[source, n, :, 0:BS]
            else:
                value = ysum[source, leaf[0, n - NS1], :, BS:2 * BS]
            for t in range(SIDE):
                ysend[axis, t, n // 9, n % 9] = value[t * SLICE:(t + 1) * SLICE, :]

    pack_rows(0, 1)
    first_hop(1, y_chunk(1), 9, yrecv.at[1], y_send_sem.at[1], y_recv_sem.at[1])

    for axis in (0, 1):
        second_hop(axis, g_chunk(axis), 48, grecv.at[axis], gcomb.at[axis], g_send_sem.at[axis], g_recv_sem.at[axis])

    def right_rows(r, carry):
        at = pl.ds(pl.multiple_of(r * BS, BS), BS)
        ysum[1, pl.ds(r * 4, 4)] = product_t((a_hi[:, at], a_lo[:, at]), (w_hi[1], w_lo[1])).reshape(4, SUB, 2 * BS)
        return carry

    lax.fori_loop(0, 3, right_rows, 0)

    def g_sum_and_exchange(axis):
        recv, recvs, sends = grecv.at[axis], g_recv_sem.at[axis], g_send_sem.at[axis]
        me = place[axis]
        arrive(recv, recvs)
        gred[axis, 0] = (gsend[axis, me, 0] + recv[3]) + recv[4]
        gred[axis, 1] = (gsend[axis, me, 1] + recv[1]) + recv[5]
        plus, minus = around[1 - axis]
        started.append(send(gred.at[axis], gexch.at[axis, 0], sends.at[6], recvs.at[6], plus))
        started.append(send(gred.at[axis], gexch.at[axis, 1], sends.at[7], recvs.at[7], minus))

    def g_exchange_on(axis):
        recvs, sends = g_recv_sem.at[axis], g_send_sem.at[axis]
        plus, minus = around[1 - axis]
        await_bytes(gexch.at[axis, 0], recvs.at[6])
        started.append(send(gexch.at[axis, 0, 0], gexch.at[axis, 2, 0], sends.at[8], recvs.at[8], plus))
        await_bytes(gexch.at[axis, 1], recvs.at[7])
        started.append(send(gexch.at[axis, 1, 1], gexch.at[axis, 2, 1], sends.at[9], recvs.at[9], minus))

    def g_spread(axis):
        recvs, sends = g_recv_sem.at[axis], g_send_sem.at[axis]
        me = place[axis]
        plus, minus = around[axis]
        await_bytes(gexch.at[axis, 2, 0], recvs.at[8])
        await_bytes(gexch.at[axis, 2, 1], recvs.at[9])
        gall[axis, me] = (gred[axis] + gexch[axis, 2]) + (gexch[axis, 0] + gexch[axis, 1])
        started.append(send(gall.at[axis, me], gall.at[axis, me], sends.at[10], recvs.at[10], plus))
        started.append(send(gall.at[axis, me], gall.at[axis, me], sends.at[11], recvs.at[11], minus))

    def g_spread_on(axis):
        recvs, sends = g_recv_sem.at[axis], g_send_sem.at[axis]
        me = place[axis]
        plus, minus = around[axis]
        prv, nxt, far = lax.rem(me + 3, SIDE), lax.rem(me + 1, SIDE), lax.rem(me + 2, SIDE)
        await_bytes(gall.at[axis, prv], recvs.at[10])
        started.append(send(gall.at[axis, prv, 0], gall.at[axis, prv, 0], sends.at[12], recvs.at[12], plus))
        await_bytes(gall.at[axis, nxt], recvs.at[11])
        started.append(send(gall.at[axis, nxt, 1], gall.at[axis, nxt, 1], sends.at[13], recvs.at[13], minus))

    for axis in (0, 1):
        g_sum_and_exchange(axis)
    pack_rows(1, 0)
    first_hop(0, y_chunk(0), 9, yrecv.at[0], y_send_sem.at[0], y_recv_sem.at[0])
    for axis in (0, 1):
        g_exchange_on(axis)
    second_hop(1, y_chunk(1), 9, yrecv.at[1], ycomb.at[1], y_send_sem.at[1], y_recv_sem.at[1])
    for axis in (0, 1):
        g_spread(axis)
    second_hop(0, y_chunk(0), 9, yrecv.at[0], ycomb.at[0], y_send_sem.at[0], y_recv_sem.at[0])
    for axis in (0, 1):
        g_spread_on(axis)

    for axis in (1, 0):
        arrive(yrecv.at[axis], y_recv_sem.at[axis])
    for half, direct, through in ((0, 3, 4), (1, 1, 5)):
        total = 0.0
        for axis in (0, 1):
            total = total + ((ysend[axis, place[axis], half] + yrecv[axis, direct]) + yrecv[axis, through])
        ycomb[2, half] = -total
    for n in range(NS1):
        mid_out[n] = ycomb[2, n // 9, n % 9]
        index, mark = leaf_of(n)
        leaf_out[n] = ycomb[2, 1, index + (NS1 - 9)] * mark

    for axis in (0, 1):
        far = lax.rem(place[axis] + 2, SIDE)
        await_bytes(gall.at[axis, far, 0], g_recv_sem.at[axis, 12])
        await_bytes(gall.at[axis, far, 1], g_recv_sem.at[axis, 13])
    total = gall[...].reshape(3 * BS, BS)
    diag_out[...] = total[0:BS] + base[0]
    parent_out[...] = total[BS:2 * BS] + base[1]
    leaf_diag_out[...] = total[2 * BS:3 * BS] + base[2]

    for copy in started:
        copy.wait_send()
    await_bytes(packed.at[pl.ds(0, SIDE * SIDE - 1)], pack_send)

    @pl.when(grid == branch)
    def _():
        await_bytes(extra.at[pl.ds(0, SIDE * SIDE - 1)], extra_send)

    await_bytes(slots(core, 0, 0, (RING - 1) * SLOTS), z_send)
    await_bytes(slots(core, 0, 0, RING * SLOTS), pair_send)


def on_device(sigma_top, mid_struct, leaf_struct, mid_inv, mid_off, leaf_inv, leaf_off):
    smem = pl.BlockSpec(memory_space=pltpu.SMEM)
    vmem = pl.BlockSpec(memory_space=pltpu.VMEM)
    hbm = pl.BlockSpec(memory_space=pl.ANY)
    dma = pltpu.SemaphoreType.DMA
    outs = pl.pallas_call(
        kernel,
        out_shape=(
            jax.ShapeDtypeStruct((NS1, SLICE, BS), F32),
            jax.ShapeDtypeStruct((BS, BS), F32),
            jax.ShapeDtypeStruct((NS1, SLICE, BS), F32),
            jax.ShapeDtypeStruct((BS, BS), F32),
            jax.ShapeDtypeStruct((BS, BS), F32),
        ),
        in_specs=[smem, smem, vmem, hbm, hbm, hbm, hbm],
        out_specs=(vmem,) * 5,
        scratch_shapes=[
            pltpu.VMEM((SIDE * SIDE, SUB, 128), F32),
            pltpu.VMEM((SIDE * SIDE, SUB, 128), F32),
            pltpu.VMEM((2 * RING * SLOTS, SUB, 128), F32),
            pltpu.VMEM((2, NS1, SUB, BS), F32),
            pltpu.VMEM((2, NS2, SUB, BS), F32),
            pltpu.VMEM((BS, BS), F32),
            pltpu.VMEM((BS, BS), F32),
            pltpu.VMEM((BS, BS), F32),
            pltpu.VMEM((2, NS2, SUB, BS), F32),
            pltpu.VMEM((BS, BS), BF16),
            pltpu.VMEM((BS, BS), BF16),
            pltpu.VMEM((3, BS, BS), F32),
            pltpu.VMEM((2, ROWS, 2 * BS), BF16),
            pltpu.VMEM((2, ROWS, 2 * BS), BF16),
            pltpu.VMEM((2 * BS, ROWS), BF16),
            pltpu.VMEM((2 * BS, ROWS), BF16),
            pltpu.VMEM((ROWS, ROWS), BF16),
            pltpu.VMEM((ROWS, ROWS), BF16),
            pltpu.VMEM((2, NS1, SUB, 2 * BS), F32),
            pltpu.VMEM((2, SIDE, 2, 9, SLICE, BS), F32),
            pltpu.VMEM((2, 6, 9, SLICE, BS), F32),
            pltpu.VMEM((3, 2, 9, SLICE, BS), F32),
            pltpu.VMEM((2, SIDE, 2, 48, BS), F32),
            pltpu.VMEM((2, 6, 48, BS), F32),
            pltpu.VMEM((2, 2, 48, BS), F32),
            pltpu.VMEM((2, 2, 48, BS), F32),
            pltpu.VMEM((2, 3, 2, 48, BS), F32),
            pltpu.VMEM((2, SIDE, 2, 48, BS), F32),
            dma((13,)),
            dma,
            dma((4,)),
            dma,
            dma,
            dma,
            dma((5, 4)),
            dma((5, 4)),
            dma,
            dma,
            dma((2, 6)),
            dma((2, 6)),
            dma((2, 14)),
            dma((2, 14)),
        ],
        compiler_params=pltpu.CompilerParams(
            collective_id=0, has_side_effects=True, vmem_limit_bytes=52 * 1024 * 1024),
    )(mid_struct, leaf_struct, sigma_top, mid_inv, mid_off, leaf_inv, leaf_off)
    return tuple(out[None] for out in outs)


def solution(mesh):
    in_specs = (
        P("grid", "branch"),
        P("branch", None),
        P("branch", None),
        P("branch", None, None),
        P("branch", None, None, None),
        P("branch", None, None),
        P("branch", None, None, None),
    )
    out_specs = (
        P("branch", None, "grid", None),
        P("branch", None, None),
        P("branch", None, "grid", None),
        P("branch", None, None),
        P("branch", None, None),
    )
    return jax.shard_map(
        on_device, mesh=mesh, in_specs=in_specs, out_specs=out_specs, check_vma=False
    )
```

```python
import jax
import jax.numpy as jnp
from jax import lax
from jax.experimental import pallas as pl
from jax.experimental.pallas import tpu as pltpu
from jax.sharding import PartitionSpec as P

MESH = pl.DeviceIdType.MESH
F32 = jnp.float32
BF16 = jnp.bfloat16
BS = 256
NS1 = 12
NS2 = 6
SIDE = 4
RING = 8
SUB = BS // SIDE
SLICE = 16
SLOTS = 17
HALF = SUB // 2
PIECES = ((0, 0, 8), (0, 8, 9), (1, 0, 8), (1, 8, 9))
ROWS = NS1 * SUB
OUTS = NS1 + NS2


def split(value):
    high = value.astype(BF16)
    return high, (value - high.astype(F32)).astype(BF16)


def product(left, right, dims=(((1,), (0,)), ((), ()))):
    def one(a, b):
        return lax.dot_general(a, b, dims, preferred_element_type=F32)
    return one(left[0], right[0]) + (one(left[0], right[1]) + one(left[1], right[0]))


def product_t(left, right):
    return product(left, right, (((0,), (0,)), ((), ())))


def kernel(
    struct_hbm, leaf_hbm, sigma_hbm, minv_hbm, moff_hbm, linv_hbm, loff_hbm,
    mid_hbm, column_hbm, gram_hbm,
    struct, leaf, sigma, packed, extra, gathered, moff, loff, first_raw, minv, linv, vblocks, v0_hi, v0_lo, base,
    w_hi, w_lo, wt_hi, wt_lo, a_hi, a_lo, ysum, ysend, yrecv, ycomb, gsend, grecv, gcomb, gred, gexch, gall,
    column_out, gram_out, out_sem,
    load_sem, pack_send, pack_recv, extra_send, extra_recv, z_send, right_recv, left_recv,
    pair_send, pair_recv, y_send_sem, y_recv_sem, g_send_sem, g_recv_sem,
):
    branch = lax.axis_index("branch")
    grid = lax.axis_index("grid")
    z, core = branch // 2, branch % 2
    y, x = grid // SIDE, grid % SIDE

    def slots(which_core, source, half, slot, size=None):
        start = ((which_core * RING + source) * 2 + half) * SLOTS + slot
        return gathered.at[start] if size is None else gathered.at[pl.ds(start, size)]

    def at_grid(index):
        return {"branch": branch, "grid": index}

    def at_branch(index):
        return {"branch": index, "grid": grid}

    up = at_branch(lax.rem(z + 1, RING) * 2 + core)
    down = at_branch(lax.rem(z + RING - 1, RING) * 2 + core)
    pair = at_branch(z * 2 + (1 - core))
    around = (
        (at_grid(y * SIDE + lax.rem(x + 1, SIDE)), at_grid(y * SIDE + lax.rem(x + SIDE - 1, SIDE))),
        (at_grid(lax.rem(y + 1, SIDE) * SIDE + x), at_grid(lax.rem(y + SIDE - 1, SIDE) * SIDE + x)),
    )
    place = (x, y)

    row_c = pl.multiple_of(y * SUB, SUB)
    loads = [
        pltpu.make_async_copy(minv_hbm.at[0], minv, load_sem.at[0]),
        pltpu.make_async_copy(linv_hbm.at[0], linv, load_sem.at[1]),
        pltpu.make_async_copy(loff_hbm.at[0, 0], first_raw, load_sem.at[2]),
        pltpu.make_async_copy(moff_hbm.at[0, :, pl.ds(row_c, SUB), :], moff.at[0], load_sem.at[3]),
        pltpu.make_async_copy(loff_hbm.at[0, pl.ds(1, NS2), pl.ds(row_c, SUB), :], loff.at[0], load_sem.at[4]),
    ]
    for m in range(SIDE):
        row_r = pl.multiple_of(m * SUB + x * SLICE, SLICE)
        into = pl.ds(m * SLICE, SLICE)
        loads.append(pltpu.make_async_copy(
            moff_hbm.at[0, :, pl.ds(row_r, SLICE), :], moff.at[1, :, into, :], load_sem.at[5 + m]))
        loads.append(pltpu.make_async_copy(
            loff_hbm.at[0, pl.ds(1, NS2), pl.ds(row_r, SLICE), :], loff.at[1, :, into, :], load_sem.at[9 + m]))
    loads.append(pltpu.make_async_copy(struct_hbm, struct, load_sem.at[13]))
    loads.append(pltpu.make_async_copy(leaf_hbm, leaf, load_sem.at[14]))
    own = pltpu.make_async_copy(sigma_hbm, sigma, load_sem.at[15])
    own.start()

    barrier = pltpu.get_barrier_semaphore()

    def greet(step, carry):
        pl.semaphore_signal(
            barrier, inc=1, device_id=at_grid(lax.rem(grid + step, SIDE * SIDE)), device_id_type=MESH)
        return carry

    lax.fori_loop(1, SIDE * SIDE, greet, 0)
    for other in (up, down, pair):
        pl.semaphore_signal(barrier, inc=1, device_id=other, device_id_type=MESH)

    for load in loads:
        load.start()
    own.wait()

    flip = (grid > branch).astype(jnp.int32)
    lane = lax.broadcasted_iota(jnp.int32, (BS, 128), 1)
    for half in range(2):
        one = sigma[0:BS, pl.ds(pl.multiple_of(flip * BS + half * 128, 128), 128)]
        two = sigma[BS:2 * BS, pl.ds(pl.multiple_of((1 - flip) * BS + half * 128, 128), 128)]
        even = jnp.where(lane < SUB, one, pltpu.roll(two, SUB, 1))
        odd = jnp.where(lane < SUB, pltpu.roll(one, SUB, 1), two)
        for side, value in ((2 * half, even), (2 * half + 1, odd)):
            for m in range(SIDE):
                for xx in range(SIDE):
                    start = m * SUB + xx * SLICE
                    packed[m // 2, side * SIDE + xx, m % 2 * SLICE:(m % 2 + 1) * SLICE, :] = value[start:start + SLICE, :]

    @pl.when(grid == branch)
    def _():
        for half in range(2):
            value = sigma[0:BS, BS + half * 128:BS + (half + 1) * 128]
            for side, turned in ((2 * half, value), (2 * half + 1, pltpu.roll(value, SUB, 1))):
                for m in range(SIDE):
                    for xx in range(SIDE):
                        start = m * SUB + xx * SLICE
                        extra[m // 2, side * SIDE + xx, m % 2 * SLICE:(m % 2 + 1) * SLICE, :] = turned[start:start + SLICE, :]

    pl.semaphore_wait(barrier, SIDE * SIDE + 2)

    for half in range(2):
        pltpu.make_async_copy(packed.at[half, grid], slots(core, z, half, grid), pack_recv.at[half]).start()

        def hand_out(step, carry):
            to = lax.rem(grid + step, SIDE * SIDE)
            pltpu.make_async_remote_copy(
                src_ref=packed.at[half, to], dst_ref=slots(core, z, half, grid), send_sem=pack_send,
                recv_sem=pack_recv.at[half], device_id=at_grid(to), device_id_type=MESH).start()
            return carry

        lax.fori_loop(1, SIDE * SIDE, hand_out, 0)

        @pl.when(grid == branch)
        def _():
            own_slot = slots(core, z, half, SLOTS - 1)
            pltpu.make_async_copy(extra.at[half, grid], own_slot, extra_recv.at[half]).start()

            def hand_extra(step, carry):
                to = lax.rem(grid + step, SIDE * SIDE)
                pltpu.make_async_remote_copy(
                    src_ref=extra.at[half, to], dst_ref=own_slot, send_sem=extra_send,
                    recv_sem=extra_recv.at[half], device_id=at_grid(to), device_id_type=MESH).start()
                return carry

            lax.fori_loop(1, SIDE * SIDE, hand_extra, 0)

    def piece_of(source, piece):
        half, start, size = PIECES[piece]
        return slots(core, source, half, start, size)

    def pass_on(source, piece, to, recv_sem):
        ref = piece_of(source, piece)
        pltpu.make_async_remote_copy(
            src_ref=ref, dst_ref=ref, send_sem=z_send, recv_sem=recv_sem, device_id=to, device_id_type=MESH).start()

    def to_pair(source, piece):
        ref = piece_of(source, piece)
        pltpu.make_async_remote_copy(
            src_ref=ref, dst_ref=ref, send_sem=pair_send, recv_sem=pair_recv, device_id=pair,
            device_id_type=MESH).start()

    def await_bytes(ref, sem):
        pltpu.make_async_copy(ref, ref, sem).wait()

    for piece in range(4):
        half = PIECES[piece][0]
        if piece % 2 == 0:
            await_bytes(slots(core, z, half, 0, SIDE * SIDE), pack_recv.at[half])
            await_bytes(slots(core, z, half, SLOTS - 1), extra_recv.at[half])
        pass_on(z, piece, up, right_recv.at[1, piece])
        pass_on(z, piece, down, left_recv.at[1, piece])
        to_pair(z, piece)

    def leaf_of(k):
        found, index = 0, 0
        for t in range(NS2):
            same = (leaf[0, t] == k).astype(jnp.int32)
            found = found + same
            index = index + same * t
        return jnp.minimum(index, NS2 - 1), found.astype(F32)

    def factors():
        for load in loads:
            load.wait()
        minv_s = split(minv[...])
        linv_s = split(linv[...])
        v0_s = split(product(split(first_raw[...]), linv_s))
        v0_hi[...], v0_lo[...] = v0_s
        for part in range(2):
            vblocks[part] = product(split(loff[part].reshape(NS2 * SUB, BS)), linv_s).reshape(NS2, SUB, BS)
        square = product_t(minv_s, minv_s)
        base[0] = square
        turned = product(split(square), v0_s)
        base[1] = -turned
        base[2] = product_t(linv_s, linv_s) + product_t(v0_s, split(turned))
        for part in range(2):
            def rows(q, carry):
                raw = moff[part, pl.ds(q * 4, 4)].reshape(BS, BS)
                u = product(split(raw), (split(minv[...])))
                u_s = split(u)
                uv = product(u_s, (v0_hi[...], v0_lo[...]))
                spread = []
                for j in range(4):
                    index, mark = leaf_of(q * 4 + j)
                    spread.append(vblocks[part, index] * mark)
                t = jnp.concatenate(spread, axis=0) - uv
                t_s = split(t)
                at = pl.ds(pl.multiple_of(q * BS, BS), BS)
                for kind, pieces in ((0, u_s), (1, t_s)):
                    w_hi[part, at, kind * BS:(kind + 1) * BS] = pieces[0]
                    w_lo[part, at, kind * BS:(kind + 1) * BS] = pieces[1]
                if part == 1:
                    for kind, value in ((0, u), (1, t)):
                        high, low = split(value.T)
                        wt_hi[kind * BS:(kind + 1) * BS, at] = high
                        wt_lo[kind * BS:(kind + 1) * BS, at] = low
                return carry
            lax.fori_loop(0, 3, rows, 0)

    factors()

    for step in range(1, 5):
        below = lax.rem(z + RING - step, RING)
        above = lax.rem(z + step, RING)
        for piece in range(4):
            if step < 4 or piece < 2:
                await_bytes(piece_of(below, piece), right_recv.at[step, piece])
                if step < 3 or (step == 3 and piece < 2):
                    pass_on(below, piece, up, right_recv.at[step + 1, piece])
                to_pair(below, piece)
            if step < 4 or piece >= 2:
                await_bytes(piece_of(above, piece), left_recv.at[step, piece])
                if step < 3 or (step == 3 and piece >= 2):
                    pass_on(above, piece, down, left_recv.at[step + 1, piece])
                to_pair(above, piece)
    await_bytes(slots(1 - core, 0, 0, 0, 2 * RING * SLOTS), pair_recv)

    narrow = lax.broadcasted_iota(jnp.int32, (HALF, 128), 1) < SUB

    def select(k, carry):
        si = struct[0, k]
        gi, ai = si >> 1, si & 1
        for p in range(NS1 // 2):
            sides = [[], []]
            for h in range(2):
                sj = struct[0, 2 * p + h]
                bj, cj = sj >> 1, sj & 1
                beyond = (gi > bj).astype(jnp.int32)
                plain = (cj == (ai ^ beyond)).astype(jnp.int32)
                own = ((gi == bj).astype(jnp.int32)) * (1 - ai) * cj
                slot = own * (SLOTS - 1) + (1 - own) * gi
                there = (1 - own) * ai
                weight = (plain + own).astype(F32) * (1.0 - 0.5 * (si == sj).astype(F32))
                stay = (there == h).astype(F32)
                for half in range(2):
                    share = gathered[(((bj & 1) * RING + (bj >> 1)) * 2 + half) * SLOTS + slot]
                    sides[half].append(
                        share * (weight * stay) + pltpu.roll(share, SUB, 1) * (weight * (1.0 - stay)))
            for half in range(2):
                row = pl.ds(pl.multiple_of(k * SUB + half * HALF, HALF), HALF)
                high, low = split(jnp.where(narrow, sides[half][0], sides[half][1]))
                a_hi[row, p * 128:(p + 1) * 128] = high
                a_lo[row, p * 128:(p + 1) * 128] = low
        return carry

    lax.fori_loop(0, NS1, select, 0)

    def send(src, dst, send_sem, recv_sem, to):
        copy = pltpu.make_async_remote_copy(
            src_ref=src, dst_ref=dst, send_sem=send_sem, recv_sem=recv_sem, device_id=to, device_id_type=MESH)
        copy.start()
        return copy

    started = []

    def first_hop(axis, chunk, recv, sends, recvs):
        plus, minus = around[axis]
        far = lax.rem(place[axis] + 2, SIDE)
        started.append(send(chunk(far, 0), recv.at[0], sends.at[0], recvs.at[0], plus))
        started.append(send(chunk(far, 1), recv.at[2], sends.at[2], recvs.at[2], minus))

    def direct_hop(axis, chunk, recv, sends, recvs):
        plus, minus = around[axis]
        nxt, prv = lax.rem(place[axis] + 1, SIDE), lax.rem(place[axis] + 3, SIDE)
        started.append(send(chunk(nxt, 1), recv.at[1], sends.at[1], recvs.at[1], plus))
        started.append(send(chunk(prv, 0), recv.at[3], sends.at[3], recvs.at[3], minus))

    def second_hop(axis, chunk, recv, comb, sends, recvs):
        me = place[axis]
        plus, minus = around[axis]
        nxt, prv = lax.rem(me + 1, SIDE), lax.rem(me + 3, SIDE)
        await_bytes(recv.at[0], recvs.at[0])
        comb[0] = recv[0] + chunk(nxt, 0)[...]
        started.append(send(comb.at[0], recv.at[4], sends.at[4], recvs.at[4], plus))
        await_bytes(recv.at[2], recvs.at[2])
        comb[1] = recv[2] + chunk(prv, 1)[...]
        started.append(send(comb.at[1], recv.at[5], sends.at[5], recvs.at[5], minus))

    def arrive(recv, recvs):
        for slot in (1, 3, 4, 5):
            await_bytes(recv.at[slot], recvs.at[slot])

    def left_rows(r, carry):
        at = pl.ds(pl.multiple_of(r * BS, BS), BS)
        ysum[0, pl.ds(r * 4, 4)] = product((a_hi[at, :], a_lo[at, :]), (w_hi[0], w_lo[0])).reshape(4, SUB, 2 * BS)
        return carry

    def gram(left, right):
        at = slice(left * BS, (left + 1) * BS)
        return product((wt_hi[at, :], wt_lo[at, :]), split(ysum[0, :, :, right * BS:(right + 1) * BS].reshape(ROWS, BS)))

    def put_gram(index, value):
        for part in range(16):
            if part * 48 // BS > index or (part * 48 + 47) // BS < index:
                continue
            low, high = max(part * 48, index * BS), min(part * 48 + 48, index * BS + BS)
            gsend[part // 8, part % 8 // 2, part % 2, low - part * 48:high - part * 48, :] = (
                value[low - index * BS:high - index * BS, :])

    def g_chunk(axis):
        return lambda t, h: gsend.at[axis, t, h]

    def y_chunk(axis):
        return lambda t, h: ysend.at[axis, t, h]

    def g_ring(axis):
        return axis, g_chunk(axis), grecv.at[axis], g_send_sem.at[axis], g_recv_sem.at[axis]

    def y_ring(axis):
        return axis, y_chunk(axis), yrecv.at[axis], y_send_sem.at[axis], y_recv_sem.at[axis]

    def pack_rows(source, axis):
        for n in range(OUTS):
            if n < NS1:
                value = ysum[source, n, :, 0:BS]
            else:
                value = ysum[source, leaf[0, n - NS1], :, BS:2 * BS]
            for t in range(SIDE):
                ysend[axis, t, n // 9, n % 9] = value[t * SLICE:(t + 1) * SLICE, :]

    def right_rows(r, carry):
        at = pl.ds(pl.multiple_of(r * BS, BS), BS)
        ysum[1, pl.ds(r * 4, 4)] = product_t((a_hi[:, at], a_lo[:, at]), (w_hi[1], w_lo[1])).reshape(4, SUB, 2 * BS)
        return carry


    def g_sum_and_exchange(axis):
        recv, recvs, sends = grecv.at[axis], g_recv_sem.at[axis], g_send_sem.at[axis]
        me = place[axis]
        arrive(recv, recvs)
        gred[axis, 0] = (gsend[axis, me, 0] + recv[3]) + recv[4]
        gred[axis, 1] = (gsend[axis, me, 1] + recv[1]) + recv[5]
        plus, minus = around[1 - axis]
        started.append(send(gred.at[axis], gexch.at[axis, 0], sends.at[6], recvs.at[6], plus))
        started.append(send(gred.at[axis], gexch.at[axis, 1], sends.at[7], recvs.at[7], minus))

    def g_exchange_on(axis):
        recvs, sends = g_recv_sem.at[axis], g_send_sem.at[axis]
        plus, minus = around[1 - axis]
        await_bytes(gexch.at[axis, 0], recvs.at[6])
        started.append(send(gexch.at[axis, 0, 0], gexch.at[axis, 2, 0], sends.at[8], recvs.at[8], plus))
        await_bytes(gexch.at[axis, 1], recvs.at[7])
        started.append(send(gexch.at[axis, 1, 1], gexch.at[axis, 2, 1], sends.at[9], recvs.at[9], minus))

    def g_spread(axis):
        recvs, sends = g_recv_sem.at[axis], g_send_sem.at[axis]
        me = place[axis]
        plus, minus = around[axis]
        await_bytes(gexch.at[axis, 2, 0], recvs.at[8])
        await_bytes(gexch.at[axis, 2, 1], recvs.at[9])
        gall[axis, me] = (gred[axis] + gexch[axis, 2]) + (gexch[axis, 0] + gexch[axis, 1])
        started.append(send(gall.at[axis, me], gall.at[axis, me], sends.at[10], recvs.at[10], plus))
        started.append(send(gall.at[axis, me], gall.at[axis, me], sends.at[11], recvs.at[11], minus))

    def g_spread_on(axis):
        recvs, sends = g_recv_sem.at[axis], g_send_sem.at[axis]
        me = place[axis]
        plus, minus = around[axis]
        prv, nxt, far = lax.rem(me + 3, SIDE), lax.rem(me + 1, SIDE), lax.rem(me + 2, SIDE)
        await_bytes(gall.at[axis, prv], recvs.at[10])
        started.append(send(gall.at[axis, prv, 0], gall.at[axis, prv, 0], sends.at[12], recvs.at[12], plus))
        await_bytes(gall.at[axis, nxt], recvs.at[11])
        started.append(send(gall.at[axis, nxt, 1], gall.at[axis, nxt, 1], sends.at[13], recvs.at[13], minus))

    def g_second(axis):
        second_hop(axis, g_chunk(axis), grecv.at[axis], gcomb.at[axis], g_send_sem.at[axis], g_recv_sem.at[axis])

    def y_second(axis):
        second_hop(axis, y_chunk(axis), yrecv.at[axis], ycomb.at[axis], y_send_sem.at[axis], y_recv_sem.at[axis])

    lax.fori_loop(0, 3, left_rows, 0)
    pack_rows(0, 1)
    first_hop(*y_ring(1))
    h00 = gram(0, 0)
    put_gram(0, h00 + h00.T)
    put_gram(1, gram(0, 1) + gram(1, 0).T)
    h11 = gram(1, 1)
    put_gram(2, h11 + h11.T)
    for axis in (0, 1):
        first_hop(*g_ring(axis))
        direct_hop(*g_ring(axis))
    direct_hop(*y_ring(1))
    lax.fori_loop(0, 3, right_rows, 0)
    pack_rows(1, 0)
    for axis in (0, 1):
        g_second(axis)
    first_hop(*y_ring(0))
    y_second(1)
    for axis in (0, 1):
        g_sum_and_exchange(axis)
    direct_hop(*y_ring(0))
    for axis in (0, 1):
        g_exchange_on(axis)
    y_second(0)
    for axis in (0, 1):
        g_spread(axis)
    for axis in (0, 1):
        g_spread_on(axis)

    for axis in (1, 0):
        arrive(yrecv.at[axis], y_recv_sem.at[axis])
    for half, direct, through in ((0, 3, 4), (1, 1, 5)):
        total = 0.0
        for axis in (0, 1):
            total = total + ((ysend[axis, place[axis], half] + yrecv[axis, direct]) + yrecv[axis, through])
        ycomb[2, half] = -total
    for n in range(NS1):
        column_out[0, n] = ycomb[2, n // 9, n % 9]
        index, mark = leaf_of(n)
        column_out[1, n] = ycomb[2, 1, index + (NS1 - 9)] * mark

    outs = [
        pltpu.make_async_copy(column_out.at[0], mid_hbm, out_sem.at[0]),
        pltpu.make_async_copy(column_out.at[1], column_hbm, out_sem.at[1]),
        pltpu.make_async_copy(gram_out, gram_hbm, out_sem.at[2]),
    ]
    outs[0].start()
    outs[1].start()
    for axis in (0, 1):
        far = lax.rem(place[axis] + 2, SIDE)
        await_bytes(gall.at[axis, far, 0], g_recv_sem.at[axis, 12])
        await_bytes(gall.at[axis, far, 1], g_recv_sem.at[axis, 13])
    gram_out[...] = gall[...].reshape(3, BS, BS) + base[...]

    outs[2].start()

    for copy in started:
        copy.wait_send()
    for half in range(2):
        await_bytes(packed.at[half, pl.ds(0, SIDE * SIDE - 1)], pack_send)

    @pl.when(grid == branch)
    def _():
        for half in range(2):
            await_bytes(extra.at[half, pl.ds(0, SIDE * SIDE - 1)], extra_send)

    await_bytes(slots(core, 0, 0, 0, 2 * (RING - 1) * SLOTS), z_send)
    await_bytes(slots(core, 0, 0, 0, 2 * RING * SLOTS), pair_send)
    for copy in outs:
        copy.wait()


def write_out(mid, leaf, gram, mid_out, diag_out, leaf_out, parent_out, leaf_diag_out, sem):
    copies = [
        pltpu.make_async_copy(src, dst.at[0], sem.at[n]) for n, (src, dst) in enumerate((
            (mid, mid_out), (leaf, leaf_out), (gram.at[0], diag_out), (gram.at[1], parent_out),
            (gram.at[2], leaf_diag_out)))]
    for copy in copies:
        copy.start()
    for copy in copies:
        copy.wait()


def on_device(sigma_top, mid_struct, leaf_struct, mid_inv, mid_off, leaf_inv, leaf_off):
    hbm = pl.BlockSpec(memory_space=pltpu.HBM)
    anywhere = pl.BlockSpec(memory_space=pl.ANY)
    dma = pltpu.SemaphoreType.DMA
    middle, leaves, grams = pl.pallas_call(
        kernel,
        out_shape=(
            jax.ShapeDtypeStruct((NS1, SLICE, BS), F32),
            jax.ShapeDtypeStruct((NS1, SLICE, BS), F32),
            jax.ShapeDtypeStruct((3, BS, BS), F32),
        ),
        in_specs=[hbm] * 7,
        out_specs=(hbm,) * 3,
        scratch_shapes=[
            pltpu.SMEM((1, NS1), jnp.int32),
            pltpu.SMEM((1, NS2), jnp.int32),
            pltpu.VMEM((2 * BS, 2 * BS), F32),
            pltpu.VMEM((2, SIDE * SIDE, HALF, 128), F32),
            pltpu.VMEM((2, SIDE * SIDE, HALF, 128), F32),
            pltpu.VMEM((4 * RING * SLOTS, HALF, 128), F32),
            pltpu.VMEM((2, NS1, SUB, BS), F32),
            pltpu.VMEM((2, NS2, SUB, BS), F32),
            pltpu.VMEM((BS, BS), F32),
            pltpu.VMEM((BS, BS), F32),
            pltpu.VMEM((BS, BS), F32),
            pltpu.VMEM((2, NS2, SUB, BS), F32),
            pltpu.VMEM((BS, BS), BF16),
            pltpu.VMEM((BS, BS), BF16),
            pltpu.VMEM((3, BS, BS), F32),
            pltpu.VMEM((2, ROWS, 2 * BS), BF16),
            pltpu.VMEM((2, ROWS, 2 * BS), BF16),
            pltpu.VMEM((2 * BS, ROWS), BF16),
            pltpu.VMEM((2 * BS, ROWS), BF16),
            pltpu.VMEM((ROWS, ROWS), BF16),
            pltpu.VMEM((ROWS, ROWS), BF16),
            pltpu.VMEM((2, NS1, SUB, 2 * BS), F32),
            pltpu.VMEM((2, SIDE, 2, 9, SLICE, BS), F32),
            pltpu.VMEM((2, 6, 9, SLICE, BS), F32),
            pltpu.VMEM((3, 2, 9, SLICE, BS), F32),
            pltpu.VMEM((2, SIDE, 2, 48, BS), F32),
            pltpu.VMEM((2, 6, 48, BS), F32),
            pltpu.VMEM((2, 2, 48, BS), F32),
            pltpu.VMEM((2, 2, 48, BS), F32),
            pltpu.VMEM((2, 3, 2, 48, BS), F32),
            pltpu.VMEM((2, SIDE, 2, 48, BS), F32),
            pltpu.VMEM((2, NS1, SLICE, BS), F32),
            pltpu.VMEM((3, BS, BS), F32),
            dma((3,)),
            dma((16,)),
            dma,
            dma((2,)),
            dma,
            dma((2,)),
            dma,
            dma((5, 4)),
            dma((5, 4)),
            dma,
            dma,
            dma((2, 6)),
            dma((2, 6)),
            dma((2, 14)),
            dma((2, 14)),
        ],
        compiler_params=pltpu.CompilerParams(
            collective_id=0, has_side_effects=True, vmem_limit_bytes=64 * 1024 * 1024),
    )(mid_struct, leaf_struct, sigma_top, mid_inv, mid_off, leaf_inv, leaf_off)
    block = jax.ShapeDtypeStruct((1, BS, BS), F32)
    column = jax.ShapeDtypeStruct((1, NS1, SLICE, BS), F32)
    return tuple(pl.pallas_call(
        write_out,
        out_shape=(column, block, column, block, block),
        in_specs=[anywhere] * 3,
        out_specs=(anywhere,) * 5,
        scratch_shapes=[dma((5,))],
    )(middle, leaves, grams))


def solution(mesh):
    in_specs = (
        P("grid", "branch"),
        P("branch", None),
        P("branch", None),
        P("branch", None, None),
        P("branch", None, None, None),
        P("branch", None, None),
        P("branch", None, None, None),
    )
    out_specs = (
        P("branch", None, "grid", None),
        P("branch", None, None),
        P("branch", None, "grid", None),
        P("branch", None, None),
        P("branch", None, None),
    )
    return jax.shard_map(
        on_device, mesh=mesh, in_specs=in_specs, out_specs=out_specs, check_vma=False
    )
```

```python
import jax
import jax.numpy as jnp
from jax import lax
from jax.experimental import pallas as pl
from jax.experimental.pallas import tpu as pltpu
from jax.sharding import PartitionSpec as P

MESH = pl.DeviceIdType.MESH
F32 = jnp.float32
BF16 = jnp.bfloat16
BS = 256
NS1 = 12
NS2 = 6
SIDE = 4
RING = 8
SUB = BS // SIDE
SLICE = 16
SLOTS = 17
HALF = SUB // 2
PIECES = ((0, 0, 8), (0, 8, 9), (1, 0, 8), (1, 8, 9))
ROWS = NS1 * SUB
OUTS = NS1 + NS2


def split(value):
    high = value.astype(BF16)
    return high, (value - high.astype(F32)).astype(BF16)


def product(left, right, dims=(((1,), (0,)), ((), ()))):
    def one(a, b):
        return lax.dot_general(a, b, dims, preferred_element_type=F32)
    return one(left[0], right[0]) + (one(left[0], right[1]) + one(left[1], right[0]))


def product_t(left, right):
    return product(left, right, (((0,), (0,)), ((), ())))


def kernel(
    struct_hbm, leaf_hbm, sigma_hbm, minv_hbm, moff_hbm, linv_hbm, loff_hbm,
    mid_hbm, column_hbm, gram_hbm,
    struct, leaf, sigma, packed, extra, gathered, moff, loff, first_raw, minv, linv, vblocks, v0_hi, v0_lo, base,
    w_hi, w_lo, wt_hi, wt_lo, a_hi, a_lo, ysum, ysend, yrecv, ycomb, gsend, grecv, gcomb, gred, gexch, gall,
    column_out, gram_out, out_sem,
    load_sem, pack_send, pack_recv, extra_send, extra_recv, z_send, right_recv, left_recv,
    pair_send, pair_recv, y_send_sem, y_recv_sem, g_send_sem, g_recv_sem,
):
    branch = lax.axis_index("branch")
    grid = lax.axis_index("grid")
    z, core = branch // 2, branch % 2
    y, x = grid // SIDE, grid % SIDE

    def slots(which_core, source, half, slot, size=None):
        start = ((which_core * RING + source) * 2 + half) * SLOTS + slot
        return gathered.at[start] if size is None else gathered.at[pl.ds(start, size)]

    def at_grid(index):
        return {"branch": branch, "grid": index}

    def at_branch(index):
        return {"branch": index, "grid": grid}

    up = at_branch(lax.rem(z + 1, RING) * 2 + core)
    down = at_branch(lax.rem(z + RING - 1, RING) * 2 + core)
    pair = at_branch(z * 2 + (1 - core))
    around = (
        (at_grid(y * SIDE + lax.rem(x + 1, SIDE)), at_grid(y * SIDE + lax.rem(x + SIDE - 1, SIDE))),
        (at_grid(lax.rem(y + 1, SIDE) * SIDE + x), at_grid(lax.rem(y + SIDE - 1, SIDE) * SIDE + x)),
    )
    place = (x, y)

    row_c = pl.multiple_of(y * SUB, SUB)
    loads = [
        pltpu.make_async_copy(minv_hbm.at[0], minv, load_sem.at[0]),
        pltpu.make_async_copy(linv_hbm.at[0], linv, load_sem.at[1]),
        pltpu.make_async_copy(loff_hbm.at[0, 0], first_raw, load_sem.at[2]),
        pltpu.make_async_copy(moff_hbm.at[0, :, pl.ds(row_c, SUB), :], moff.at[0], load_sem.at[3]),
        pltpu.make_async_copy(loff_hbm.at[0, pl.ds(1, NS2), pl.ds(row_c, SUB), :], loff.at[0], load_sem.at[4]),
    ]
    for m in range(SIDE):
        row_r = pl.multiple_of(m * SUB + x * SLICE, SLICE)
        into = pl.ds(m * SLICE, SLICE)
        loads.append(pltpu.make_async_copy(
            moff_hbm.at[0, :, pl.ds(row_r, SLICE), :], moff.at[1, :, into, :], load_sem.at[5 + m]))
        loads.append(pltpu.make_async_copy(
            loff_hbm.at[0, pl.ds(1, NS2), pl.ds(row_r, SLICE), :], loff.at[1, :, into, :], load_sem.at[9 + m]))
    loads.append(pltpu.make_async_copy(struct_hbm, struct, load_sem.at[13]))
    loads.append(pltpu.make_async_copy(leaf_hbm, leaf, load_sem.at[14]))
    own = pltpu.make_async_copy(sigma_hbm, sigma, load_sem.at[15])
    own.start()

    barrier = pltpu.get_barrier_semaphore()

    def greet(step, carry):
        pl.semaphore_signal(
            barrier, inc=1, device_id=at_grid(lax.rem(grid + step, SIDE * SIDE)), device_id_type=MESH)
        return carry

    lax.fori_loop(1, SIDE * SIDE, greet, 0)
    for other in (up, down, pair):
        pl.semaphore_signal(barrier, inc=1, device_id=other, device_id_type=MESH)

    for load in loads:
        load.start()
    own.wait()

    flip = (grid > branch).astype(jnp.int32)
    lane = lax.broadcasted_iota(jnp.int32, (BS, 128), 1)
    for half in range(2):
        one = sigma[0:BS, pl.ds(pl.multiple_of(flip * BS + half * 128, 128), 128)]
        two = sigma[BS:2 * BS, pl.ds(pl.multiple_of((1 - flip) * BS + half * 128, 128), 128)]
        even = jnp.where(lane < SUB, one, pltpu.roll(two, SUB, 1))
        odd = jnp.where(lane < SUB, pltpu.roll(one, SUB, 1), two)
        for side, value in ((2 * half, even), (2 * half + 1, odd)):
            for m in range(SIDE):
                for xx in range(SIDE):
                    start = m * SUB + xx * SLICE
                    packed[m // 2, side * SIDE + xx, m % 2 * SLICE:(m % 2 + 1) * SLICE, :] = value[start:start + SLICE, :]

    @pl.when(grid == branch)
    def _():
        for half in range(2):
            value = sigma[0:BS, BS + half * 128:BS + (half + 1) * 128]
            for side, turned in ((2 * half, value), (2 * half + 1, pltpu.roll(value, SUB, 1))):
                for m in range(SIDE):
                    for xx in range(SIDE):
                        start = m * SUB + xx * SLICE
                        extra[m // 2, side * SIDE + xx, m % 2 * SLICE:(m % 2 + 1) * SLICE, :] = turned[start:start + SLICE, :]

    pl.semaphore_wait(barrier, SIDE * SIDE + 2)

    for half in range(2):
        pltpu.make_async_copy(packed.at[half, grid], slots(core, z, half, grid), pack_recv.at[half]).start()

        def hand_out(step, carry):
            to = lax.rem(grid + step, SIDE * SIDE)
            pltpu.make_async_remote_copy(
                src_ref=packed.at[half, to], dst_ref=slots(core, z, half, grid), send_sem=pack_send,
                recv_sem=pack_recv.at[half], device_id=at_grid(to), device_id_type=MESH).start()
            return carry

        lax.fori_loop(1, SIDE * SIDE, hand_out, 0)

        @pl.when(grid == branch)
        def _():
            own_slot = slots(core, z, half, SLOTS - 1)
            pltpu.make_async_copy(extra.at[half, grid], own_slot, extra_recv.at[half]).start()

            def hand_extra(step, carry):
                to = lax.rem(grid + step, SIDE * SIDE)
                pltpu.make_async_remote_copy(
                    src_ref=extra.at[half, to], dst_ref=own_slot, send_sem=extra_send,
                    recv_sem=extra_recv.at[half], device_id=at_grid(to), device_id_type=MESH).start()
                return carry

            lax.fori_loop(1, SIDE * SIDE, hand_extra, 0)

    def piece_of(source, piece):
        half, start, size = PIECES[piece]
        return slots(core, source, half, start, size)

    def pass_on(source, piece, to, recv_sem):
        ref = piece_of(source, piece)
        pltpu.make_async_remote_copy(
            src_ref=ref, dst_ref=ref, send_sem=z_send, recv_sem=recv_sem, device_id=to, device_id_type=MESH).start()

    def to_pair(source, piece):
        ref = piece_of(source, piece)
        pltpu.make_async_remote_copy(
            src_ref=ref, dst_ref=ref, send_sem=pair_send, recv_sem=pair_recv, device_id=pair,
            device_id_type=MESH).start()

    def await_bytes(ref, sem):
        pltpu.make_async_copy(ref, ref, sem).wait()

    for piece in range(4):
        half = PIECES[piece][0]
        if piece % 2 == 0:
            await_bytes(slots(core, z, half, 0, SIDE * SIDE), pack_recv.at[half])
            await_bytes(slots(core, z, half, SLOTS - 1), extra_recv.at[half])
        pass_on(z, piece, up, right_recv.at[1, piece])
        pass_on(z, piece, down, left_recv.at[1, piece])
        to_pair(z, piece)

    def leaf_of(k):
        found, index = 0, 0
        for t in range(NS2):
            same = (leaf[0, t] == k).astype(jnp.int32)
            found = found + same
            index = index + same * t
        return jnp.minimum(index, NS2 - 1), found.astype(F32)

    def factors():
        for load in loads:
            load.wait()
        minv_s = split(minv[...])
        linv_s = split(linv[...])
        v0_s = split(product(split(first_raw[...]), linv_s))
        v0_hi[...], v0_lo[...] = v0_s
        for part in range(2):
            vblocks[part] = product(split(loff[part].reshape(NS2 * SUB, BS)), linv_s).reshape(NS2, SUB, BS)
        square = product_t(minv_s, minv_s)
        base[0] = square
        turned = product(split(square), v0_s)
        base[1] = -turned
        base[2] = product_t(linv_s, linv_s) + product_t(v0_s, split(turned))
        for part in range(2):
            def rows(q, carry):
                raw = moff[part, pl.ds(q * 4, 4)].reshape(BS, BS)
                u = product(split(raw), (split(minv[...])))
                u_s = split(u)
                uv = product(u_s, (v0_hi[...], v0_lo[...]))
                spread = []
                for j in range(4):
                    index, mark = leaf_of(q * 4 + j)
                    spread.append(vblocks[part, index] * mark)
                t = jnp.concatenate(spread, axis=0) - uv
                t_s = split(t)
                at = pl.ds(pl.multiple_of(q * BS, BS), BS)
                for kind, pieces in ((0, u_s), (1, t_s)):
                    w_hi[part, at, kind * BS:(kind + 1) * BS] = pieces[0]
                    w_lo[part, at, kind * BS:(kind + 1) * BS] = pieces[1]
                if part == 1:
                    for kind, value in ((0, u), (1, t)):
                        high, low = split(value.T)
                        wt_hi[kind * BS:(kind + 1) * BS, at] = high
                        wt_lo[kind * BS:(kind + 1) * BS, at] = low
                return carry
            lax.fori_loop(0, 3, rows, 0)

    factors()

    for step in range(1, 5):
        below = lax.rem(z + RING - step, RING)
        above = lax.rem(z + step, RING)
        for piece in range(4):
            if step < 4 or piece < 2:
                await_bytes(piece_of(below, piece), right_recv.at[step, piece])
                if step < 3 or (step == 3 and piece < 2):
                    pass_on(below, piece, up, right_recv.at[step + 1, piece])
                to_pair(below, piece)
            if step < 4 or piece >= 2:
                await_bytes(piece_of(above, piece), left_recv.at[step, piece])
                if step < 3 or (step == 3 and piece >= 2):
                    pass_on(above, piece, down, left_recv.at[step + 1, piece])
                to_pair(above, piece)
    await_bytes(slots(1 - core, 0, 0, 0, 2 * RING * SLOTS), pair_recv)

    narrow = lax.broadcasted_iota(jnp.int32, (HALF, 128), 1) < SUB

    def select(k, carry):
        si = struct[0, k]
        gi, ai = si >> 1, si & 1
        for p in range(NS1 // 2):
            sides = [[], []]
            for h in range(2):
                sj = struct[0, 2 * p + h]
                bj, cj = sj >> 1, sj & 1
                beyond = (gi > bj).astype(jnp.int32)
                plain = (cj == (ai ^ beyond)).astype(jnp.int32)
                own = ((gi == bj).astype(jnp.int32)) * (1 - ai) * cj
                slot = own * (SLOTS - 1) + (1 - own) * gi
                there = (1 - own) * ai
                weight = (plain + own).astype(F32) * (1.0 - 0.5 * (si == sj).astype(F32))
                stay = (there == h).astype(F32)
                for half in range(2):
                    share = gathered[(((bj & 1) * RING + (bj >> 1)) * 2 + half) * SLOTS + slot]
                    sides[half].append(
                        share * (weight * stay) + pltpu.roll(share, SUB, 1) * (weight * (1.0 - stay)))
            for half in range(2):
                row = pl.ds(pl.multiple_of(k * SUB + half * HALF, HALF), HALF)
                high, low = split(jnp.where(narrow, sides[half][0], sides[half][1]))
                a_hi[row, p * 128:(p + 1) * 128] = high
                a_lo[row, p * 128:(p + 1) * 128] = low
        return carry

    lax.fori_loop(0, NS1, select, 0)

    def send(src, dst, send_sem, recv_sem, to):
        copy = pltpu.make_async_remote_copy(
            src_ref=src, dst_ref=dst, send_sem=send_sem, recv_sem=recv_sem, device_id=to, device_id_type=MESH)
        copy.start()
        return copy

    started = []

    def first_hop(axis, chunk, recv, sends, recvs):
        plus, minus = around[axis]
        far = lax.rem(place[axis] + 2, SIDE)
        started.append(send(chunk(far, 0), recv.at[0], sends.at[0], recvs.at[0], plus))
        started.append(send(chunk(far, 1), recv.at[2], sends.at[2], recvs.at[2], minus))

    def direct_hop(axis, chunk, recv, sends, recvs):
        plus, minus = around[axis]
        nxt, prv = lax.rem(place[axis] + 1, SIDE), lax.rem(place[axis] + 3, SIDE)
        started.append(send(chunk(nxt, 1), recv.at[1], sends.at[1], recvs.at[1], plus))
        started.append(send(chunk(prv, 0), recv.at[3], sends.at[3], recvs.at[3], minus))

    def second_hop(axis, chunk, recv, comb, sends, recvs):
        me = place[axis]
        plus, minus = around[axis]
        nxt, prv = lax.rem(me + 1, SIDE), lax.rem(me + 3, SIDE)
        await_bytes(recv.at[0], recvs.at[0])
        comb[0] = recv[0] + chunk(nxt, 0)[...]
        started.append(send(comb.at[0], recv.at[4], sends.at[4], recvs.at[4], plus))
        await_bytes(recv.at[2], recvs.at[2])
        comb[1] = recv[2] + chunk(prv, 1)[...]
        started.append(send(comb.at[1], recv.at[5], sends.at[5], recvs.at[5], minus))

    def arrive(recv, recvs):
        for slot in (1, 3, 4, 5):
            await_bytes(recv.at[slot], recvs.at[slot])

    def left_rows(r, carry):
        at = pl.ds(pl.multiple_of(r * BS, BS), BS)
        ysum[0, pl.ds(r * 4, 4)] = product((a_hi[at, :], a_lo[at, :]), (w_hi[0], w_lo[0])).reshape(4, SUB, 2 * BS)
        return carry

    def gram(left, right):
        at = slice(left * BS, (left + 1) * BS)
        return product((wt_hi[at, :], wt_lo[at, :]), split(ysum[0, :, :, right * BS:(right + 1) * BS].reshape(ROWS, BS)))

    def put_gram(index, value):
        for part in range(16):
            if part * 48 // BS > index or (part * 48 + 47) // BS < index:
                continue
            low, high = max(part * 48, index * BS), min(part * 48 + 48, index * BS + BS)
            gsend[part // 8, part % 8 // 2, part % 2, low - part * 48:high - part * 48, :] = (
                value[low - index * BS:high - index * BS, :])

    def g_chunk(axis):
        return lambda t, h: gsend.at[axis, t, h]

    def y_chunk(axis):
        return lambda t, h: ysend.at[axis, t, h]

    def g_ring(axis):
        return axis, g_chunk(axis), grecv.at[axis], g_send_sem.at[axis], g_recv_sem.at[axis]

    def y_ring(axis):
        return axis, y_chunk(axis), yrecv.at[axis], y_send_sem.at[axis], y_recv_sem.at[axis]

    def pack_rows(source, axis):
        for n in range(OUTS):
            if n < NS1:
                value = ysum[source, n, :, 0:BS]
            else:
                value = ysum[source, leaf[0, n - NS1], :, BS:2 * BS]
            for t in range(SIDE):
                ysend[axis, t, n // 9, n % 9] = value[t * SLICE:(t + 1) * SLICE, :]

    def right_rows(r, carry):
        at = pl.ds(pl.multiple_of(r * BS, BS), BS)
        ysum[1, pl.ds(r * 4, 4)] = product_t((a_hi[:, at], a_lo[:, at]), (w_hi[1], w_lo[1])).reshape(4, SUB, 2 * BS)
        return carry


    def g_sum_and_exchange(axis):
        recv, recvs, sends = grecv.at[axis], g_recv_sem.at[axis], g_send_sem.at[axis]
        me = place[axis]
        arrive(recv, recvs)
        gred[axis, 0] = (gsend[axis, me, 0] + recv[3]) + recv[4]
        gred[axis, 1] = (gsend[axis, me, 1] + recv[1]) + recv[5]
        plus, minus = around[1 - axis]
        started.append(send(gred.at[axis], gexch.at[axis, 0], sends.at[6], recvs.at[6], plus))
        started.append(send(gred.at[axis], gexch.at[axis, 1], sends.at[7], recvs.at[7], minus))

    def g_exchange_on(axis):
        recvs, sends = g_recv_sem.at[axis], g_send_sem.at[axis]
        plus, minus = around[1 - axis]
        await_bytes(gexch.at[axis, 0], recvs.at[6])
        started.append(send(gexch.at[axis, 0, 0], gexch.at[axis, 2, 0], sends.at[8], recvs.at[8], plus))
        await_bytes(gexch.at[axis, 1], recvs.at[7])
        started.append(send(gexch.at[axis, 1, 1], gexch.at[axis, 2, 1], sends.at[9], recvs.at[9], minus))

    def g_spread(axis):
        recvs, sends = g_recv_sem.at[axis], g_send_sem.at[axis]
        me = place[axis]
        plus, minus = around[axis]
        await_bytes(gexch.at[axis, 2, 0], recvs.at[8])
        await_bytes(gexch.at[axis, 2, 1], recvs.at[9])
        gall[axis, me] = (gred[axis] + gexch[axis, 2]) + (gexch[axis, 0] + gexch[axis, 1])
        started.append(send(gall.at[axis, me], gall.at[axis, me], sends.at[10], recvs.at[10], plus))
        started.append(send(gall.at[axis, me], gall.at[axis, me], sends.at[11], recvs.at[11], minus))

    def g_spread_on(axis):
        recvs, sends = g_recv_sem.at[axis], g_send_sem.at[axis]
        me = place[axis]
        plus, minus = around[axis]
        prv, nxt, far = lax.rem(me + 3, SIDE), lax.rem(me + 1, SIDE), lax.rem(me + 2, SIDE)
        await_bytes(gall.at[axis, prv], recvs.at[10])
        started.append(send(gall.at[axis, prv, 0], gall.at[axis, prv, 0], sends.at[12], recvs.at[12], plus))
        await_bytes(gall.at[axis, nxt], recvs.at[11])
        started.append(send(gall.at[axis, nxt, 1], gall.at[axis, nxt, 1], sends.at[13], recvs.at[13], minus))

    def g_second(axis):
        second_hop(axis, g_chunk(axis), grecv.at[axis], gcomb.at[axis], g_send_sem.at[axis], g_recv_sem.at[axis])

    def y_second(axis):
        second_hop(axis, y_chunk(axis), yrecv.at[axis], ycomb.at[axis], y_send_sem.at[axis], y_recv_sem.at[axis])

    lax.fori_loop(0, 3, left_rows, 0)
    pack_rows(0, 1)
    first_hop(*y_ring(1))
    h00 = gram(0, 0)
    put_gram(0, h00 + h00.T)
    put_gram(1, gram(0, 1) + gram(1, 0).T)
    h11 = gram(1, 1)
    put_gram(2, h11 + h11.T)
    for axis in (0, 1):
        first_hop(*g_ring(axis))
        direct_hop(*g_ring(axis))
    direct_hop(*y_ring(1))
    lax.fori_loop(0, 3, right_rows, 0)
    pack_rows(1, 0)
    for axis in (0, 1):
        g_second(axis)
    first_hop(*y_ring(0))
    y_second(1)
    for axis in (0, 1):
        g_sum_and_exchange(axis)
    direct_hop(*y_ring(0))
    for axis in (0, 1):
        g_exchange_on(axis)
    y_second(0)
    for axis in (0, 1):
        g_spread(axis)
    for axis in (0, 1):
        g_spread_on(axis)

    for axis in (1, 0):
        arrive(yrecv.at[axis], y_recv_sem.at[axis])
    for half, direct, through in ((0, 3, 4), (1, 1, 5)):
        total = 0.0
        for axis in (0, 1):
            total = total + ((ysend[axis, place[axis], half] + yrecv[axis, direct]) + yrecv[axis, through])
        ycomb[2, half] = -total
    for n in range(NS1):
        column_out[0, n] = ycomb[2, n // 9, n % 9]
        index, mark = leaf_of(n)
        column_out[1, n] = ycomb[2, 1, index + (NS1 - 9)] * mark

    outs = [
        pltpu.make_async_copy(column_out.at[0], mid_hbm, out_sem.at[0]),
        pltpu.make_async_copy(column_out.at[1], column_hbm, out_sem.at[1]),
        pltpu.make_async_copy(gram_out, gram_hbm, out_sem.at[2]),
    ]
    outs[0].start()
    outs[1].start()
    for axis in (0, 1):
        far = lax.rem(place[axis] + 2, SIDE)
        await_bytes(gall.at[axis, far, 0], g_recv_sem.at[axis, 12])
        await_bytes(gall.at[axis, far, 1], g_recv_sem.at[axis, 13])
    gram_out[...] = gall[...].reshape(3, BS, BS) + base[...]

    outs[2].start()

    for copy in started:
        copy.wait_send()
    for half in range(2):
        await_bytes(packed.at[half, pl.ds(0, SIDE * SIDE - 1)], pack_send)

    @pl.when(grid == branch)
    def _():
        for half in range(2):
            await_bytes(extra.at[half, pl.ds(0, SIDE * SIDE - 1)], extra_send)

    await_bytes(slots(core, 0, 0, 0, 2 * (RING - 1) * SLOTS), z_send)
    await_bytes(slots(core, 0, 0, 0, 2 * RING * SLOTS), pair_send)
    for copy in outs:
        copy.wait()


def write_out(mid, leaf, gram, mid_out, diag_out, leaf_out, parent_out, leaf_diag_out, columns, blocks, in_sem, out_sem):
    parts = (
        (mid, columns.at[0], mid_out), (leaf, columns.at[1], leaf_out), (gram.at[0], blocks.at[0], diag_out),
        (gram.at[1], blocks.at[1], parent_out), (gram.at[2], blocks.at[2], leaf_diag_out))
    ins = [pltpu.make_async_copy(src, held, in_sem.at[n]) for n, (src, held, _) in enumerate(parts)]
    outs = [pltpu.make_async_copy(held, dst.at[0], out_sem.at[n]) for n, (_, held, dst) in enumerate(parts)]
    for copy in ins:
        copy.start()
    for came, goes in zip(ins, outs):
        came.wait()
        goes.start()
    for copy in outs:
        copy.wait()


def on_device(sigma_top, mid_struct, leaf_struct, mid_inv, mid_off, leaf_inv, leaf_off):
    hbm = pl.BlockSpec(memory_space=pltpu.HBM)
    dma = pltpu.SemaphoreType.DMA
    middle, leaves, grams = pl.pallas_call(
        kernel,
        out_shape=(
            jax.ShapeDtypeStruct((NS1, SLICE, BS), F32),
            jax.ShapeDtypeStruct((NS1, SLICE, BS), F32),
            jax.ShapeDtypeStruct((3, BS, BS), F32),
        ),
        in_specs=[hbm] * 7,
        out_specs=(hbm,) * 3,
        scratch_shapes=[
            pltpu.SMEM((1, NS1), jnp.int32),
            pltpu.SMEM((1, NS2), jnp.int32),
            pltpu.VMEM((2 * BS, 2 * BS), F32),
            pltpu.VMEM((2, SIDE * SIDE, HALF, 128), F32),
            pltpu.VMEM((2, SIDE * SIDE, HALF, 128), F32),
            pltpu.VMEM((4 * RING * SLOTS, HALF, 128), F32),
            pltpu.VMEM((2, NS1, SUB, BS), F32),
            pltpu.VMEM((2, NS2, SUB, BS), F32),
            pltpu.VMEM((BS, BS), F32),
            pltpu.VMEM((BS, BS), F32),
            pltpu.VMEM((BS, BS), F32),
            pltpu.VMEM((2, NS2, SUB, BS), F32),
            pltpu.VMEM((BS, BS), BF16),
            pltpu.VMEM((BS, BS), BF16),
            pltpu.VMEM((3, BS, BS), F32),
            pltpu.VMEM((2, ROWS, 2 * BS), BF16),
            pltpu.VMEM((2, ROWS, 2 * BS), BF16),
            pltpu.VMEM((2 * BS, ROWS), BF16),
            pltpu.VMEM((2 * BS, ROWS), BF16),
            pltpu.VMEM((ROWS, ROWS), BF16),
            pltpu.VMEM((ROWS, ROWS), BF16),
            pltpu.VMEM((2, NS1, SUB, 2 * BS), F32),
            pltpu.VMEM((2, SIDE, 2, 9, SLICE, BS), F32),
            pltpu.VMEM((2, 6, 9, SLICE, BS), F32),
            pltpu.VMEM((3, 2, 9, SLICE, BS), F32),
            pltpu.VMEM((2, SIDE, 2, 48, BS), F32),
            pltpu.VMEM((2, 6, 48, BS), F32),
            pltpu.VMEM((2, 2, 48, BS), F32),
            pltpu.VMEM((2, 2, 48, BS), F32),
            pltpu.VMEM((2, 3, 2, 48, BS), F32),
            pltpu.VMEM((2, SIDE, 2, 48, BS), F32),
            pltpu.VMEM((2, NS1, SLICE, BS), F32),
            pltpu.VMEM((3, BS, BS), F32),
            dma((3,)),
            dma((16,)),
            dma,
            dma((2,)),
            dma,
            dma((2,)),
            dma,
            dma((5, 4)),
            dma((5, 4)),
            dma,
            dma,
            dma((2, 6)),
            dma((2, 6)),
            dma((2, 14)),
            dma((2, 14)),
        ],
        compiler_params=pltpu.CompilerParams(
            collective_id=0, has_side_effects=True, vmem_limit_bytes=64 * 1024 * 1024),
    )(mid_struct, leaf_struct, sigma_top, mid_inv, mid_off, leaf_inv, leaf_off)
    block = jax.ShapeDtypeStruct((1, BS, BS), F32)
    column = jax.ShapeDtypeStruct((1, NS1, SLICE, BS), F32)
    return tuple(pl.pallas_call(
        write_out,
        out_shape=(column, block, column, block, block),
        in_specs=[hbm] * 3,
        out_specs=(hbm,) * 5,
        scratch_shapes=[
            pltpu.VMEM((2, NS1, SLICE, BS), F32), pltpu.VMEM((3, BS, BS), F32), dma((5,)), dma((5,))],
        compiler_params=pltpu.CompilerParams(vmem_limit_bytes=64 * 1024 * 1024),
    )(middle, leaves, grams))


def solution(mesh):
    in_specs = (
        P("grid", "branch"),
        P("branch", None),
        P("branch", None),
        P("branch", None, None),
        P("branch", None, None, None),
        P("branch", None, None),
        P("branch", None, None, None),
    )
    out_specs = (
        P("branch", None, "grid", None),
        P("branch", None, None),
        P("branch", None, "grid", None),
        P("branch", None, None),
        P("branch", None, None),
    )
    return jax.shard_map(
        on_device, mesh=mesh, in_specs=in_specs, out_specs=out_specs, check_vma=False
    )
```

```python
import jax
import jax.numpy as jnp
from jax import lax
from jax.experimental import pallas as pl
from jax.experimental.pallas import tpu as pltpu
from jax.sharding import PartitionSpec as P

MESH = pl.DeviceIdType.MESH
F32 = jnp.float32
BF16 = jnp.bfloat16
BS = 256
NS1 = 12
NS2 = 6
SIDE = 4
RING = 8
SUB = BS // SIDE
SLICE = 16
SLOTS = 17
HALF = SUB // 2
THIN = SLICE // 2
PIECES = ((0, 8), (8, 9))
ROWS = NS1 * SUB
HROWS = NS1 * HALF
OUTS = NS1 + NS2


def split(value):
    high = value.astype(BF16)
    return high, (value - high.astype(F32)).astype(BF16)


def product(left, right, dims=(((1,), (0,)), ((), ()))):
    def one(a, b):
        return lax.dot_general(a, b, dims, preferred_element_type=F32)
    return one(left[0], right[0]) + (one(left[0], right[1]) + one(left[1], right[0]))


def product_t(left, right):
    return product(left, right, (((0,), (0,)), ((), ())))


def kernel(
    struct_hbm, leaf_hbm, sigma_hbm, minv_hbm, moff_hbm, linv_hbm, loff_hbm,
    mid_hbm, column_hbm, gram_hbm,
    struct, leaf, sigma, packed, extra, gathered_a, gathered_b, moff_c, loff_c, moff_r, loff_r, first_raw, minv, linv,
    vblocks_c, vblocks_r, v0_hi, v0_lo, base, wc_hi, wc_lo, wr_hi, wr_lo, wt_hi, wt_lo, a_hi, a_lo, y1, y2, gram_sum,
    y1send, y1recv, y1comb, y2send, y2recv, y2comb, gsend, grecv, gcomb, gred, gexch, gall,
    column_out, gram_out, out_sem, load_sem, pack_send, pack_recv, extra_send, extra_recv, z_send, right_recv, left_recv,
    pair_send, pair_recv, y1_send_sem, y1_recv_sem, y2_send_sem, y2_recv_sem, g_send_sem, g_recv_sem,
):
    branch = lax.axis_index("branch")
    grid = lax.axis_index("grid")
    z, core = branch // 2, branch % 2
    y, x = grid // SIDE, grid % SIDE

    gathered = (gathered_a, gathered_b)

    def slots(half, which_core, source, slot, size=None):
        start = (which_core * RING + source) * SLOTS + slot
        return gathered[half].at[start] if size is None else gathered[half].at[pl.ds(start, size)]

    def at_grid(index):
        return {"branch": branch, "grid": index}

    def at_branch(index):
        return {"branch": index, "grid": grid}

    up = at_branch(lax.rem(z + 1, RING) * 2 + core)
    down = at_branch(lax.rem(z + RING - 1, RING) * 2 + core)
    pair = at_branch(z * 2 + (1 - core))
    around = (
        (at_grid(y * SIDE + lax.rem(x + 1, SIDE)), at_grid(y * SIDE + lax.rem(x + SIDE - 1, SIDE))),
        (at_grid(lax.rem(y + 1, SIDE) * SIDE + x), at_grid(lax.rem(y + SIDE - 1, SIDE) * SIDE + x)),
    )
    place = (x, y)

    row_c = pl.multiple_of(y * SUB, SUB)
    loads = [
        pltpu.make_async_copy(minv_hbm.at[0], minv, load_sem.at[0]),
        pltpu.make_async_copy(linv_hbm.at[0], linv, load_sem.at[1]),
        pltpu.make_async_copy(loff_hbm.at[0, 0], first_raw, load_sem.at[2]),
        pltpu.make_async_copy(moff_hbm.at[0, :, pl.ds(row_c, SUB), :], moff_c, load_sem.at[3]),
        pltpu.make_async_copy(loff_hbm.at[0, pl.ds(1, NS2), pl.ds(row_c, SUB), :], loff_c, load_sem.at[4]),
    ]
    for m in range(SIDE):
        for half in range(2):
            row_r = pl.multiple_of(m * SUB + x * SLICE + half * THIN, THIN)
            into = pl.ds(m * THIN, THIN)
            loads.append(pltpu.make_async_copy(
                moff_hbm.at[0, :, pl.ds(row_r, THIN), :], moff_r.at[half, :, into, :], load_sem.at[len(loads)]))
            loads.append(pltpu.make_async_copy(
                loff_hbm.at[0, pl.ds(1, NS2), pl.ds(row_r, THIN), :], loff_r.at[half, :, into, :],
                load_sem.at[len(loads)]))
    loads.append(pltpu.make_async_copy(struct_hbm, struct, load_sem.at[21]))
    loads.append(pltpu.make_async_copy(leaf_hbm, leaf, load_sem.at[22]))
    own = pltpu.make_async_copy(sigma_hbm, sigma, load_sem.at[23])
    own.start()

    barrier = pltpu.get_barrier_semaphore()

    def greet(step, carry):
        pl.semaphore_signal(
            barrier, inc=1, device_id=at_grid(lax.rem(grid + step, SIDE * SIDE)), device_id_type=MESH)
        return carry

    lax.fori_loop(1, SIDE * SIDE, greet, 0)
    for other in (up, down, pair):
        pl.semaphore_signal(barrier, inc=1, device_id=other, device_id_type=MESH)

    for load in loads:
        load.start()
    own.wait()

    flip = (grid > branch).astype(jnp.int32)
    lane = lax.broadcasted_iota(jnp.int32, (BS, 128), 1)
    for half in range(2):
        one = sigma[0:BS, pl.ds(pl.multiple_of(flip * BS + half * 128, 128), 128)]
        two = sigma[BS:2 * BS, pl.ds(pl.multiple_of((1 - flip) * BS + half * 128, 128), 128)]
        even = jnp.where(lane < SUB, one, pltpu.roll(two, SUB, 1))
        odd = jnp.where(lane < SUB, pltpu.roll(one, SUB, 1), two)
        for side, value in ((2 * half, even), (2 * half + 1, odd)):
            for m in range(SIDE):
                for xx in range(SIDE):
                    for part in range(2):
                        start = m * SUB + xx * SLICE + part * THIN
                        packed[part, side * SIDE + xx, m * THIN:(m + 1) * THIN, :] = value[start:start + THIN, :]

    @pl.when(grid == branch)
    def _():
        for half in range(2):
            value = sigma[0:BS, BS + half * 128:BS + (half + 1) * 128]
            for side, turned in ((2 * half, value), (2 * half + 1, pltpu.roll(value, SUB, 1))):
                for m in range(SIDE):
                    for xx in range(SIDE):
                        for part in range(2):
                            start = m * SUB + xx * SLICE + part * THIN
                            extra[part, side * SIDE + xx, m * THIN:(m + 1) * THIN, :] = turned[start:start + THIN, :]

    pl.semaphore_wait(barrier, SIDE * SIDE + 2)

    for half in range(2):
        pltpu.make_async_copy(packed.at[half, grid], slots(half, core, z, grid), pack_recv.at[half]).start()

        def hand_out(step, carry):
            to = lax.rem(grid + step, SIDE * SIDE)
            pltpu.make_async_remote_copy(
                src_ref=packed.at[half, to], dst_ref=slots(half, core, z, grid), send_sem=pack_send,
                recv_sem=pack_recv.at[half], device_id=at_grid(to), device_id_type=MESH).start()
            return carry

        lax.fori_loop(1, SIDE * SIDE, hand_out, 0)

        @pl.when(grid == branch)
        def _():
            own_slot = slots(half, core, z, SLOTS - 1)
            pltpu.make_async_copy(extra.at[half, grid], own_slot, extra_recv.at[half]).start()

            def hand_extra(step, carry):
                to = lax.rem(grid + step, SIDE * SIDE)
                pltpu.make_async_remote_copy(
                    src_ref=extra.at[half, to], dst_ref=own_slot, send_sem=extra_send,
                    recv_sem=extra_recv.at[half], device_id=at_grid(to), device_id_type=MESH).start()
                return carry

            lax.fori_loop(1, SIDE * SIDE, hand_extra, 0)

    def piece_of(half, source, piece):
        return slots(half, core, source, *PIECES[piece])

    def pass_on(half, source, piece, to, recv_sem):
        ref = piece_of(half, source, piece)
        pltpu.make_async_remote_copy(
            src_ref=ref, dst_ref=ref, send_sem=z_send, recv_sem=recv_sem, device_id=to, device_id_type=MESH).start()

    def to_pair(half, source, piece):
        ref = piece_of(half, source, piece)
        pltpu.make_async_remote_copy(
            src_ref=ref, dst_ref=ref, send_sem=pair_send, recv_sem=pair_recv.at[half], device_id=pair,
            device_id_type=MESH).start()

    def await_bytes(ref, sem):
        pltpu.make_async_copy(ref, ref, sem).wait()

    def begin(half):
        await_bytes(slots(half, core, z, 0, SIDE * SIDE), pack_recv.at[half])
        await_bytes(slots(half, core, z, SLOTS - 1), extra_recv.at[half])
        for piece in range(2):
            pass_on(half, z, piece, up, right_recv.at[half, 1, piece])
            pass_on(half, z, piece, down, left_recv.at[half, 1, piece])
            to_pair(half, z, piece)

    def gather_step(half, step):
        below = lax.rem(z + RING - step, RING)
        above = lax.rem(z + step, RING)
        for piece in range(2):
            if step < 4 or piece == 0:
                await_bytes(piece_of(half, below, piece), right_recv.at[half, step, piece])
                if step < 3 or (step == 3 and piece == 0):
                    pass_on(half, below, piece, up, right_recv.at[half, step + 1, piece])
                to_pair(half, below, piece)
            if step < 4 or piece == 1:
                await_bytes(piece_of(half, above, piece), left_recv.at[half, step, piece])
                if step < 3 or (step == 3 and piece == 1):
                    pass_on(half, above, piece, down, left_recv.at[half, step + 1, piece])
                to_pair(half, above, piece)

    def leaf_of(k):
        found, index = 0, 0
        for t in range(NS2):
            same = (leaf[0, t] == k).astype(jnp.int32)
            found = found + same
            index = index + same * t
        return jnp.minimum(index, NS2 - 1), found.astype(F32)

    def factors_c():
        for load in loads:
            load.wait()
        minv_s = split(minv[...])
        linv_s = split(linv[...])
        v0_s = split(product(split(first_raw[...]), linv_s))
        v0_hi[...], v0_lo[...] = v0_s
        vblocks_c[...] = product(split(loff_c[...].reshape(NS2 * SUB, BS)), linv_s).reshape(NS2, SUB, BS)

        def rows(q, carry):
            u = product(split(moff_c[pl.ds(q * 4, 4)].reshape(BS, BS)), split(minv[...]))
            u_s = split(u)
            uv = product(u_s, (v0_hi[...], v0_lo[...]))
            spread = []
            for j in range(4):
                index, mark = leaf_of(q * 4 + j)
                spread.append(vblocks_c[index] * mark)
            t_s = split(jnp.concatenate(spread, axis=0) - uv)
            at = pl.ds(pl.multiple_of(q * BS, BS), BS)
            for kind, pieces in ((0, u_s), (1, t_s)):
                wc_hi[at, kind * BS:(kind + 1) * BS] = pieces[0]
                wc_lo[at, kind * BS:(kind + 1) * BS] = pieces[1]
            return carry

        lax.fori_loop(0, 3, rows, 0)

    def factors_r():
        minv_s = split(minv[...])
        linv_s = split(linv[...])
        v0_s = (v0_hi[...], v0_lo[...])
        square = product_t(minv_s, minv_s)
        base[0] = square
        turned = product(split(square), v0_s)
        base[1] = -turned
        base[2] = product_t(linv_s, linv_s) + product_t(v0_s, split(turned))
        vblocks_r[...] = product(split(loff_r[...].reshape(2 * NS2 * HALF, BS)), linv_s).reshape(2 * NS2, HALF, BS)

        def rows(half, carry):
            u = product(split(moff_r[half].reshape(HROWS, BS)), split(minv[...]))
            u_s = split(u)
            uv = product(u_s, (v0_hi[...], v0_lo[...]))
            spread = []
            for k in range(NS1):
                index, mark = leaf_of(k)
                spread.append(vblocks_r[half * NS2 + index] * mark)
            t = jnp.concatenate(spread, axis=0) - uv
            t_s = split(t)
            at = pl.ds(pl.multiple_of(half * HROWS, HROWS), HROWS)
            for kind, value, pieces in ((0, u, u_s), (1, t, t_s)):
                wr_hi[at, kind * BS:(kind + 1) * BS] = pieces[0]
                wr_lo[at, kind * BS:(kind + 1) * BS] = pieces[1]
                high, low = split(value.T)
                wt_hi[half, kind * BS:(kind + 1) * BS, :] = high
                wt_lo[half, kind * BS:(kind + 1) * BS, :] = low
            return carry

        lax.fori_loop(0, 2, rows, 0)

    narrow = lax.broadcasted_iota(jnp.int32, (HALF, 128), 1) < SUB

    def select(half):
        def row_block(k, carry):
            si = struct[0, k]
            gi, ai = si >> 1, si & 1
            for p in range(NS1 // 2):
                sides = []
                for h in range(2):
                    sj = struct[0, 2 * p + h]
                    bj, cj = sj >> 1, sj & 1
                    beyond = (gi > bj).astype(jnp.int32)
                    plain = (cj == (ai ^ beyond)).astype(jnp.int32)
                    own = ((gi == bj).astype(jnp.int32)) * (1 - ai) * cj
                    slot = own * (SLOTS - 1) + (1 - own) * gi
                    there = (1 - own) * ai
                    weight = (plain + own).astype(F32) * (1.0 - 0.5 * (si == sj).astype(F32))
                    stay = (there == h).astype(F32)
                    share = gathered[half][((bj & 1) * RING + (bj >> 1)) * SLOTS + slot]
                    sides.append(share * (weight * stay) + pltpu.roll(share, SUB, 1) * (weight * (1.0 - stay)))
                row = pl.ds(pl.multiple_of(half * HROWS + k * HALF, HALF), HALF)
                high, low = split(jnp.where(narrow, sides[0], sides[1]))
                a_hi[row, p * 128:(p + 1) * 128] = high
                a_lo[row, p * 128:(p + 1) * 128] = low
            return carry

        lax.fori_loop(0, NS1, row_block, 0)

    def send(src, dst, send_sem, recv_sem, to):
        copy = pltpu.make_async_remote_copy(
            src_ref=src, dst_ref=dst, send_sem=send_sem, recv_sem=recv_sem, device_id=to, device_id_type=MESH)
        copy.start()
        return copy

    started = []

    def first_hop(axis, chunk, recv, sends, recvs):
        plus, minus = around[axis]
        far = lax.rem(place[axis] + 2, SIDE)
        started.append(send(chunk(far, 0), recv.at[0], sends.at[0], recvs.at[0], plus))
        started.append(send(chunk(far, 1), recv.at[2], sends.at[2], recvs.at[2], minus))

    def direct_hop(axis, chunk, recv, sends, recvs):
        plus, minus = around[axis]
        nxt, prv = lax.rem(place[axis] + 1, SIDE), lax.rem(place[axis] + 3, SIDE)
        started.append(send(chunk(nxt, 1), recv.at[1], sends.at[1], recvs.at[1], plus))
        started.append(send(chunk(prv, 0), recv.at[3], sends.at[3], recvs.at[3], minus))

    def second_hop(axis, chunk, recv, comb, sends, recvs):
        me = place[axis]
        plus, minus = around[axis]
        nxt, prv = lax.rem(me + 1, SIDE), lax.rem(me + 3, SIDE)
        await_bytes(recv.at[0], recvs.at[0])
        comb[0] = recv[0] + chunk(nxt, 0)[...]
        started.append(send(comb.at[0], recv.at[4], sends.at[4], recvs.at[4], plus))
        await_bytes(recv.at[2], recvs.at[2])
        comb[1] = recv[2] + chunk(prv, 1)[...]
        started.append(send(comb.at[1], recv.at[5], sends.at[5], recvs.at[5], minus))

    def arrive(recv, recvs):
        for slot in (1, 3, 4, 5):
            await_bytes(recv.at[slot], recvs.at[slot])

    def left_rows(half):
        at = slice(half * HROWS, (half + 1) * HROWS)
        for kind in range(2):
            cols = slice(kind * BS, (kind + 1) * BS)
            value = product((a_hi[at, :], a_lo[at, :]), (wc_hi[:, cols], wc_lo[:, cols]))
            y1[half, :, :, cols] = value.reshape(NS1, HALF, BS)
            term = product((wt_hi[half], wt_lo[half]), split(value))
            gram_sum[:, cols] = term if half == 0 else gram_sum[:, cols] + term

    def gram(left, right):
        return gram_sum[left * BS:(left + 1) * BS, right * BS:(right + 1) * BS]

    def put_gram(index, value):
        for part in range(16):
            if part * 48 // BS > index or (part * 48 + 47) // BS < index:
                continue
            low, high = max(part * 48, index * BS), min(part * 48 + 48, index * BS + BS)
            gsend[part // 8, part % 8 // 2, part % 2, low - part * 48:high - part * 48, :] = (
                value[low - index * BS:high - index * BS, :])

    def g_chunk(axis):
        return lambda t, h: gsend.at[axis, t, h]

    def g_ring(axis):
        return axis, g_chunk(axis), grecv.at[axis], g_send_sem.at[axis], g_recv_sem.at[axis]

    def y1_ring(half):
        return 1, lambda t, h: y1send.at[half, t, h], y1recv.at[half], y1_send_sem.at[half], y1_recv_sem.at[half]

    y2_ring = (0, lambda t, h: y2send.at[t, h], y2recv, y2_send_sem, y2_recv_sem)

    def pack_rows(blocks, put, thickness):
        for n in range(OUTS):
            value = blocks(n) if n < NS1 else blocks(None, leaf[0, n - NS1])
            for t in range(SIDE):
                put(t, n // 9, n % 9, value[t * thickness:(t + 1) * thickness, :])

    def pack_y1(half):
        def blocks(n, found=None):
            return y1[half, n, :, 0:BS] if found is None else y1[half, found, :, BS:2 * BS]

        def put(t, side, n, value):
            y1send[half, t, side, n] = value

        pack_rows(blocks, put, THIN)

    def pack_y2():
        def blocks(n, found=None):
            return y2[n, :, 0:BS] if found is None else y2[found, :, BS:2 * BS]

        def put(t, side, n, value):
            y2send[t, side, n] = value

        pack_rows(blocks, put, SLICE)

    def right_rows(r, carry):
        at = pl.ds(pl.multiple_of(r * BS, BS), BS)
        y2[pl.ds(r * 4, 4)] = product_t((a_hi[:, at], a_lo[:, at]), (wr_hi[...], wr_lo[...])).reshape(4, SUB, 2 * BS)
        return carry

    def g_sum_and_exchange(axis):
        recv, recvs, sends = grecv.at[axis], g_recv_sem.at[axis], g_send_sem.at[axis]
        me = place[axis]
        arrive(recv, recvs)
        gred[axis, 0] = (gsend[axis, me, 0] + recv[3]) + recv[4]
        gred[axis, 1] = (gsend[axis, me, 1] + recv[1]) + recv[5]
        plus, minus = around[1 - axis]
        started.append(send(gred.at[axis], gexch.at[axis, 0], sends.at[6], recvs.at[6], plus))
        started.append(send(gred.at[axis], gexch.at[axis, 1], sends.at[7], recvs.at[7], minus))

    def g_exchange_on(axis):
        recvs, sends = g_recv_sem.at[axis], g_send_sem.at[axis]
        plus, minus = around[1 - axis]
        await_bytes(gexch.at[axis, 0], recvs.at[6])
        started.append(send(gexch.at[axis, 0, 0], gexch.at[axis, 2, 0], sends.at[8], recvs.at[8], plus))
        await_bytes(gexch.at[axis, 1], recvs.at[7])
        started.append(send(gexch.at[axis, 1, 1], gexch.at[axis, 2, 1], sends.at[9], recvs.at[9], minus))

    def g_spread(axis):
        recvs, sends = g_recv_sem.at[axis], g_send_sem.at[axis]
        me = place[axis]
        plus, minus = around[axis]
        await_bytes(gexch.at[axis, 2, 0], recvs.at[8])
        await_bytes(gexch.at[axis, 2, 1], recvs.at[9])
        gall[axis, me] = (gred[axis] + gexch[axis, 2]) + (gexch[axis, 0] + gexch[axis, 1])
        started.append(send(gall.at[axis, me], gall.at[axis, me], sends.at[10], recvs.at[10], plus))
        started.append(send(gall.at[axis, me], gall.at[axis, me], sends.at[11], recvs.at[11], minus))

    def g_spread_on(axis):
        recvs, sends = g_recv_sem.at[axis], g_send_sem.at[axis]
        me = place[axis]
        plus, minus = around[axis]
        prv, nxt, far = lax.rem(me + 3, SIDE), lax.rem(me + 1, SIDE), lax.rem(me + 2, SIDE)
        await_bytes(gall.at[axis, prv], recvs.at[10])
        started.append(send(gall.at[axis, prv, 0], gall.at[axis, prv, 0], sends.at[12], recvs.at[12], plus))
        await_bytes(gall.at[axis, nxt], recvs.at[11])
        started.append(send(gall.at[axis, nxt, 1], gall.at[axis, nxt, 1], sends.at[13], recvs.at[13], minus))

    def g_second(axis):
        second_hop(axis, g_chunk(axis), grecv.at[axis], gcomb.at[axis], g_send_sem.at[axis], g_recv_sem.at[axis])

    def y1_second(half):
        axis, chunk, recv, sends, recvs = y1_ring(half)
        second_hop(axis, chunk, recv, y1comb.at[half], sends, recvs)

    def y2_second():
        axis, chunk, recv, sends, recvs = y2_ring
        second_hop(axis, chunk, recv, y2comb, sends, recvs)

    begin(0)
    factors_c()
    gather_step(0, 1)
    factors_r()
    gather_step(0, 2)
    gather_step(0, 3)
    begin(1)
    gather_step(0, 4)
    await_bytes(slots(0, 1 - core, 0, 0, RING * SLOTS), pair_recv.at[0])
    select(0)
    left_rows(0)
    gather_step(1, 1)
    pack_y1(0)
    first_hop(*y1_ring(0))
    direct_hop(*y1_ring(0))
    gather_step(1, 2)
    y1_second(0)
    gather_step(1, 3)
    gather_step(1, 4)
    await_bytes(slots(1, 1 - core, 0, 0, RING * SLOTS), pair_recv.at[1])
    select(1)
    left_rows(1)
    h00 = gram(0, 0)
    put_gram(0, h00 + h00.T)
    put_gram(1, gram(0, 1) + gram(1, 0).T)
    h11 = gram(1, 1)
    put_gram(2, h11 + h11.T)
    for axis in (0, 1):
        first_hop(*g_ring(axis))
        direct_hop(*g_ring(axis))
    pack_y1(1)
    first_hop(*y1_ring(1))
    lax.fori_loop(0, 3, right_rows, 0)
    pack_y2()
    first_hop(*y2_ring)
    for axis in (0, 1):
        g_second(axis)
    direct_hop(*y1_ring(1))
    direct_hop(*y2_ring)
    for axis in (0, 1):
        g_sum_and_exchange(axis)
    y1_second(1)
    for axis in (0, 1):
        g_exchange_on(axis)
    y2_second()
    for axis in (0, 1):
        g_spread(axis)
    for axis in (0, 1):
        g_spread_on(axis)

    for half in range(2):
        arrive(y1recv.at[half], y1_recv_sem.at[half])
    arrive(y2recv, y2_recv_sem)
    for side, direct, through in ((0, 3, 4), (1, 1, 5)):
        total = (y2send[x, side] + y2recv[direct]) + y2recv[through]
        for half in range(2):
            rows = slice(half * THIN, (half + 1) * THIN)
            part = (y1send[half, y, side] + y1recv[half, direct]) + y1recv[half, through]
            y2comb[2 + side, :, rows, :] = -(total[:, rows, :] + part)
    for n in range(NS1):
        column_out[0, n] = y2comb[2 + n // 9, n % 9]
        index, mark = leaf_of(n)
        column_out[1, n] = y2comb[3, index + (NS1 - 9)] * mark

    outs = [
        pltpu.make_async_copy(column_out.at[0], mid_hbm, out_sem.at[0]),
        pltpu.make_async_copy(column_out.at[1], column_hbm, out_sem.at[1]),
        pltpu.make_async_copy(gram_out, gram_hbm, out_sem.at[2]),
    ]
    outs[0].start()
    outs[1].start()
    for axis in (0, 1):
        far = lax.rem(place[axis] + 2, SIDE)
        await_bytes(gall.at[axis, far, 0], g_recv_sem.at[axis, 12])
        await_bytes(gall.at[axis, far, 1], g_recv_sem.at[axis, 13])
    gram_out[...] = gall[...].reshape(3, BS, BS) + base[...]

    outs[2].start()

    for copy in started:
        copy.wait_send()
    for half in range(2):
        await_bytes(packed.at[half, pl.ds(0, SIDE * SIDE - 1)], pack_send)

    @pl.when(grid == branch)
    def _():
        for half in range(2):
            await_bytes(extra.at[half, pl.ds(0, SIDE * SIDE - 1)], extra_send)

    await_bytes(slots(0, 0, 0, 0, 2 * (RING - 1) * SLOTS), z_send)
    await_bytes(slots(0, 0, 0, 0, 2 * RING * SLOTS), pair_send)
    for copy in outs:
        copy.wait()


def write_out(mid, leaf, gram, mid_out, diag_out, leaf_out, parent_out, leaf_diag_out, columns, blocks, in_sem, out_sem):
    parts = (
        (mid, columns.at[0], mid_out), (leaf, columns.at[1], leaf_out), (gram.at[0], blocks.at[0], diag_out),
        (gram.at[1], blocks.at[1], parent_out), (gram.at[2], blocks.at[2], leaf_diag_out))
    ins = [pltpu.make_async_copy(src, held, in_sem.at[n]) for n, (src, held, _) in enumerate(parts)]
    outs = [pltpu.make_async_copy(held, dst.at[0], out_sem.at[n]) for n, (_, held, dst) in enumerate(parts)]
    for copy in ins:
        copy.start()
    for came, goes in zip(ins, outs):
        came.wait()
        goes.start()
    for copy in outs:
        copy.wait()


def on_device(sigma_top, mid_struct, leaf_struct, mid_inv, mid_off, leaf_inv, leaf_off):
    hbm = pl.BlockSpec(memory_space=pltpu.HBM)
    dma = pltpu.SemaphoreType.DMA
    middle, leaves, grams = pl.pallas_call(
        kernel,
        out_shape=(
            jax.ShapeDtypeStruct((NS1, SLICE, BS), F32),
            jax.ShapeDtypeStruct((NS1, SLICE, BS), F32),
            jax.ShapeDtypeStruct((3, BS, BS), F32),
        ),
        in_specs=[hbm] * 7,
        out_specs=(hbm,) * 3,
        scratch_shapes=[
            pltpu.SMEM((1, NS1), jnp.int32),
            pltpu.SMEM((1, NS2), jnp.int32),
            pltpu.VMEM((2 * BS, 2 * BS), F32),
            pltpu.VMEM((2, SIDE * SIDE, HALF, 128), F32),
            pltpu.VMEM((2, SIDE * SIDE, HALF, 128), F32),
            pltpu.VMEM((2 * RING * SLOTS, HALF, 128), F32),
            pltpu.VMEM((2 * RING * SLOTS, HALF, 128), F32),
            pltpu.VMEM((NS1, SUB, BS), F32),
            pltpu.VMEM((NS2, SUB, BS), F32),
            pltpu.VMEM((2, NS1, HALF, BS), F32),
            pltpu.VMEM((2, NS2, HALF, BS), F32),
            pltpu.VMEM((BS, BS), F32),
            pltpu.VMEM((BS, BS), F32),
            pltpu.VMEM((BS, BS), F32),
            pltpu.VMEM((NS2, SUB, BS), F32),
            pltpu.VMEM((2 * NS2, HALF, BS), F32),
            pltpu.VMEM((BS, BS), BF16),
            pltpu.VMEM((BS, BS), BF16),
            pltpu.VMEM((3, BS, BS), F32),
            pltpu.VMEM((ROWS, 2 * BS), BF16),
            pltpu.VMEM((ROWS, 2 * BS), BF16),
            pltpu.VMEM((ROWS, 2 * BS), BF16),
            pltpu.VMEM((ROWS, 2 * BS), BF16),
            pltpu.VMEM((2, 2 * BS, HROWS), BF16),
            pltpu.VMEM((2, 2 * BS, HROWS), BF16),
            pltpu.VMEM((ROWS, ROWS), BF16),
            pltpu.VMEM((ROWS, ROWS), BF16),
            pltpu.VMEM((2, NS1, HALF, 2 * BS), F32),
            pltpu.VMEM((NS1, SUB, 2 * BS), F32),
            pltpu.VMEM((2 * BS, 2 * BS), F32),
            pltpu.VMEM((2, SIDE, 2, 9, THIN, BS), F32),
            pltpu.VMEM((2, 6, 9, THIN, BS), F32),
            pltpu.VMEM((2, 2, 9, THIN, BS), F32),
            pltpu.VMEM((SIDE, 2, 9, SLICE, BS), F32),
            pltpu.VMEM((6, 9, SLICE, BS), F32),
            pltpu.VMEM((4, 9, SLICE, BS), F32),
            pltpu.VMEM((2, SIDE, 2, 48, BS), F32),
            pltpu.VMEM((2, 6, 48, BS), F32),
            pltpu.VMEM((2, 2, 48, BS), F32),
            pltpu.VMEM((2, 2, 48, BS), F32),
            pltpu.VMEM((2, 3, 2, 48, BS), F32),
            pltpu.VMEM((2, SIDE, 2, 48, BS), F32),
            pltpu.VMEM((2, NS1, SLICE, BS), F32),
            pltpu.VMEM((3, BS, BS), F32),
            dma((3,)),
            dma((24,)),
            dma,
            dma((2,)),
            dma,
            dma((2,)),
            dma,
            dma((2, 5, 2)),
            dma((2, 5, 2)),
            dma,
            dma((2,)),
            dma((2, 6)),
            dma((2, 6)),
            dma((6,)),
            dma((6,)),
            dma((2, 14)),
            dma((2, 14)),
        ],
        compiler_params=pltpu.CompilerParams(
            collective_id=0, has_side_effects=True, vmem_limit_bytes=64 * 1024 * 1024),
    )(mid_struct, leaf_struct, sigma_top, mid_inv, mid_off, leaf_inv, leaf_off)
    block = jax.ShapeDtypeStruct((1, BS, BS), F32)
    column = jax.ShapeDtypeStruct((1, NS1, SLICE, BS), F32)
    return tuple(pl.pallas_call(
        write_out,
        out_shape=(column, block, column, block, block),
        in_specs=[hbm] * 3,
        out_specs=(hbm,) * 5,
        scratch_shapes=[
            pltpu.VMEM((2, NS1, SLICE, BS), F32), pltpu.VMEM((3, BS, BS), F32), dma((5,)), dma((5,))],
        compiler_params=pltpu.CompilerParams(vmem_limit_bytes=64 * 1024 * 1024),
    )(middle, leaves, grams))


def solution(mesh):
    in_specs = (
        P("grid", "branch"),
        P("branch", None),
        P("branch", None),
        P("branch", None, None),
        P("branch", None, None, None),
        P("branch", None, None),
        P("branch", None, None, None),
    )
    out_specs = (
        P("branch", None, "grid", None),
        P("branch", None, None),
        P("branch", None, "grid", None),
        P("branch", None, None),
        P("branch", None, None),
    )
    return jax.shard_map(
        on_device, mesh=mesh, in_specs=in_specs, out_specs=out_specs, check_vma=False
    )
```

```python
import jax
import jax.numpy as jnp
from jax import lax
from jax.experimental import pallas as pl
from jax.experimental.pallas import tpu as pltpu
from jax.sharding import PartitionSpec as P

MESH = pl.DeviceIdType.MESH
F32 = jnp.float32
BF16 = jnp.bfloat16
BS = 256
NS1 = 12
NS2 = 6
SIDE = 4
RING = 8
SUB = BS // SIDE
SLICE = 16
SLOTS = 17
HALF = SUB // 2
TILES = 2 * SLOTS - 1
PIECES = ((0, 0, 8), (0, 8, 9), (1, 0, 8), (1, 8, 8))
ROWS = NS1 * SUB
OUTS = NS1 + NS2


def split(value):
    high = value.astype(BF16)
    return high, (value - high.astype(F32)).astype(BF16)


def product(left, right, dims=(((1,), (0,)), ((), ()))):
    def one(a, b):
        return lax.dot_general(a, b, dims, preferred_element_type=F32)
    return one(left[0], right[0]) + (one(left[0], right[1]) + one(left[1], right[0]))


def product_t(left, right):
    return product(left, right, (((0,), (0,)), ((), ())))


def kernel(
    struct_hbm, leaf_hbm, sigma_hbm, minv_hbm, moff_hbm, linv_hbm, loff_hbm,
    mid_hbm, column_hbm, gram_hbm,
    struct, leaf, sigma, packed, extra, gathered, moff, loff, first_raw, minv, linv, vblocks, v0_hi, v0_lo, base,
    w_hi, w_lo, wt_hi, wt_lo, a_hi, a_lo, ysum, ysend, yrecv, ycomb, gsend, grecv, gcomb, gred, gexch, gall,
    column_out, gram_out, out_sem,
    load_sem, pack_send, pack_recv, extra_send, extra_recv, z_send, right_recv, left_recv,
    pair_send, pair_recv, y_send_sem, y_recv_sem, g_send_sem, g_recv_sem,
):
    branch = lax.axis_index("branch")
    grid = lax.axis_index("grid")
    z, core = branch // 2, branch % 2
    y, x = grid // SIDE, grid % SIDE

    def slots(which_core, source, half, slot, size=None):
        start = (which_core * RING + source) * TILES + half * SLOTS + slot
        return gathered.at[start] if size is None else gathered.at[pl.ds(start, size)]

    def at_grid(index):
        return {"branch": branch, "grid": index}

    def at_branch(index):
        return {"branch": index, "grid": grid}

    up = at_branch(lax.rem(z + 1, RING) * 2 + core)
    down = at_branch(lax.rem(z + RING - 1, RING) * 2 + core)
    pair = at_branch(z * 2 + (1 - core))
    around = (
        (at_grid(y * SIDE + lax.rem(x + 1, SIDE)), at_grid(y * SIDE + lax.rem(x + SIDE - 1, SIDE))),
        (at_grid(lax.rem(y + 1, SIDE) * SIDE + x), at_grid(lax.rem(y + SIDE - 1, SIDE) * SIDE + x)),
    )
    place = (x, y)

    row_c = pl.multiple_of(y * SUB, SUB)
    loads = [
        pltpu.make_async_copy(minv_hbm.at[0], minv, load_sem.at[0]),
        pltpu.make_async_copy(linv_hbm.at[0], linv, load_sem.at[1]),
        pltpu.make_async_copy(loff_hbm.at[0, 0], first_raw, load_sem.at[2]),
        pltpu.make_async_copy(moff_hbm.at[0, :, pl.ds(row_c, SUB), :], moff.at[0], load_sem.at[3]),
        pltpu.make_async_copy(loff_hbm.at[0, pl.ds(1, NS2), pl.ds(row_c, SUB), :], loff.at[0], load_sem.at[4]),
    ]
    for m in range(SIDE):
        row_r = pl.multiple_of(m * SUB + x * SLICE, SLICE)
        into = pl.ds(m * SLICE, SLICE)
        loads.append(pltpu.make_async_copy(
            moff_hbm.at[0, :, pl.ds(row_r, SLICE), :], moff.at[1, :, into, :], load_sem.at[5 + m]))
        loads.append(pltpu.make_async_copy(
            loff_hbm.at[0, pl.ds(1, NS2), pl.ds(row_r, SLICE), :], loff.at[1, :, into, :], load_sem.at[9 + m]))
    loads.append(pltpu.make_async_copy(struct_hbm, struct, load_sem.at[13]))
    loads.append(pltpu.make_async_copy(leaf_hbm, leaf, load_sem.at[14]))
    own = pltpu.make_async_copy(sigma_hbm, sigma, load_sem.at[15])
    own.start()

    barrier = pltpu.get_barrier_semaphore()

    def greet(step, carry):
        pl.semaphore_signal(
            barrier, inc=1, device_id=at_grid(lax.rem(grid + step, SIDE * SIDE)), device_id_type=MESH)
        return carry

    lax.fori_loop(1, SIDE * SIDE, greet, 0)
    for other in (up, down, pair):
        pl.semaphore_signal(barrier, inc=1, device_id=other, device_id_type=MESH)

    for load in loads:
        load.start()
    own.wait()

    flip = (grid > branch).astype(jnp.int32)
    lane = lax.broadcasted_iota(jnp.int32, (BS, 128), 1)
    for half in range(2):
        one = sigma[0:BS, pl.ds(pl.multiple_of(flip * BS + half * 128, 128), 128)]
        two = sigma[BS:2 * BS, pl.ds(pl.multiple_of((1 - flip) * BS + half * 128, 128), 128)]
        even = jnp.where(lane < SUB, one, pltpu.roll(two, SUB, 1))
        odd = jnp.where(lane < SUB, pltpu.roll(one, SUB, 1), two)
        for side, value in ((2 * half, even), (2 * half + 1, odd)):
            for m in range(SIDE):
                for xx in range(SIDE):
                    start = m * SUB + xx * SLICE
                    packed[m // 2, side * SIDE + xx, m % 2 * SLICE:(m % 2 + 1) * SLICE, :] = value[start:start + SLICE, :]

    @pl.when(grid == branch)
    def _():
        for half in range(2):
            value = sigma[0:BS, BS + half * 128:BS + (half + 1) * 128]
            turned = pltpu.roll(value, SUB, 1)
            for side, upper, lower in ((2 * half, value, turned), (2 * half + 1, turned, value)):
                for m in range(2):
                    for xx in range(SIDE):
                        start = m * SUB + xx * SLICE
                        extra[side * SIDE + xx, m * SLICE:(m + 1) * SLICE, :] = jnp.where(
                            lane[0:SLICE] < SUB, upper[start:start + SLICE, :],
                            lower[2 * SUB + start:2 * SUB + start + SLICE, :])

    pl.semaphore_wait(barrier, SIDE * SIDE + 2)

    def exchange(half):
        pltpu.make_async_copy(packed.at[half, grid], slots(core, z, half, grid), pack_recv.at[half]).start()

        def hand_out(step, carry):
            to = lax.rem(grid + step, SIDE * SIDE)
            pltpu.make_async_remote_copy(
                src_ref=packed.at[half, to], dst_ref=slots(core, z, half, grid), send_sem=pack_send,
                recv_sem=pack_recv.at[half], device_id=at_grid(to), device_id_type=MESH).start()
            return carry

        lax.fori_loop(1, SIDE * SIDE, hand_out, 0)

        if half == 0:
            @pl.when(grid == branch)
            def _():
                own_slot = slots(core, z, 0, SLOTS - 1)
                pltpu.make_async_copy(extra.at[grid], own_slot, extra_recv).start()

                def hand_extra(step, carry):
                    to = lax.rem(grid + step, SIDE * SIDE)
                    pltpu.make_async_remote_copy(
                        src_ref=extra.at[to], dst_ref=own_slot, send_sem=extra_send,
                        recv_sem=extra_recv, device_id=at_grid(to), device_id_type=MESH).start()
                    return carry

                lax.fori_loop(1, SIDE * SIDE, hand_extra, 0)

    def piece_of(source, piece):
        half, start, size = PIECES[piece]
        return slots(core, source, half, start, size)

    def pass_on(source, piece, to, recv_sem):
        ref = piece_of(source, piece)
        pltpu.make_async_remote_copy(
            src_ref=ref, dst_ref=ref, send_sem=z_send, recv_sem=recv_sem, device_id=to, device_id_type=MESH).start()

    def to_pair(source, piece):
        ref = piece_of(source, piece)
        pltpu.make_async_remote_copy(
            src_ref=ref, dst_ref=ref, send_sem=pair_send, recv_sem=pair_recv, device_id=pair,
            device_id_type=MESH).start()

    def await_bytes(ref, sem):
        pltpu.make_async_copy(ref, ref, sem).wait()

    exchange(0)
    for piece in range(4):
        half = PIECES[piece][0]
        if piece % 2 == 0:
            await_bytes(slots(core, z, half, 0, SIDE * SIDE), pack_recv.at[half])
        if piece == 0:
            await_bytes(slots(core, z, 0, SLOTS - 1), extra_recv)
        pass_on(z, piece, up, right_recv.at[1, piece])
        pass_on(z, piece, down, left_recv.at[1, piece])
        to_pair(z, piece)
        if piece == 1:
            exchange(1)

    def leaf_of(k):
        found, index = 0, 0
        for t in range(NS2):
            same = (leaf[0, t] == k).astype(jnp.int32)
            found = found + same
            index = index + same * t
        return jnp.minimum(index, NS2 - 1), found.astype(F32)

    def factors():
        for load in loads:
            load.wait()
        minv_s = split(minv[...])
        linv_s = split(linv[...])
        v0_s = split(product(split(first_raw[...]), linv_s))
        v0_hi[...], v0_lo[...] = v0_s
        for part in range(2):
            vblocks[part] = product(split(loff[part].reshape(NS2 * SUB, BS)), linv_s).reshape(NS2, SUB, BS)
        square = product_t(minv_s, minv_s)
        base[0] = square
        turned = product(split(square), v0_s)
        base[1] = -turned
        base[2] = product_t(linv_s, linv_s) + product_t(v0_s, split(turned))
        for part in range(2):
            def rows(q, carry):
                raw = moff[part, pl.ds(q * 4, 4)].reshape(BS, BS)
                u = product(split(raw), (split(minv[...])))
                u_s = split(u)
                uv = product(u_s, (v0_hi[...], v0_lo[...]))
                spread = []
                for j in range(4):
                    index, mark = leaf_of(q * 4 + j)
                    spread.append(vblocks[part, index] * mark)
                t = jnp.concatenate(spread, axis=0) - uv
                t_s = split(t)
                at = pl.ds(pl.multiple_of(q * BS, BS), BS)
                for kind, pieces in ((0, u_s), (1, t_s)):
                    w_hi[part, at, kind * BS:(kind + 1) * BS] = pieces[0]
                    w_lo[part, at, kind * BS:(kind + 1) * BS] = pieces[1]
                if part == 1:
                    for kind, value in ((0, u), (1, t)):
                        high, low = split(value.T)
                        wt_hi[kind * BS:(kind + 1) * BS, at] = high
                        wt_lo[kind * BS:(kind + 1) * BS, at] = low
                return carry
            lax.fori_loop(0, 3, rows, 0)

    factors()

    for step in range(1, 5):
        below = lax.rem(z + RING - step, RING)
        above = lax.rem(z + step, RING)
        for piece in range(4):
            if step < 4 or piece < 2:
                await_bytes(piece_of(below, piece), right_recv.at[step, piece])
                if step < 3 or (step == 3 and piece < 2):
                    pass_on(below, piece, up, right_recv.at[step + 1, piece])
                to_pair(below, piece)
            if step < 4 or piece >= 2:
                await_bytes(piece_of(above, piece), left_recv.at[step, piece])
                if step < 3 or (step == 3 and piece >= 2):
                    pass_on(above, piece, down, left_recv.at[step + 1, piece])
                to_pair(above, piece)
    await_bytes(slots(1 - core, 0, 0, 0, RING * TILES), pair_recv)

    narrow = lax.broadcasted_iota(jnp.int32, (HALF, 128), 1) < SUB

    def select(k, carry):
        si = struct[0, k]
        gi, ai = si >> 1, si & 1
        for p in range(NS1 // 2):
            sides = [[], []]
            for h in range(2):
                sj = struct[0, 2 * p + h]
                bj, cj = sj >> 1, sj & 1
                beyond = (gi > bj).astype(jnp.int32)
                plain = (cj == (ai ^ beyond)).astype(jnp.int32)
                own = ((gi == bj).astype(jnp.int32)) * (1 - ai) * cj
                weight = (plain + own).astype(F32) * (1.0 - 0.5 * (si == sj).astype(F32))
                for half in range(2):
                    slot = own * (SLOTS - 1) + (1 - own) * (half * SLOTS + gi)
                    there = own * half + (1 - own) * ai
                    stay = (there == h).astype(F32)
                    share = gathered[((bj & 1) * RING + (bj >> 1)) * TILES + slot]
                    sides[half].append(
                        share * (weight * stay) + pltpu.roll(share, SUB, 1) * (weight * (1.0 - stay)))
            for half in range(2):
                row = pl.ds(pl.multiple_of(k * SUB + half * HALF, HALF), HALF)
                high, low = split(jnp.where(narrow, sides[half][0], sides[half][1]))
                a_hi[row, p * 128:(p + 1) * 128] = high
                a_lo[row, p * 128:(p + 1) * 128] = low
        return carry

    lax.fori_loop(0, NS1, select, 0)

    def send(src, dst, send_sem, recv_sem, to):
        copy = pltpu.make_async_remote_copy(
            src_ref=src, dst_ref=dst, send_sem=send_sem, recv_sem=recv_sem, device_id=to, device_id_type=MESH)
        copy.start()
        return copy

    started = []

    def first_hop(axis, chunk, recv, sends, recvs):
        plus, minus = around[axis]
        far = lax.rem(place[axis] + 2, SIDE)
        started.append(send(chunk(far, 0), recv.at[0], sends.at[0], recvs.at[0], plus))
        started.append(send(chunk(far, 1), recv.at[2], sends.at[2], recvs.at[2], minus))

    def direct_hop(axis, chunk, recv, sends, recvs):
        plus, minus = around[axis]
        nxt, prv = lax.rem(place[axis] + 1, SIDE), lax.rem(place[axis] + 3, SIDE)
        started.append(send(chunk(nxt, 1), recv.at[1], sends.at[1], recvs.at[1], plus))
        started.append(send(chunk(prv, 0), recv.at[3], sends.at[3], recvs.at[3], minus))

    def second_hop(axis, chunk, recv, comb, sends, recvs):
        me = place[axis]
        plus, minus = around[axis]
        nxt, prv = lax.rem(me + 1, SIDE), lax.rem(me + 3, SIDE)
        await_bytes(recv.at[0], recvs.at[0])
        comb[0] = recv[0] + chunk(nxt, 0)[...]
        started.append(send(comb.at[0], recv.at[4], sends.at[4], recvs.at[4], plus))
        await_bytes(recv.at[2], recvs.at[2])
        comb[1] = recv[2] + chunk(prv, 1)[...]
        started.append(send(comb.at[1], recv.at[5], sends.at[5], recvs.at[5], minus))

    def arrive(recv, recvs):
        for slot in (1, 3, 4, 5):
            await_bytes(recv.at[slot], recvs.at[slot])

    def left_rows(r, carry):
        at = pl.ds(pl.multiple_of(r * BS, BS), BS)
        ysum[0, pl.ds(r * 4, 4)] = product((a_hi[at, :], a_lo[at, :]), (w_hi[0], w_lo[0])).reshape(4, SUB, 2 * BS)
        return carry

    def gram(left, right):
        at = slice(left * BS, (left + 1) * BS)
        return product((wt_hi[at, :], wt_lo[at, :]), split(ysum[0, :, :, right * BS:(right + 1) * BS].reshape(ROWS, BS)))

    def put_gram(first, value):
        for part in range(16):
            low, high = max(part * 40, first), min(part * 40 + 40, first + value.shape[0])
            if low < high:
                gsend[part // 8, part % 8 // 2, part % 2, low - part * 40:high - part * 40, :] = (
                    value[low - first:high - first, :])

    def g_chunk(axis):
        return lambda t, h: gsend.at[axis, t, h]

    def y_chunk(axis):
        return lambda t, h: ysend.at[axis, t, h]

    def g_ring(axis):
        return axis, g_chunk(axis), grecv.at[axis], g_send_sem.at[axis], g_recv_sem.at[axis]

    def y_ring(axis):
        return axis, y_chunk(axis), yrecv.at[axis], y_send_sem.at[axis], y_recv_sem.at[axis]

    def pack_rows(source, axis):
        for n in range(OUTS):
            if n < NS1:
                value = ysum[source, n, :, 0:BS]
            else:
                value = ysum[source, leaf[0, n - NS1], :, BS:2 * BS]
            for t in range(SIDE):
                ysend[axis, t, n // 9, n % 9] = value[t * SLICE:(t + 1) * SLICE, :]

    def right_rows(r, carry):
        at = pl.ds(pl.multiple_of(r * BS, BS), BS)
        ysum[1, pl.ds(r * 4, 4)] = product_t((a_hi[:, at], a_lo[:, at]), (w_hi[1], w_lo[1])).reshape(4, SUB, 2 * BS)
        return carry


    def g_sum_and_exchange(axis):
        recv, recvs, sends = grecv.at[axis], g_recv_sem.at[axis], g_send_sem.at[axis]
        me = place[axis]
        arrive(recv, recvs)
        gred[axis, 0] = (gsend[axis, me, 0] + recv[3]) + recv[4]
        gred[axis, 1] = (gsend[axis, me, 1] + recv[1]) + recv[5]
        plus, minus = around[1 - axis]
        started.append(send(gred.at[axis], gexch.at[axis, 0], sends.at[6], recvs.at[6], plus))
        started.append(send(gred.at[axis], gexch.at[axis, 1], sends.at[7], recvs.at[7], minus))

    def g_exchange_on(axis):
        recvs, sends = g_recv_sem.at[axis], g_send_sem.at[axis]
        plus, minus = around[1 - axis]
        await_bytes(gexch.at[axis, 0], recvs.at[6])
        started.append(send(gexch.at[axis, 0, 0], gexch.at[axis, 2, 0], sends.at[8], recvs.at[8], plus))
        await_bytes(gexch.at[axis, 1], recvs.at[7])
        started.append(send(gexch.at[axis, 1, 1], gexch.at[axis, 2, 1], sends.at[9], recvs.at[9], minus))

    def g_spread(axis):
        recvs, sends = g_recv_sem.at[axis], g_send_sem.at[axis]
        me = place[axis]
        plus, minus = around[axis]
        await_bytes(gexch.at[axis, 2, 0], recvs.at[8])
        await_bytes(gexch.at[axis, 2, 1], recvs.at[9])
        gall[axis, me] = (gred[axis] + gexch[axis, 2]) + (gexch[axis, 0] + gexch[axis, 1])
        started.append(send(gall.at[axis, me], gall.at[axis, me], sends.at[10], recvs.at[10], plus))
        started.append(send(gall.at[axis, me], gall.at[axis, me], sends.at[11], recvs.at[11], minus))

    def g_spread_on(axis):
        recvs, sends = g_recv_sem.at[axis], g_send_sem.at[axis]
        me = place[axis]
        plus, minus = around[axis]
        prv, nxt, far = lax.rem(me + 3, SIDE), lax.rem(me + 1, SIDE), lax.rem(me + 2, SIDE)
        await_bytes(gall.at[axis, prv], recvs.at[10])
        started.append(send(gall.at[axis, prv, 0], gall.at[axis, prv, 0], sends.at[12], recvs.at[12], plus))
        await_bytes(gall.at[axis, nxt], recvs.at[11])
        started.append(send(gall.at[axis, nxt, 1], gall.at[axis, nxt, 1], sends.at[13], recvs.at[13], minus))

    def g_second(axis):
        second_hop(axis, g_chunk(axis), grecv.at[axis], gcomb.at[axis], g_send_sem.at[axis], g_recv_sem.at[axis])

    def y_second(axis):
        second_hop(axis, y_chunk(axis), yrecv.at[axis], ycomb.at[axis], y_send_sem.at[axis], y_recv_sem.at[axis])

    lax.fori_loop(0, 3, left_rows, 0)
    pack_rows(0, 1)
    first_hop(*y_ring(1))
    h00 = gram(0, 0)
    h00 = h00 + h00.T
    put_gram(0, h00[0:128])
    put_gram(384, gram(0, 1) + gram(1, 0).T)
    h11 = gram(1, 1)
    h11 = h11 + h11.T
    put_gram(128, h11[0:128])
    put_gram(256, jnp.concatenate([h00[128:, 128:], h11[128:, 128:]], axis=1))
    for axis in (0, 1):
        first_hop(*g_ring(axis))
        direct_hop(*g_ring(axis))
    direct_hop(*y_ring(1))
    lax.fori_loop(0, 3, right_rows, 0)
    pack_rows(1, 0)
    for axis in (0, 1):
        g_second(axis)
    first_hop(*y_ring(0))
    y_second(1)
    for axis in (0, 1):
        g_sum_and_exchange(axis)
    direct_hop(*y_ring(0))
    for axis in (0, 1):
        g_exchange_on(axis)
    y_second(0)
    for axis in (0, 1):
        g_spread(axis)
    for axis in (0, 1):
        g_spread_on(axis)

    for axis in (1, 0):
        arrive(yrecv.at[axis], y_recv_sem.at[axis])
    for half, direct, through in ((0, 3, 4), (1, 1, 5)):
        total = 0.0
        for axis in (0, 1):
            total = total + ((ysend[axis, place[axis], half] + yrecv[axis, direct]) + yrecv[axis, through])
        ycomb[2, half] = -total
    for n in range(NS1):
        column_out[0, n] = ycomb[2, n // 9, n % 9]
        index, mark = leaf_of(n)
        column_out[1, n] = ycomb[2, 1, index + (NS1 - 9)] * mark

    outs = [
        pltpu.make_async_copy(column_out.at[0], mid_hbm, out_sem.at[0]),
        pltpu.make_async_copy(column_out.at[1], column_hbm, out_sem.at[1]),
        pltpu.make_async_copy(gram_out, gram_hbm, out_sem.at[2]),
    ]
    outs[0].start()
    outs[1].start()
    for axis in (0, 1):
        far = lax.rem(place[axis] + 2, SIDE)
        await_bytes(gall.at[axis, far, 0], g_recv_sem.at[axis, 12])
        await_bytes(gall.at[axis, far, 1], g_recv_sem.at[axis, 13])
    total = gall[...].reshape(640, BS)
    gram_out[1] = total[384:640] + base[1]
    for index, first in ((0, 0), (2, 128)):
        upper = total[first:first + 128]
        gram_out[index, 0:128, :] = upper + base[index, 0:128, :]
        gram_out[index, 128:256, 0:128] = upper[:, 128:].T + base[index, 128:256, 0:128]
        gram_out[index, 128:256, 128:256] = total[256:384, first:first + 128] + base[index, 128:256, 128:256]

    outs[2].start()

    for copy in started:
        copy.wait_send()
    for half in range(2):
        await_bytes(packed.at[half, pl.ds(0, SIDE * SIDE - 1)], pack_send)

    @pl.when(grid == branch)
    def _():
        await_bytes(extra.at[pl.ds(0, SIDE * SIDE - 1)], extra_send)

    await_bytes(slots(core, 0, 0, 0, (RING - 1) * TILES), z_send)
    await_bytes(slots(core, 0, 0, 0, RING * TILES), pair_send)
    for copy in outs:
        copy.wait()


def write_out(mid, leaf, gram, mid_out, diag_out, leaf_out, parent_out, leaf_diag_out, columns, blocks, in_sem, out_sem):
    parts = (
        (mid, columns.at[0], mid_out), (leaf, columns.at[1], leaf_out), (gram.at[0], blocks.at[0], diag_out),
        (gram.at[1], blocks.at[1], parent_out), (gram.at[2], blocks.at[2], leaf_diag_out))
    ins = [pltpu.make_async_copy(src, held, in_sem.at[n]) for n, (src, held, _) in enumerate(parts)]
    outs = [pltpu.make_async_copy(held, dst.at[0], out_sem.at[n]) for n, (_, held, dst) in enumerate(parts)]
    for copy in ins:
        copy.start()
    for came, goes in zip(ins, outs):
        came.wait()
        goes.start()
    for copy in outs:
        copy.wait()


def on_device(sigma_top, mid_struct, leaf_struct, mid_inv, mid_off, leaf_inv, leaf_off):
    hbm = pl.BlockSpec(memory_space=pltpu.HBM)
    dma = pltpu.SemaphoreType.DMA
    middle, leaves, grams = pl.pallas_call(
        kernel,
        out_shape=(
            jax.ShapeDtypeStruct((NS1, SLICE, BS), F32),
            jax.ShapeDtypeStruct((NS1, SLICE, BS), F32),
            jax.ShapeDtypeStruct((3, BS, BS), F32),
        ),
        in_specs=[hbm] * 7,
        out_specs=(hbm,) * 3,
        scratch_shapes=[
            pltpu.SMEM((1, NS1), jnp.int32),
            pltpu.SMEM((1, NS2), jnp.int32),
            pltpu.VMEM((2 * BS, 2 * BS), F32),
            pltpu.VMEM((2, SIDE * SIDE, HALF, 128), F32),
            pltpu.VMEM((SIDE * SIDE, HALF, 128), F32),
            pltpu.VMEM((2 * RING * TILES, HALF, 128), F32),
            pltpu.VMEM((2, NS1, SUB, BS), F32),
            pltpu.VMEM((2, NS2, SUB, BS), F32),
            pltpu.VMEM((BS, BS), F32),
            pltpu.VMEM((BS, BS), F32),
            pltpu.VMEM((BS, BS), F32),
            pltpu.VMEM((2, NS2, SUB, BS), F32),
            pltpu.VMEM((BS, BS), BF16),
            pltpu.VMEM((BS, BS), BF16),
            pltpu.VMEM((3, BS, BS), F32),
            pltpu.VMEM((2, ROWS, 2 * BS), BF16),
            pltpu.VMEM((2, ROWS, 2 * BS), BF16),
            pltpu.VMEM((2 * BS, ROWS), BF16),
            pltpu.VMEM((2 * BS, ROWS), BF16),
            pltpu.VMEM((ROWS, ROWS), BF16),
            pltpu.VMEM((ROWS, ROWS), BF16),
            pltpu.VMEM((2, NS1, SUB, 2 * BS), F32),
            pltpu.VMEM((2, SIDE, 2, 9, SLICE, BS), F32),
            pltpu.VMEM((2, 6, 9, SLICE, BS), F32),
            pltpu.VMEM((3, 2, 9, SLICE, BS), F32),
            pltpu.VMEM((2, SIDE, 2, 40, BS), F32),
            pltpu.VMEM((2, 6, 40, BS), F32),
            pltpu.VMEM((2, 2, 40, BS), F32),
            pltpu.VMEM((2, 2, 40, BS), F32),
            pltpu.VMEM((2, 3, 2, 40, BS), F32),
            pltpu.VMEM((2, SIDE, 2, 40, BS), F32),
            pltpu.VMEM((2, NS1, SLICE, BS), F32),
            pltpu.VMEM((3, BS, BS), F32),
            dma((3,)),
            dma((16,)),
            dma,
            dma((2,)),
            dma,
            dma,
            dma,
            dma((5, 4)),
            dma((5, 4)),
            dma,
            dma,
            dma((2, 6)),
            dma((2, 6)),
            dma((2, 14)),
            dma((2, 14)),
        ],
        compiler_params=pltpu.CompilerParams(
            collective_id=0, has_side_effects=True, vmem_limit_bytes=64 * 1024 * 1024),
    )(mid_struct, leaf_struct, sigma_top, mid_inv, mid_off, leaf_inv, leaf_off)
    block = jax.ShapeDtypeStruct((1, BS, BS), F32)
    column = jax.ShapeDtypeStruct((1, NS1, SLICE, BS), F32)
    return tuple(pl.pallas_call(
        write_out,
        out_shape=(column, block, column, block, block),
        in_specs=[hbm] * 3,
        out_specs=(hbm,) * 5,
        scratch_shapes=[
            pltpu.VMEM((2, NS1, SLICE, BS), F32), pltpu.VMEM((3, BS, BS), F32), dma((5,)), dma((5,))],
        compiler_params=pltpu.CompilerParams(vmem_limit_bytes=64 * 1024 * 1024),
    )(middle, leaves, grams))


def solution(mesh):
    in_specs = (
        P("grid", "branch"),
        P("branch", None),
        P("branch", None),
        P("branch", None, None),
        P("branch", None, None, None),
        P("branch", None, None),
        P("branch", None, None, None),
    )
    out_specs = (
        P("branch", None, "grid", None),
        P("branch", None, None),
        P("branch", None, "grid", None),
        P("branch", None, None),
        P("branch", None, None),
    )
    return jax.shard_map(
        on_device, mesh=mesh, in_specs=in_specs, out_specs=out_specs, check_vma=False
    )
```

```python
import jax
import jax.numpy as jnp
from jax import lax
from jax.experimental import pallas as pl
from jax.experimental.pallas import tpu as pltpu
from jax.sharding import PartitionSpec as P

MESH = pl.DeviceIdType.MESH
F32 = jnp.float32
BF16 = jnp.bfloat16
BS = 256
NS1 = 12
NS2 = 6
SIDE = 4
RING = 8
SUB = BS // SIDE
SLICE = 16
SLOTS = 17
HALF = SUB // 2
TILES = 2 * SLOTS - 1
PIECES = ((0, 0, 8), (0, 8, 9), (1, 0, 8), (1, 8, 8))
ROWS = NS1 * SUB
OUTS = NS1 + NS2


def split(value):
    high = value.astype(BF16)
    return high, (value - high.astype(F32)).astype(BF16)


def product(left, right, dims=(((1,), (0,)), ((), ()))):
    def one(a, b):
        return lax.dot_general(a, b, dims, preferred_element_type=F32)
    return one(left[0], right[0]) + (one(left[0], right[1]) + one(left[1], right[0]))


def product_t(left, right):
    return product(left, right, (((0,), (0,)), ((), ())))


def kernel(
    struct_hbm, leaf_hbm, sigma_hbm, minv_hbm, moff_hbm, linv_hbm, loff_hbm,
    mid_hbm, column_hbm, gram_hbm,
    struct, leaf, sigma, packed, extra, gathered, moff, loff, first_raw, minv, linv, vblocks, v0_hi, v0_lo, base,
    w_hi, w_lo, wt_hi, wt_lo, a_hi, a_lo, ysum, ysend, yrecv, ycomb, gsend, grecv, gcomb, gred, gexch, gall,
    column_out, gram_out, out_sem,
    load_sem, pack_send, pack_recv, extra_send, extra_recv, z_send, right_recv, left_recv,
    pair_send, pair_recv, y_send_sem, y_recv_sem, g_send_sem, g_recv_sem,
):
    branch = lax.axis_index("branch")
    grid = lax.axis_index("grid")
    z, core = branch // 2, branch % 2
    y, x = grid // SIDE, grid % SIDE

    def slots(which_core, source, half, slot, size=None):
        start = (which_core * RING + source) * TILES + half * SLOTS + slot
        return gathered.at[start] if size is None else gathered.at[pl.ds(start, size)]

    def at_grid(index):
        return {"branch": branch, "grid": index}

    def at_branch(index):
        return {"branch": index, "grid": grid}

    up = at_branch(lax.rem(z + 1, RING) * 2 + core)
    down = at_branch(lax.rem(z + RING - 1, RING) * 2 + core)
    pair = at_branch(z * 2 + (1 - core))
    around = (
        (at_grid(y * SIDE + lax.rem(x + 1, SIDE)), at_grid(y * SIDE + lax.rem(x + SIDE - 1, SIDE))),
        (at_grid(lax.rem(y + 1, SIDE) * SIDE + x), at_grid(lax.rem(y + SIDE - 1, SIDE) * SIDE + x)),
    )
    place = (x, y)

    row_c = pl.multiple_of(y * SUB, SUB)
    loads = [
        pltpu.make_async_copy(minv_hbm.at[0], minv, load_sem.at[0]),
        pltpu.make_async_copy(linv_hbm.at[0], linv, load_sem.at[1]),
        pltpu.make_async_copy(loff_hbm.at[0, 0], first_raw, load_sem.at[2]),
        pltpu.make_async_copy(moff_hbm.at[0, :, pl.ds(row_c, SUB), :], moff.at[0], load_sem.at[3]),
        pltpu.make_async_copy(loff_hbm.at[0, pl.ds(1, NS2), pl.ds(row_c, SUB), :], loff.at[0], load_sem.at[4]),
    ]
    for m in range(SIDE):
        row_r = pl.multiple_of(m * SUB + x * SLICE, SLICE)
        into = pl.ds(m * SLICE, SLICE)
        loads.append(pltpu.make_async_copy(
            moff_hbm.at[0, :, pl.ds(row_r, SLICE), :], moff.at[1, :, into, :], load_sem.at[5 + m]))
        loads.append(pltpu.make_async_copy(
            loff_hbm.at[0, pl.ds(1, NS2), pl.ds(row_r, SLICE), :], loff.at[1, :, into, :], load_sem.at[9 + m]))
    loads.append(pltpu.make_async_copy(struct_hbm, struct, load_sem.at[13]))
    loads.append(pltpu.make_async_copy(leaf_hbm, leaf, load_sem.at[14]))
    own = pltpu.make_async_copy(sigma_hbm, sigma, load_sem.at[15])
    own.start()

    barrier = pltpu.get_barrier_semaphore()

    def greet(step, carry):
        pl.semaphore_signal(
            barrier, inc=1, device_id=at_grid(lax.rem(grid + step, SIDE * SIDE)), device_id_type=MESH)
        return carry

    lax.fori_loop(1, SIDE * SIDE, greet, 0)
    for other in (up, down, pair):
        pl.semaphore_signal(barrier, inc=1, device_id=other, device_id_type=MESH)

    for load in loads:
        load.start()
    own.wait()

    flip = (grid > branch).astype(jnp.int32)
    lane = lax.broadcasted_iota(jnp.int32, (BS, 128), 1)
    for half in range(2):
        one = sigma[0:BS, pl.ds(pl.multiple_of(flip * BS + half * 128, 128), 128)]
        two = sigma[BS:2 * BS, pl.ds(pl.multiple_of((1 - flip) * BS + half * 128, 128), 128)]
        even = jnp.where(lane < SUB, one, pltpu.roll(two, SUB, 1))
        odd = jnp.where(lane < SUB, pltpu.roll(one, SUB, 1), two)
        for side, value in ((2 * half, even), (2 * half + 1, odd)):
            for m in range(SIDE):
                for xx in range(SIDE):
                    start = m * SUB + xx * SLICE
                    packed[m // 2, side * SIDE + xx, m % 2 * SLICE:(m % 2 + 1) * SLICE, :] = value[start:start + SLICE, :]

    @pl.when(grid == branch)
    def _():
        for half in range(2):
            value = sigma[0:BS, BS + half * 128:BS + (half + 1) * 128]
            turned = pltpu.roll(value, SUB, 1)
            for side, upper, lower in ((2 * half, value, turned), (2 * half + 1, turned, value)):
                for m in range(2):
                    for xx in range(SIDE):
                        start = m * SUB + xx * SLICE
                        extra[side * SIDE + xx, m * SLICE:(m + 1) * SLICE, :] = jnp.where(
                            lane[0:SLICE] < SUB, upper[start:start + SLICE, :],
                            lower[2 * SUB + start:2 * SUB + start + SLICE, :])

    pl.semaphore_wait(barrier, SIDE * SIDE + 2)

    def exchange(half):
        pltpu.make_async_copy(packed.at[half, grid], slots(core, z, half, grid), pack_recv.at[half]).start()

        def hand_out(step, carry):
            to = lax.rem(grid + step, SIDE * SIDE)
            pltpu.make_async_remote_copy(
                src_ref=packed.at[half, to], dst_ref=slots(core, z, half, grid), send_sem=pack_send,
                recv_sem=pack_recv.at[half], device_id=at_grid(to), device_id_type=MESH).start()
            return carry

        lax.fori_loop(1, SIDE * SIDE, hand_out, 0)

        if half == 0:
            @pl.when(grid == branch)
            def _():
                own_slot = slots(core, z, 0, SLOTS - 1)
                pltpu.make_async_copy(extra.at[grid], own_slot, extra_recv).start()

                def hand_extra(step, carry):
                    to = lax.rem(grid + step, SIDE * SIDE)
                    pltpu.make_async_remote_copy(
                        src_ref=extra.at[to], dst_ref=own_slot, send_sem=extra_send,
                        recv_sem=extra_recv, device_id=at_grid(to), device_id_type=MESH).start()
                    return carry

                lax.fori_loop(1, SIDE * SIDE, hand_extra, 0)

    def piece_of(source, piece):
        half, start, size = PIECES[piece]
        return slots(core, source, half, start, size)

    def pass_on(source, piece, to, recv_sem):
        ref = piece_of(source, piece)
        pltpu.make_async_remote_copy(
            src_ref=ref, dst_ref=ref, send_sem=z_send, recv_sem=recv_sem, device_id=to, device_id_type=MESH).start()

    def to_pair(source, piece):
        ref = piece_of(source, piece)
        pltpu.make_async_remote_copy(
            src_ref=ref, dst_ref=ref, send_sem=pair_send, recv_sem=pair_recv, device_id=pair,
            device_id_type=MESH).start()

    def await_bytes(ref, sem):
        pltpu.make_async_copy(ref, ref, sem).wait()

    exchange(0)
    for piece in range(4):
        half = PIECES[piece][0]
        if piece % 2 == 0:
            await_bytes(slots(core, z, half, 0, SIDE * SIDE), pack_recv.at[half])
        if piece == 0:
            await_bytes(slots(core, z, 0, SLOTS - 1), extra_recv)
        pass_on(z, piece, up, right_recv.at[1, piece])
        pass_on(z, piece, down, left_recv.at[1, piece])
        to_pair(z, piece)
        if piece == 1:
            exchange(1)

    def leaf_of(k):
        found, index = 0, 0
        for t in range(NS2):
            same = (leaf[0, t] == k).astype(jnp.int32)
            found = found + same
            index = index + same * t
        return jnp.minimum(index, NS2 - 1), found.astype(F32)

    def factors():
        for load in loads:
            load.wait()
        minv_s = split(minv[...])
        linv_s = split(linv[...])
        v0_s = split(product(split(first_raw[...]), linv_s))
        v0_hi[...], v0_lo[...] = v0_s
        for part in range(2):
            vblocks[part] = product(split(loff[part].reshape(NS2 * SUB, BS)), linv_s).reshape(NS2, SUB, BS)
        square = product_t(minv_s, minv_s)
        base[0] = square
        turned = product(split(square), v0_s)
        base[1] = -turned
        base[2] = product_t(linv_s, linv_s) + product_t(v0_s, split(turned))
        for part in range(2):
            def rows(q, carry):
                raw = moff[part, pl.ds(q * 4, 4)].reshape(BS, BS)
                u = product(split(raw), (split(minv[...])))
                u_s = split(u)
                uv = product(u_s, (v0_hi[...], v0_lo[...]))
                spread = []
                for j in range(4):
                    index, mark = leaf_of(q * 4 + j)
                    spread.append(vblocks[part, index] * mark)
                t = jnp.concatenate(spread, axis=0) - uv
                t_s = split(t)
                at = pl.ds(pl.multiple_of(q * BS, BS), BS)
                for kind, pieces in ((0, u_s), (1, t_s)):
                    w_hi[part, at, kind * BS:(kind + 1) * BS] = pieces[0]
                    w_lo[part, at, kind * BS:(kind + 1) * BS] = pieces[1]
                if part == 1:
                    for kind, value in ((0, u), (1, t)):
                        high, low = split(value.T)
                        wt_hi[kind * BS:(kind + 1) * BS, at] = high
                        wt_lo[kind * BS:(kind + 1) * BS, at] = low
                return carry
            lax.fori_loop(0, 3, rows, 0)

    factors()

    for step in range(1, 5):
        below = lax.rem(z + RING - step, RING)
        above = lax.rem(z + step, RING)
        for piece in range(4):
            if step < 4 or piece < 2:
                await_bytes(piece_of(below, piece), right_recv.at[step, piece])
                if step < 3 or (step == 3 and piece < 2):
                    pass_on(below, piece, up, right_recv.at[step + 1, piece])
                to_pair(below, piece)
            if step < 4 or piece >= 2:
                await_bytes(piece_of(above, piece), left_recv.at[step, piece])
                if step < 3 or (step == 3 and piece >= 2):
                    pass_on(above, piece, down, left_recv.at[step + 1, piece])
                to_pair(above, piece)
    await_bytes(slots(1 - core, 0, 0, 0, RING * TILES), pair_recv)

    narrow = lax.broadcasted_iota(jnp.int32, (HALF, 128), 1) < SUB

    def select(k, carry):
        si = struct[0, k]
        gi, ai = si >> 1, si & 1
        for p in range(NS1 // 2):
            sides = [[], []]
            for h in range(2):
                sj = struct[0, 2 * p + h]
                bj, cj = sj >> 1, sj & 1
                beyond = (gi > bj).astype(jnp.int32)
                plain = (cj == (ai ^ beyond)).astype(jnp.int32)
                own = ((gi == bj).astype(jnp.int32)) * (1 - ai) * cj
                weight = (plain + own).astype(F32) * (1.0 - 0.5 * (si == sj).astype(F32))
                for half in range(2):
                    slot = own * (SLOTS - 1) + (1 - own) * (half * SLOTS + gi)
                    there = own * half + (1 - own) * ai
                    stay = (there == h).astype(F32)
                    share = gathered[((bj & 1) * RING + (bj >> 1)) * TILES + slot]
                    sides[half].append(
                        share * (weight * stay) + pltpu.roll(share, SUB, 1) * (weight * (1.0 - stay)))
            for half in range(2):
                row = pl.ds(pl.multiple_of(k * SUB + half * HALF, HALF), HALF)
                high, low = split(jnp.where(narrow, sides[half][0], sides[half][1]))
                a_hi[row, p * 128:(p + 1) * 128] = high
                a_lo[row, p * 128:(p + 1) * 128] = low
        return carry

    lax.fori_loop(0, NS1, select, 0)

    def send(src, dst, send_sem, recv_sem, to):
        copy = pltpu.make_async_remote_copy(
            src_ref=src, dst_ref=dst, send_sem=send_sem, recv_sem=recv_sem, device_id=to, device_id_type=MESH)
        copy.start()
        return copy

    started = []

    def first_hop(axis, chunk, recv, sends, recvs):
        plus, minus = around[axis]
        far = lax.rem(place[axis] + 2, SIDE)
        started.append(send(chunk(far, 0), recv.at[0], sends.at[0], recvs.at[0], plus))
        started.append(send(chunk(far, 1), recv.at[2], sends.at[2], recvs.at[2], minus))

    def direct_hop(axis, chunk, recv, sends, recvs):
        plus, minus = around[axis]
        nxt, prv = lax.rem(place[axis] + 1, SIDE), lax.rem(place[axis] + 3, SIDE)
        started.append(send(chunk(nxt, 1), recv.at[1], sends.at[1], recvs.at[1], plus))
        started.append(send(chunk(prv, 0), recv.at[3], sends.at[3], recvs.at[3], minus))

    def second_hop(axis, chunk, recv, comb, sends, recvs):
        me = place[axis]
        plus, minus = around[axis]
        nxt, prv = lax.rem(me + 1, SIDE), lax.rem(me + 3, SIDE)
        await_bytes(recv.at[0], recvs.at[0])
        comb[0] = recv[0] + chunk(nxt, 0)[...]
        started.append(send(comb.at[0], recv.at[4], sends.at[4], recvs.at[4], plus))
        await_bytes(recv.at[2], recvs.at[2])
        comb[1] = recv[2] + chunk(prv, 1)[...]
        started.append(send(comb.at[1], recv.at[5], sends.at[5], recvs.at[5], minus))

    def arrive(recv, recvs):
        for slot in (1, 3, 4, 5):
            await_bytes(recv.at[slot], recvs.at[slot])

    def left_rows(r, carry):
        at = pl.ds(pl.multiple_of(r * BS, BS), BS)
        ysum[0, pl.ds(r * 4, 4)] = product((a_hi[at, :], a_lo[at, :]), (w_hi[0], w_lo[0])).reshape(4, SUB, 2 * BS)
        return carry

    def gram(left, right):
        at = slice(left * BS, (left + 1) * BS)
        return product((wt_hi[at, :], wt_lo[at, :]), split(ysum[0, :, :, right * BS:(right + 1) * BS].reshape(ROWS, BS)))

    def put_gram(first, value):
        for part in range(16):
            low, high = max(part * 40, first), min(part * 40 + 40, first + value.shape[0])
            if low < high:
                gsend[part // 8, part % 8 // 2, part % 2, low - part * 40:high - part * 40, :] = (
                    value[low - first:high - first, :])

    def g_chunk(axis):
        return lambda t, h: gsend.at[axis, t, h]

    def y_chunk(axis):
        return lambda t, h: ysend.at[axis, t, h]

    def g_ring(axis):
        return axis, g_chunk(axis), grecv.at[axis], g_send_sem.at[axis], g_recv_sem.at[axis]

    def y_ring(axis):
        return axis, y_chunk(axis), yrecv.at[axis], y_send_sem.at[axis], y_recv_sem.at[axis]

    def pack_rows(source, axis):
        for n in range(OUTS):
            if n < NS1:
                value = ysum[source, n, :, 0:BS]
            else:
                value = ysum[source, leaf[0, n - NS1], :, BS:2 * BS]
            for t in range(SIDE):
                ysend[axis, t, n // 9, n % 9] = value[t * SLICE:(t + 1) * SLICE, :]

    def right_rows(r, carry):
        at = pl.ds(pl.multiple_of(r * BS, BS), BS)
        ysum[1, pl.ds(r * 4, 4)] = product_t((a_hi[:, at], a_lo[:, at]), (w_hi[1], w_lo[1])).reshape(4, SUB, 2 * BS)
        return carry


    def g_sum_and_exchange(axis):
        recv, recvs, sends = grecv.at[axis], g_recv_sem.at[axis], g_send_sem.at[axis]
        me = place[axis]
        arrive(recv, recvs)
        gred[axis, 0] = (gsend[axis, me, 0] + recv[3]) + recv[4]
        gred[axis, 1] = (gsend[axis, me, 1] + recv[1]) + recv[5]
        plus, minus = around[1 - axis]
        started.append(send(gred.at[axis], gexch.at[axis, 0], sends.at[6], recvs.at[6], plus))
        started.append(send(gred.at[axis], gexch.at[axis, 1], sends.at[7], recvs.at[7], minus))

    def g_exchange_on(axis):
        recvs, sends = g_recv_sem.at[axis], g_send_sem.at[axis]
        plus, minus = around[1 - axis]
        await_bytes(gexch.at[axis, 0], recvs.at[6])
        started.append(send(gexch.at[axis, 0, 0], gexch.at[axis, 2, 0], sends.at[8], recvs.at[8], plus))
        await_bytes(gexch.at[axis, 1], recvs.at[7])
        started.append(send(gexch.at[axis, 1, 1], gexch.at[axis, 2, 1], sends.at[9], recvs.at[9], minus))

    def g_spread(axis):
        recvs, sends = g_recv_sem.at[axis], g_send_sem.at[axis]
        me = place[axis]
        plus, minus = around[axis]
        await_bytes(gexch.at[axis, 2, 0], recvs.at[8])
        await_bytes(gexch.at[axis, 2, 1], recvs.at[9])
        gall[axis, me] = (gred[axis] + gexch[axis, 2]) + (gexch[axis, 0] + gexch[axis, 1])
        started.append(send(gall.at[axis, me], gall.at[axis, me], sends.at[10], recvs.at[10], plus))
        started.append(send(gall.at[axis, me], gall.at[axis, me], sends.at[11], recvs.at[11], minus))

    def g_spread_on(axis):
        recvs, sends = g_recv_sem.at[axis], g_send_sem.at[axis]
        me = place[axis]
        plus, minus = around[axis]
        prv, nxt, far = lax.rem(me + 3, SIDE), lax.rem(me + 1, SIDE), lax.rem(me + 2, SIDE)
        await_bytes(gall.at[axis, prv], recvs.at[10])
        started.append(send(gall.at[axis, prv, 0], gall.at[axis, prv, 0], sends.at[12], recvs.at[12], plus))
        await_bytes(gall.at[axis, nxt], recvs.at[11])
        started.append(send(gall.at[axis, nxt, 1], gall.at[axis, nxt, 1], sends.at[13], recvs.at[13], minus))

    def g_second(axis):
        second_hop(axis, g_chunk(axis), grecv.at[axis], gcomb.at[axis], g_send_sem.at[axis], g_recv_sem.at[axis])

    def y_second(axis):
        second_hop(axis, y_chunk(axis), yrecv.at[axis], ycomb.at[axis], y_send_sem.at[axis], y_recv_sem.at[axis])

    lax.fori_loop(0, 3, left_rows, 0)
    pack_rows(0, 1)
    first_hop(*y_ring(1))
    h00 = gram(0, 0)
    h00 = h00 + h00.T
    put_gram(0, h00[0:128])
    put_gram(384, gram(0, 1) + gram(1, 0).T)
    h11 = gram(1, 1)
    h11 = h11 + h11.T
    put_gram(128, h11[0:128])
    put_gram(256, jnp.concatenate([h00[128:, 128:], h11[128:, 128:]], axis=1))
    for axis in (0, 1):
        first_hop(*g_ring(axis))
        direct_hop(*g_ring(axis))
    direct_hop(*y_ring(1))
    lax.fori_loop(0, 3, right_rows, 0)
    pack_rows(1, 0)
    for axis in (0, 1):
        g_second(axis)
    first_hop(*y_ring(0))
    y_second(1)
    for axis in (0, 1):
        g_sum_and_exchange(axis)
    direct_hop(*y_ring(0))
    for axis in (0, 1):
        g_exchange_on(axis)
    y_second(0)
    for axis in (0, 1):
        g_spread(axis)
    for axis in (0, 1):
        g_spread_on(axis)

    for axis in (1, 0):
        arrive(yrecv.at[axis], y_recv_sem.at[axis])
    for half, direct, through in ((0, 3, 4), (1, 1, 5)):
        total = 0.0
        for axis in (0, 1):
            total = total + ((ysend[axis, place[axis], half] + yrecv[axis, direct]) + yrecv[axis, through])
        ycomb[2, half] = -total
    for n in range(NS1):
        column_out[0, n] = ycomb[2, n // 9, n % 9]
        index, mark = leaf_of(n)
        column_out[1, n] = ycomb[2, 1, index + (NS1 - 9)] * mark

    outs = [
        pltpu.make_async_copy(column_out.at[0], mid_hbm, out_sem.at[0]),
        pltpu.make_async_copy(column_out.at[1], column_hbm, out_sem.at[1]),
        pltpu.make_async_copy(gram_out, gram_hbm, out_sem.at[2]),
    ]
    outs[0].start()
    outs[1].start()
    for copy in started[:-4]:
        copy.wait_send()
    for half in range(2):
        await_bytes(packed.at[half, pl.ds(0, SIDE * SIDE - 1)], pack_send)

    @pl.when(grid == branch)
    def _():
        await_bytes(extra.at[pl.ds(0, SIDE * SIDE - 1)], extra_send)

    await_bytes(slots(core, 0, 0, 0, (RING - 1) * TILES), z_send)
    await_bytes(slots(core, 0, 0, 0, RING * TILES), pair_send)
    for axis in (0, 1):
        far = lax.rem(place[axis] + 2, SIDE)
        await_bytes(gall.at[axis, far, 0], g_recv_sem.at[axis, 12])
        await_bytes(gall.at[axis, far, 1], g_recv_sem.at[axis, 13])
    total = gall[...].reshape(640, BS)
    gram_out[1] = total[384:640] + base[1]
    for index, first in ((0, 0), (2, 128)):
        upper = total[first:first + 128]
        gram_out[index, 0:128, :] = upper + base[index, 0:128, :]
        gram_out[index, 128:256, 0:128] = upper[:, 128:].T + base[index, 128:256, 0:128]
        gram_out[index, 128:256, 128:256] = total[256:384, first:first + 128] + base[index, 128:256, 128:256]

    outs[2].start()

    for copy in started[-4:]:
        copy.wait_send()
    for copy in outs:
        copy.wait()


def write_out(mid, leaf, gram, mid_out, diag_out, leaf_out, parent_out, leaf_diag_out, columns, blocks, in_sem, out_sem):
    parts = (
        (mid, columns.at[0], mid_out), (leaf, columns.at[1], leaf_out), (gram.at[0], blocks.at[0], diag_out),
        (gram.at[1], blocks.at[1], parent_out), (gram.at[2], blocks.at[2], leaf_diag_out))
    ins = [pltpu.make_async_copy(src, held, in_sem.at[n]) for n, (src, held, _) in enumerate(parts)]
    outs = [pltpu.make_async_copy(held, dst.at[0], out_sem.at[n]) for n, (_, held, dst) in enumerate(parts)]
    for copy in ins:
        copy.start()
    for came, goes in zip(ins, outs):
        came.wait()
        goes.start()
    for copy in outs:
        copy.wait()


def on_device(sigma_top, mid_struct, leaf_struct, mid_inv, mid_off, leaf_inv, leaf_off):
    hbm = pl.BlockSpec(memory_space=pltpu.HBM)
    dma = pltpu.SemaphoreType.DMA
    middle, leaves, grams = pl.pallas_call(
        kernel,
        out_shape=(
            jax.ShapeDtypeStruct((NS1, SLICE, BS), F32),
            jax.ShapeDtypeStruct((NS1, SLICE, BS), F32),
            jax.ShapeDtypeStruct((3, BS, BS), F32),
        ),
        in_specs=[hbm] * 7,
        out_specs=(hbm,) * 3,
        scratch_shapes=[
            pltpu.SMEM((1, NS1), jnp.int32),
            pltpu.SMEM((1, NS2), jnp.int32),
            pltpu.VMEM((2 * BS, 2 * BS), F32),
            pltpu.VMEM((2, SIDE * SIDE, HALF, 128), F32),
            pltpu.VMEM((SIDE * SIDE, HALF, 128), F32),
            pltpu.VMEM((2 * RING * TILES, HALF, 128), F32),
            pltpu.VMEM((2, NS1, SUB, BS), F32),
            pltpu.VMEM((2, NS2, SUB, BS), F32),
            pltpu.VMEM((BS, BS), F32),
            pltpu.VMEM((BS, BS), F32),
            pltpu.VMEM((BS, BS), F32),
            pltpu.VMEM((2, NS2, SUB, BS), F32),
            pltpu.VMEM((BS, BS), BF16),
            pltpu.VMEM((BS, BS), BF16),
            pltpu.VMEM((3, BS, BS), F32),
            pltpu.VMEM((2, ROWS, 2 * BS), BF16),
            pltpu.VMEM((2, ROWS, 2 * BS), BF16),
            pltpu.VMEM((2 * BS, ROWS), BF16),
            pltpu.VMEM((2 * BS, ROWS), BF16),
            pltpu.VMEM((ROWS, ROWS), BF16),
            pltpu.VMEM((ROWS, ROWS), BF16),
            pltpu.VMEM((2, NS1, SUB, 2 * BS), F32),
            pltpu.VMEM((2, SIDE, 2, 9, SLICE, BS), F32),
            pltpu.VMEM((2, 6, 9, SLICE, BS), F32),
            pltpu.VMEM((3, 2, 9, SLICE, BS), F32),
            pltpu.VMEM((2, SIDE, 2, 40, BS), F32),
            pltpu.VMEM((2, 6, 40, BS), F32),
            pltpu.VMEM((2, 2, 40, BS), F32),
            pltpu.VMEM((2, 2, 40, BS), F32),
            pltpu.VMEM((2, 3, 2, 40, BS), F32),
            pltpu.VMEM((2, SIDE, 2, 40, BS), F32),
            pltpu.VMEM((2, NS1, SLICE, BS), F32),
            pltpu.VMEM((3, BS, BS), F32),
            dma((3,)),
            dma((16,)),
            dma,
            dma((2,)),
            dma,
            dma,
            dma,
            dma((5, 4)),
            dma((5, 4)),
            dma,
            dma,
            dma((2, 6)),
            dma((2, 6)),
            dma((2, 14)),
            dma((2, 14)),
        ],
        compiler_params=pltpu.CompilerParams(
            collective_id=0, has_side_effects=True, vmem_limit_bytes=64 * 1024 * 1024),
    )(mid_struct, leaf_struct, sigma_top, mid_inv, mid_off, leaf_inv, leaf_off)
    block = jax.ShapeDtypeStruct((1, BS, BS), F32)
    column = jax.ShapeDtypeStruct((1, NS1, SLICE, BS), F32)
    return tuple(pl.pallas_call(
        write_out,
        out_shape=(column, block, column, block, block),
        in_specs=[hbm] * 3,
        out_specs=(hbm,) * 5,
        scratch_shapes=[
            pltpu.VMEM((2, NS1, SLICE, BS), F32), pltpu.VMEM((3, BS, BS), F32), dma((5,)), dma((5,))],
        compiler_params=pltpu.CompilerParams(vmem_limit_bytes=64 * 1024 * 1024),
    )(middle, leaves, grams))


def solution(mesh):
    in_specs = (
        P("grid", "branch"),
        P("branch", None),
        P("branch", None),
        P("branch", None, None),
        P("branch", None, None, None),
        P("branch", None, None),
        P("branch", None, None, None),
    )
    out_specs = (
        P("branch", None, "grid", None),
        P("branch", None, None),
        P("branch", None, "grid", None),
        P("branch", None, None),
        P("branch", None, None),
    )
    return jax.shard_map(
        on_device, mesh=mesh, in_specs=in_specs, out_specs=out_specs, check_vma=False
    )
```

```python
import jax
import jax.numpy as jnp
from jax import lax
from jax.experimental import pallas as pl
from jax.experimental.pallas import tpu as pltpu
from jax.sharding import PartitionSpec as P

MESH = pl.DeviceIdType.MESH
F32 = jnp.float32
BF16 = jnp.bfloat16
BS = 256
NS1 = 12
NS2 = 6
SIDE = 4
RING = 8
SUB = BS // SIDE
SLICE = 16
SLOTS = 17
HALF = SUB // 2
TILES = 2 * SLOTS - 1
PIECES = ((0, 0, 8), (0, 8, 9), (1, 0, 8), (1, 8, 8))
ROWS = NS1 * SUB
OUTS = NS1 + NS2


def split(value):
    high = value.astype(BF16)
    return high, (value - high.astype(F32)).astype(BF16)


def product(left, right, dims=(((1,), (0,)), ((), ()))):
    def one(a, b):
        return lax.dot_general(a, b, dims, preferred_element_type=F32)
    return one(left[0], right[0]) + (one(left[0], right[1]) + one(left[1], right[0]))


def product_t(left, right):
    return product(left, right, (((0,), (0,)), ((), ())))


def kernel(
    struct_hbm, leaf_hbm, sigma_hbm, minv_hbm, moff_hbm, linv_hbm, loff_hbm,
    mid_hbm, column_hbm, gram_hbm,
    struct, leaf, sigma, packed, extra, gathered, moff, loff, first_raw, minv, linv, vblocks, v0_hi, v0_lo, base,
    w_hi, w_lo, wt_hi, wt_lo, a_hi, a_lo, ysum, ysend, yrecv, ycomb, gsend, grecv, gcomb, gred, gexch, gall,
    column_out, gram_out, out_sem,
    load_sem, pack_send, pack_recv, extra_send, extra_recv, z_send, right_recv, left_recv,
    pair_send, pair_recv, y_send_sem, y_recv_sem, g_send_sem, g_recv_sem,
):
    branch = lax.axis_index("branch")
    grid = lax.axis_index("grid")
    z, core = branch // 2, branch % 2
    y, x = grid // SIDE, grid % SIDE

    def slots(which_core, source, half, slot, size=None):
        start = (which_core * RING + source) * TILES + half * SLOTS + slot
        return gathered.at[start] if size is None else gathered.at[pl.ds(start, size)]

    def at_grid(index):
        return {"branch": branch, "grid": index}

    def at_branch(index):
        return {"branch": index, "grid": grid}

    up = at_branch(lax.rem(z + 1, RING) * 2 + core)
    down = at_branch(lax.rem(z + RING - 1, RING) * 2 + core)
    pair = at_branch(z * 2 + (1 - core))
    around = (
        (at_grid(y * SIDE + lax.rem(x + 1, SIDE)), at_grid(y * SIDE + lax.rem(x + SIDE - 1, SIDE))),
        (at_grid(lax.rem(y + 1, SIDE) * SIDE + x), at_grid(lax.rem(y + SIDE - 1, SIDE) * SIDE + x)),
    )
    place = (x, y)

    row_c = pl.multiple_of(y * SUB, SUB)
    loads = [
        pltpu.make_async_copy(minv_hbm.at[0], minv, load_sem.at[0]),
        pltpu.make_async_copy(linv_hbm.at[0], linv, load_sem.at[1]),
        pltpu.make_async_copy(loff_hbm.at[0, 0], first_raw, load_sem.at[2]),
        pltpu.make_async_copy(moff_hbm.at[0, :, pl.ds(row_c, SUB), :], moff.at[0], load_sem.at[3]),
        pltpu.make_async_copy(loff_hbm.at[0, pl.ds(1, NS2), pl.ds(row_c, SUB), :], loff.at[0], load_sem.at[4]),
    ]
    for m in range(SIDE):
        row_r = pl.multiple_of(m * SUB + x * SLICE, SLICE)
        into = pl.ds(m * SLICE, SLICE)
        loads.append(pltpu.make_async_copy(
            moff_hbm.at[0, :, pl.ds(row_r, SLICE), :], moff.at[1, :, into, :], load_sem.at[5 + m]))
        loads.append(pltpu.make_async_copy(
            loff_hbm.at[0, pl.ds(1, NS2), pl.ds(row_r, SLICE), :], loff.at[1, :, into, :], load_sem.at[9 + m]))
    loads.append(pltpu.make_async_copy(struct_hbm, struct, load_sem.at[13]))
    loads.append(pltpu.make_async_copy(leaf_hbm, leaf, load_sem.at[14]))
    own = pltpu.make_async_copy(sigma_hbm, sigma, load_sem.at[15])
    own.start()

    barrier = pltpu.get_barrier_semaphore()

    def greet(step, carry):
        pl.semaphore_signal(
            barrier, inc=1, device_id=at_grid(lax.rem(grid + step, SIDE * SIDE)), device_id_type=MESH)
        return carry

    lax.fori_loop(1, SIDE * SIDE, greet, 0)
    for other in (up, down, pair):
        pl.semaphore_signal(barrier, inc=1, device_id=other, device_id_type=MESH)

    for load in loads:
        load.start()
    own.wait()

    flip = (grid > branch).astype(jnp.int32)
    lane = lax.broadcasted_iota(jnp.int32, (BS, 128), 1)
    for half in range(2):
        one = sigma[0:BS, pl.ds(pl.multiple_of(flip * BS + half * 128, 128), 128)]
        two = sigma[BS:2 * BS, pl.ds(pl.multiple_of((1 - flip) * BS + half * 128, 128), 128)]
        even = jnp.where(lane < SUB, one, pltpu.roll(two, SUB, 1))
        odd = jnp.where(lane < SUB, pltpu.roll(one, SUB, 1), two)
        for side, value in ((2 * half, even), (2 * half + 1, odd)):
            for m in range(SIDE):
                for xx in range(SIDE):
                    start = m * SUB + xx * SLICE
                    packed[m // 2, side * SIDE + xx, m % 2 * SLICE:(m % 2 + 1) * SLICE, :] = value[start:start + SLICE, :]

    @pl.when(grid == branch)
    def _():
        for half in range(2):
            value = sigma[0:BS, BS + half * 128:BS + (half + 1) * 128]
            turned = pltpu.roll(value, SUB, 1)
            for side, upper, lower in ((2 * half, value, turned), (2 * half + 1, turned, value)):
                for m in range(2):
                    for xx in range(SIDE):
                        start = m * SUB + xx * SLICE
                        extra[side * SIDE + xx, m * SLICE:(m + 1) * SLICE, :] = jnp.where(
                            lane[0:SLICE] < SUB, upper[start:start + SLICE, :],
                            lower[2 * SUB + start:2 * SUB + start + SLICE, :])

    pl.semaphore_wait(barrier, SIDE * SIDE + 2)

    def exchange(half):
        pltpu.make_async_copy(packed.at[half, grid], slots(core, z, half, grid), pack_recv.at[half]).start()

        def hand_out(step, carry):
            to = lax.rem(grid + step, SIDE * SIDE)
            pltpu.make_async_remote_copy(
                src_ref=packed.at[half, to], dst_ref=slots(core, z, half, grid), send_sem=pack_send,
                recv_sem=pack_recv.at[half], device_id=at_grid(to), device_id_type=MESH).start()
            return carry

        lax.fori_loop(1, SIDE * SIDE, hand_out, 0)

        if half == 0:
            @pl.when(grid == branch)
            def _():
                own_slot = slots(core, z, 0, SLOTS - 1)
                pltpu.make_async_copy(extra.at[grid], own_slot, extra_recv).start()

                def hand_extra(step, carry):
                    to = lax.rem(grid + step, SIDE * SIDE)
                    pltpu.make_async_remote_copy(
                        src_ref=extra.at[to], dst_ref=own_slot, send_sem=extra_send,
                        recv_sem=extra_recv, device_id=at_grid(to), device_id_type=MESH).start()
                    return carry

                lax.fori_loop(1, SIDE * SIDE, hand_extra, 0)

    def piece_of(source, piece):
        half, start, size = PIECES[piece]
        return slots(core, source, half, start, size)

    def pass_on(source, piece, to, recv_sem):
        ref = piece_of(source, piece)
        pltpu.make_async_remote_copy(
            src_ref=ref, dst_ref=ref, send_sem=z_send, recv_sem=recv_sem, device_id=to, device_id_type=MESH).start()

    def to_pair(source, piece):
        ref = piece_of(source, piece)
        pltpu.make_async_remote_copy(
            src_ref=ref, dst_ref=ref, send_sem=pair_send, recv_sem=pair_recv, device_id=pair,
            device_id_type=MESH).start()

    def await_bytes(ref, sem):
        pltpu.make_async_copy(ref, ref, sem).wait()

    exchange(0)
    for piece in range(4):
        half = PIECES[piece][0]
        if piece % 2 == 0:
            await_bytes(slots(core, z, half, 0, SIDE * SIDE), pack_recv.at[half])
        if piece == 0:
            await_bytes(slots(core, z, 0, SLOTS - 1), extra_recv)
        pass_on(z, piece, up, right_recv.at[1, piece])
        pass_on(z, piece, down, left_recv.at[1, piece])
        to_pair(z, piece)
        if piece == 1:
            exchange(1)

    def leaf_of(k):
        found, index = 0, 0
        for t in range(NS2):
            same = (leaf[0, t] == k).astype(jnp.int32)
            found = found + same
            index = index + same * t
        return jnp.minimum(index, NS2 - 1), found.astype(F32)

    def factors():
        for load in loads:
            load.wait()
        minv_s = split(minv[...])
        linv_s = split(linv[...])
        v0_s = split(product(split(first_raw[...]), linv_s))
        v0_hi[...], v0_lo[...] = v0_s
        for part in range(2):
            vblocks[part] = product(split(loff[part].reshape(NS2 * SUB, BS)), linv_s).reshape(NS2, SUB, BS)
        square = product_t(minv_s, minv_s)
        base[0] = square
        turned = product(split(square), v0_s)
        base[1] = -turned
        base[2] = product_t(linv_s, linv_s) + product_t(v0_s, split(turned))
        for part in range(2):
            def rows(q, carry):
                raw = moff[part, pl.ds(q * 4, 4)].reshape(BS, BS)
                u = product(split(raw), (split(minv[...])))
                u_s = split(u)
                uv = product(u_s, (v0_hi[...], v0_lo[...]))
                spread = []
                for j in range(4):
                    index, mark = leaf_of(q * 4 + j)
                    spread.append(vblocks[part, index] * mark)
                t = jnp.concatenate(spread, axis=0) - uv
                t_s = split(t)
                at = pl.ds(pl.multiple_of(q * BS, BS), BS)
                for kind, pieces in ((0, u_s), (1, t_s)):
                    w_hi[part, at, kind * BS:(kind + 1) * BS] = pieces[0]
                    w_lo[part, at, kind * BS:(kind + 1) * BS] = pieces[1]
                if part == 1:
                    for kind, value in ((0, u), (1, t)):
                        high, low = split(value.T)
                        wt_hi[kind * BS:(kind + 1) * BS, at] = high
                        wt_lo[kind * BS:(kind + 1) * BS, at] = low
                return carry
            lax.fori_loop(0, 3, rows, 0)

    factors()

    for step in range(1, 5):
        below = lax.rem(z + RING - step, RING)
        above = lax.rem(z + step, RING)
        for piece in range(4):
            if step < 4 or piece < 2:
                await_bytes(piece_of(below, piece), right_recv.at[step, piece])
                if step < 3 or (step == 3 and piece < 2):
                    pass_on(below, piece, up, right_recv.at[step + 1, piece])
                to_pair(below, piece)
            if step < 4 or piece >= 2:
                await_bytes(piece_of(above, piece), left_recv.at[step, piece])
                if step < 3 or (step == 3 and piece >= 2):
                    pass_on(above, piece, down, left_recv.at[step + 1, piece])
                to_pair(above, piece)
    await_bytes(slots(1 - core, 0, 0, 0, RING * TILES), pair_recv)

    narrow = lax.broadcasted_iota(jnp.int32, (HALF, 128), 1) < SUB

    def select(k, carry):
        si = struct[0, k]
        gi, ai = si >> 1, si & 1
        for p in range(NS1 // 2):
            sides = [[], []]
            for h in range(2):
                sj = struct[0, 2 * p + h]
                bj, cj = sj >> 1, sj & 1
                beyond = (gi > bj).astype(jnp.int32)
                plain = (cj == (ai ^ beyond)).astype(jnp.int32)
                own = ((gi == bj).astype(jnp.int32)) * (1 - ai) * cj
                weight = (plain + own).astype(F32) * (1.0 - 0.5 * (si == sj).astype(F32))
                for half in range(2):
                    slot = own * (SLOTS - 1) + (1 - own) * (half * SLOTS + gi)
                    there = own * half + (1 - own) * ai
                    stay = (there == h).astype(F32)
                    share = gathered[((bj & 1) * RING + (bj >> 1)) * TILES + slot]
                    sides[half].append(
                        share * (weight * stay) + pltpu.roll(share, SUB, 1) * (weight * (1.0 - stay)))
            for half in range(2):
                row = pl.ds(pl.multiple_of(k * SUB + half * HALF, HALF), HALF)
                high, low = split(jnp.where(narrow, sides[half][0], sides[half][1]))
                a_hi[row, p * 128:(p + 1) * 128] = high
                a_lo[row, p * 128:(p + 1) * 128] = low
        return carry

    lax.fori_loop(0, NS1, select, 0)

    def send(src, dst, send_sem, recv_sem, to):
        copy = pltpu.make_async_remote_copy(
            src_ref=src, dst_ref=dst, send_sem=send_sem, recv_sem=recv_sem, device_id=to, device_id_type=MESH)
        copy.start()
        return copy

    started = []

    def first_hop(axis, chunk, recv, sends, recvs):
        plus, minus = around[axis]
        far = lax.rem(place[axis] + 2, SIDE)
        started.append(send(chunk(far, 0), recv.at[0], sends.at[0], recvs.at[0], plus))
        started.append(send(chunk(far, 1), recv.at[2], sends.at[2], recvs.at[2], minus))

    def direct_hop(axis, chunk, recv, sends, recvs):
        plus, minus = around[axis]
        nxt, prv = lax.rem(place[axis] + 1, SIDE), lax.rem(place[axis] + 3, SIDE)
        started.append(send(chunk(nxt, 1), recv.at[1], sends.at[1], recvs.at[1], plus))
        started.append(send(chunk(prv, 0), recv.at[3], sends.at[3], recvs.at[3], minus))

    def second_hop(axis, chunk, recv, comb, sends, recvs):
        me = place[axis]
        plus, minus = around[axis]
        nxt, prv = lax.rem(me + 1, SIDE), lax.rem(me + 3, SIDE)
        await_bytes(recv.at[0], recvs.at[0])
        comb[0] = recv[0] + chunk(nxt, 0)[...]
        started.append(send(comb.at[0], recv.at[4], sends.at[4], recvs.at[4], plus))
        await_bytes(recv.at[2], recvs.at[2])
        comb[1] = recv[2] + chunk(prv, 1)[...]
        started.append(send(comb.at[1], recv.at[5], sends.at[5], recvs.at[5], minus))

    def arrive(recv, recvs):
        for slot in (1, 3, 4, 5):
            await_bytes(recv.at[slot], recvs.at[slot])

    def left_rows(r, carry):
        at = pl.ds(pl.multiple_of(r * BS, BS), BS)
        ysum[0, pl.ds(r * 4, 4)] = product((a_hi[at, :], a_lo[at, :]), (w_hi[0], w_lo[0])).reshape(4, SUB, 2 * BS)
        return carry

    def gram(left, right):
        at = slice(left * BS, (left + 1) * BS)
        return product((wt_hi[at, :], wt_lo[at, :]), split(ysum[0, :, :, right * BS:(right + 1) * BS].reshape(ROWS, BS)))

    def put_gram(first, value):
        for part in range(16):
            low, high = max(part * 40, first), min(part * 40 + 40, first + value.shape[0])
            if low < high:
                gsend[part // 8, part % 8 // 2, part % 2, low - part * 40:high - part * 40, :] = (
                    value[low - first:high - first, :])

    def g_chunk(axis):
        return lambda t, h: gsend.at[axis, t, h]

    def y_chunk(axis):
        return lambda t, h: ysend.at[axis, t, h]

    def g_ring(axis):
        return axis, g_chunk(axis), grecv.at[axis], g_send_sem.at[axis], g_recv_sem.at[axis]

    def y_ring(axis):
        return axis, y_chunk(axis), yrecv.at[axis], y_send_sem.at[axis], y_recv_sem.at[axis]

    def pack_rows(source, axis):
        for n in range(OUTS):
            if n < NS1:
                value = ysum[source, n, :, 0:BS]
            else:
                value = ysum[source, leaf[0, n - NS1], :, BS:2 * BS]
            for t in range(SIDE):
                ysend[axis, t, n // 9, n % 9] = value[t * SLICE:(t + 1) * SLICE, :]

    def right_rows(r, carry):
        at = pl.ds(pl.multiple_of(r * BS, BS), BS)
        ysum[1, pl.ds(r * 4, 4)] = product_t((a_hi[:, at], a_lo[:, at]), (w_hi[1], w_lo[1])).reshape(4, SUB, 2 * BS)
        return carry


    def g_sum_and_exchange(axis):
        recv, recvs, sends = grecv.at[axis], g_recv_sem.at[axis], g_send_sem.at[axis]
        me = place[axis]
        arrive(recv, recvs)
        gred[axis, 0] = (gsend[axis, me, 0] + recv[3]) + recv[4]
        gred[axis, 1] = (gsend[axis, me, 1] + recv[1]) + recv[5]
        plus, minus = around[1 - axis]
        started.append(send(gred.at[axis], gexch.at[axis, 0], sends.at[6], recvs.at[6], plus))
        started.append(send(gred.at[axis], gexch.at[axis, 1], sends.at[7], recvs.at[7], minus))

    def g_exchange_on(axis):
        recvs, sends = g_recv_sem.at[axis], g_send_sem.at[axis]
        plus, minus = around[1 - axis]
        await_bytes(gexch.at[axis, 0], recvs.at[6])
        started.append(send(gexch.at[axis, 0, 0], gexch.at[axis, 2, 0], sends.at[8], recvs.at[8], plus))
        await_bytes(gexch.at[axis, 1], recvs.at[7])
        started.append(send(gexch.at[axis, 1, 1], gexch.at[axis, 2, 1], sends.at[9], recvs.at[9], minus))

    def g_spread(axis):
        recvs, sends = g_recv_sem.at[axis], g_send_sem.at[axis]
        me = place[axis]
        plus, minus = around[axis]
        await_bytes(gexch.at[axis, 2, 0], recvs.at[8])
        await_bytes(gexch.at[axis, 2, 1], recvs.at[9])
        gall[axis, me] = (gred[axis] + gexch[axis, 2]) + (gexch[axis, 0] + gexch[axis, 1])
        started.append(send(gall.at[axis, me], gall.at[axis, me], sends.at[10], recvs.at[10], plus))
        started.append(send(gall.at[axis, me], gall.at[axis, me], sends.at[11], recvs.at[11], minus))

    def g_spread_on(axis):
        recvs, sends = g_recv_sem.at[axis], g_send_sem.at[axis]
        me = place[axis]
        plus, minus = around[axis]
        prv, nxt, far = lax.rem(me + 3, SIDE), lax.rem(me + 1, SIDE), lax.rem(me + 2, SIDE)
        await_bytes(gall.at[axis, prv], recvs.at[10])
        started.append(send(gall.at[axis, prv, 0], gall.at[axis, prv, 0], sends.at[12], recvs.at[12], plus))
        await_bytes(gall.at[axis, nxt], recvs.at[11])
        started.append(send(gall.at[axis, nxt, 1], gall.at[axis, nxt, 1], sends.at[13], recvs.at[13], minus))

    def g_second(axis):
        second_hop(axis, g_chunk(axis), grecv.at[axis], gcomb.at[axis], g_send_sem.at[axis], g_recv_sem.at[axis])

    def y_second(axis):
        second_hop(axis, y_chunk(axis), yrecv.at[axis], ycomb.at[axis], y_send_sem.at[axis], y_recv_sem.at[axis])

    lax.fori_loop(0, 3, left_rows, 0)
    pack_rows(0, 1)
    first_hop(*y_ring(1))
    put_gram(0, gram(0, 1) + gram(1, 0).T)
    h00 = gram(0, 0)
    h00 = h00 + h00.T
    put_gram(256, h00[0:128])
    first_hop(*g_ring(0))
    direct_hop(*g_ring(0))
    h11 = gram(1, 1)
    h11 = h11 + h11.T
    put_gram(384, h11[0:128])
    put_gram(512, jnp.concatenate([h00[128:, 128:], h11[128:, 128:]], axis=1))
    first_hop(*g_ring(1))
    direct_hop(*g_ring(1))
    direct_hop(*y_ring(1))
    lax.fori_loop(0, 3, right_rows, 0)
    pack_rows(1, 0)
    for axis in (0, 1):
        g_second(axis)
    first_hop(*y_ring(0))
    y_second(1)
    for axis in (0, 1):
        g_sum_and_exchange(axis)
    direct_hop(*y_ring(0))
    for axis in (0, 1):
        g_exchange_on(axis)
    y_second(0)
    for axis in (0, 1):
        g_spread(axis)
    for axis in (0, 1):
        g_spread_on(axis)

    for axis in (1, 0):
        arrive(yrecv.at[axis], y_recv_sem.at[axis])
    for half, direct, through in ((0, 3, 4), (1, 1, 5)):
        total = 0.0
        for axis in (0, 1):
            total = total + ((ysend[axis, place[axis], half] + yrecv[axis, direct]) + yrecv[axis, through])
        ycomb[2, half] = -total
    for n in range(NS1):
        column_out[0, n] = ycomb[2, n // 9, n % 9]
        index, mark = leaf_of(n)
        column_out[1, n] = ycomb[2, 1, index + (NS1 - 9)] * mark

    outs = [
        pltpu.make_async_copy(column_out.at[0], mid_hbm, out_sem.at[0]),
        pltpu.make_async_copy(column_out.at[1], column_hbm, out_sem.at[1]),
        pltpu.make_async_copy(gram_out, gram_hbm, out_sem.at[2]),
    ]
    outs[0].start()
    outs[1].start()
    for axis in (0, 1):
        far = lax.rem(place[axis] + 2, SIDE)
        await_bytes(gall.at[axis, far, 0], g_recv_sem.at[axis, 12])
        await_bytes(gall.at[axis, far, 1], g_recv_sem.at[axis, 13])
    total = gall[...].reshape(640, BS)
    gram_out[1] = total[0:256] + base[1]
    for index, first, side in ((0, 256, 0), (2, 384, 128)):
        upper = total[first:first + 128]
        gram_out[index, 0:128, :] = upper + base[index, 0:128, :]
        gram_out[index, 128:256, 0:128] = upper[:, 128:].T + base[index, 128:256, 0:128]
        gram_out[index, 128:256, 128:256] = total[512:640, side:side + 128] + base[index, 128:256, 128:256]

    outs[2].start()

    for copy in started:
        copy.wait_send()
    for half in range(2):
        await_bytes(packed.at[half, pl.ds(0, SIDE * SIDE - 1)], pack_send)

    @pl.when(grid == branch)
    def _():
        await_bytes(extra.at[pl.ds(0, SIDE * SIDE - 1)], extra_send)

    await_bytes(slots(core, 0, 0, 0, (RING - 1) * TILES), z_send)
    await_bytes(slots(core, 0, 0, 0, RING * TILES), pair_send)
    for copy in outs:
        copy.wait()


def write_out(mid, leaf, gram, mid_out, diag_out, leaf_out, parent_out, leaf_diag_out, columns, blocks, in_sem, out_sem):
    parts = (
        (mid, columns.at[0], mid_out), (leaf, columns.at[1], leaf_out), (gram.at[0], blocks.at[0], diag_out),
        (gram.at[1], blocks.at[1], parent_out), (gram.at[2], blocks.at[2], leaf_diag_out))
    ins = [pltpu.make_async_copy(src, held, in_sem.at[n]) for n, (src, held, _) in enumerate(parts)]
    outs = [pltpu.make_async_copy(held, dst.at[0], out_sem.at[n]) for n, (_, held, dst) in enumerate(parts)]
    for copy in ins:
        copy.start()
    for came, goes in zip(ins, outs):
        came.wait()
        goes.start()
    for copy in outs:
        copy.wait()


def on_device(sigma_top, mid_struct, leaf_struct, mid_inv, mid_off, leaf_inv, leaf_off):
    hbm = pl.BlockSpec(memory_space=pltpu.HBM)
    dma = pltpu.SemaphoreType.DMA
    middle, leaves, grams = pl.pallas_call(
        kernel,
        out_shape=(
            jax.ShapeDtypeStruct((NS1, SLICE, BS), F32),
            jax.ShapeDtypeStruct((NS1, SLICE, BS), F32),
            jax.ShapeDtypeStruct((3, BS, BS), F32),
        ),
        in_specs=[hbm] * 7,
        out_specs=(hbm,) * 3,
        scratch_shapes=[
            pltpu.SMEM((1, NS1), jnp.int32),
            pltpu.SMEM((1, NS2), jnp.int32),
            pltpu.VMEM((2 * BS, 2 * BS), F32),
            pltpu.VMEM((2, SIDE * SIDE, HALF, 128), F32),
            pltpu.VMEM((SIDE * SIDE, HALF, 128), F32),
            pltpu.VMEM((2 * RING * TILES, HALF, 128), F32),
            pltpu.VMEM((2, NS1, SUB, BS), F32),
            pltpu.VMEM((2, NS2, SUB, BS), F32),
            pltpu.VMEM((BS, BS), F32),
            pltpu.VMEM((BS, BS), F32),
            pltpu.VMEM((BS, BS), F32),
            pltpu.VMEM((2, NS2, SUB, BS), F32),
            pltpu.VMEM((BS, BS), BF16),
            pltpu.VMEM((BS, BS), BF16),
            pltpu.VMEM((3, BS, BS), F32),
            pltpu.VMEM((2, ROWS, 2 * BS), BF16),
            pltpu.VMEM((2, ROWS, 2 * BS), BF16),
            pltpu.VMEM((2 * BS, ROWS), BF16),
            pltpu.VMEM((2 * BS, ROWS), BF16),
            pltpu.VMEM((ROWS, ROWS), BF16),
            pltpu.VMEM((ROWS, ROWS), BF16),
            pltpu.VMEM((2, NS1, SUB, 2 * BS), F32),
            pltpu.VMEM((2, SIDE, 2, 9, SLICE, BS), F32),
            pltpu.VMEM((2, 6, 9, SLICE, BS), F32),
            pltpu.VMEM((3, 2, 9, SLICE, BS), F32),
            pltpu.VMEM((2, SIDE, 2, 40, BS), F32),
            pltpu.VMEM((2, 6, 40, BS), F32),
            pltpu.VMEM((2, 2, 40, BS), F32),
            pltpu.VMEM((2, 2, 40, BS), F32),
            pltpu.VMEM((2, 3, 2, 40, BS), F32),
            pltpu.VMEM((2, SIDE, 2, 40, BS), F32),
            pltpu.VMEM((2, NS1, SLICE, BS), F32),
            pltpu.VMEM((3, BS, BS), F32),
            dma((3,)),
            dma((16,)),
            dma,
            dma((2,)),
            dma,
            dma,
            dma,
            dma((5, 4)),
            dma((5, 4)),
            dma,
            dma,
            dma((2, 6)),
            dma((2, 6)),
            dma((2, 14)),
            dma((2, 14)),
        ],
        compiler_params=pltpu.CompilerParams(
            collective_id=0, has_side_effects=True, vmem_limit_bytes=64 * 1024 * 1024),
    )(mid_struct, leaf_struct, sigma_top, mid_inv, mid_off, leaf_inv, leaf_off)
    block = jax.ShapeDtypeStruct((1, BS, BS), F32)
    column = jax.ShapeDtypeStruct((1, NS1, SLICE, BS), F32)
    return tuple(pl.pallas_call(
        write_out,
        out_shape=(column, block, column, block, block),
        in_specs=[hbm] * 3,
        out_specs=(hbm,) * 5,
        scratch_shapes=[
            pltpu.VMEM((2, NS1, SLICE, BS), F32), pltpu.VMEM((3, BS, BS), F32), dma((5,)), dma((5,))],
        compiler_params=pltpu.CompilerParams(vmem_limit_bytes=64 * 1024 * 1024),
    )(middle, leaves, grams))


def solution(mesh):
    in_specs = (
        P("grid", "branch"),
        P("branch", None),
        P("branch", None),
        P("branch", None, None),
        P("branch", None, None, None),
        P("branch", None, None),
        P("branch", None, None, None),
    )
    out_specs = (
        P("branch", None, "grid", None),
        P("branch", None, None),
        P("branch", None, "grid", None),
        P("branch", None, None),
        P("branch", None, None),
    )
    return jax.shard_map(
        on_device, mesh=mesh, in_specs=in_specs, out_specs=out_specs, check_vma=False
    )
```
